32 devices in a mesh: seed: 8 (over y, x, core), hid: 4 (over z).
Axes of the slice: x: 2, y: 2, z: 4, core: 2. Of those that a mesh axis runs over, the one named last changes fastest.
Arguments:
- features: bfloat16 [262144, 100], P('seed'), may hold values from -6 to 6
- links_first: int32 [65536, 10], P('seed'), may hold values from -1 to 32767, as said below
- links_second: int32 [8192, 10], P('seed'), may hold values from -1 to 8191, as said below
- links_third: int32 [1024, 25], P('seed'), may hold values from -1 to 1023, as said below
- labels: int32 [1024], P('seed'), may hold values from 0 to 46
- valid: int32 [1024], P('seed'), may hold values from 0 to 1, as said below
- weight_first: float32 [200, 256], P(None, 'hid'), may hold values from -1.5 to 1.5
- moment_first: float32 [200, 256], P(None, 'hid')
- square_first: float32 [200, 256], P(None, 'hid'), as said below
- weight_stack: float32 [2, 512, 256], P(None, 'seed', 'hid'), may hold values from -4 to 4
- moment_stack: float32 [2, 512, 256], P(None, 'seed', 'hid')
- square_stack: float32 [2, 512, 256], P(None, 'seed', 'hid'), as said below
- weight_head: float32 [256, 47], P('hid'), may hold values from -6 to 6
- moment_head: float32 [256, 47], P('hid')
- square_head: float32 [256, 47], P('hid'), as said below
Outputs:
- loss_sum: float32 [], replicated
- count: float32 [], replicated
- new_moment_first: float32 [200, 256], P(None, 'hid')
- new_square_first: float32 [200, 256], P(None, 'hid')
- new_weight_first: float32 [200, 256], P(None, 'hid')
- new_moment_stack: float32 [2, 512, 256], P(None, 'seed', 'hid')
- new_square_stack: float32 [2, 512, 256], P(None, 'seed', 'hid')
- new_weight_stack: float32 [2, 512, 256], P(None, 'seed', 'hid')
- new_moment_head: float32 [256, 47], P('hid')
- new_square_head: float32 [256, 47], P('hid')
- new_weight_head: float32 [256, 47], P('hid')
The draws below stay inside these ranges and needn't reach their ends.
Inputs may be any that keep to these rules, and one draw needn't show every extreme that they name: `links_first`: each row's nonempty slots come first, one or more; row i of a block names only rows 4 i to 4 i + 3 of the next level in the same block (its own sampled rows). `links_second`: each row's nonempty slots come first, one or more; row i of a block names only rows 8 i to 8 i + 7 of the next level in the same block (its own sampled rows). `links_third`: each row's nonempty slots come first, one or more; row i of a block names only rows 8 i to 8 i + 7 of the next level in the same block (its own sampled rows). The first seed is valid. `square_first`: positive. `square_stack`: positive. `square_head`: positive.
All inputs are finite; a program needn't handle non-finite values.
Results may differ from the reference program's by a relative error of at most 0.012.
The reference program's roundings to bfloat16 on the way count: a program that leaves them out, or rounds other values in their place, can miss the bound.
Values may be sent and summed in bfloat16 or wider, within the bound.
A program may use at most 128 MiB of HBM per device.

```python
import math
import jax
import jax.numpy as jnp
from jax import lax

IN = 100
HID = 256
CLS = 47
FAN_A = 25
FAN_B = 10
FAN_C = 10
STEP = 5
SEED_DEV = 128
ROWS1 = 1024
ROWS2 = 8192
ROWS3 = 32768
SEEDS = 1024
N_SEED = 8


def neighbor_block(key, total, fanout, rows_out, ratio):
    key_degree, key_index = jax.random.split(key)
    degree = jax.random.randint(key_degree, (total,), 1, fanout + 1)
    degree = degree.at[0].set(fanout).at[1].set(1)
    offsets = jax.random.randint(key_index, (total, fanout), 0, ratio)
    local_row = jnp.arange(total) % rows_out
    picks = local_row[:, None] * ratio + offsets
    picks = picks.at[rows_out - 1, 0].set(rows_out * ratio - 1)
    slots = jnp.arange(fanout)[None, :]
    return jnp.where(slots < degree[:, None], picks, -1).astype(jnp.int32)


def signed_moment(key, shape, magnitude):
    key_size, key_sign = jax.random.split(key)
    spread = jax.random.uniform(key_size, shape, jnp.float32, 0.5, 1.5)
    signs = jax.random.rademacher(key_sign, shape, jnp.float32)
    return magnitude * spread * signs


def second_moment(key, shape, magnitude):
    factor = jnp.exp(jax.random.uniform(key, shape, jnp.float32, 0.0, math.log(4.0)))
    return magnitude * magnitude * factor


def scale_first():
    return 0.008 / math.sqrt(SEEDS)


def scale_stack():
    return jnp.array([0.005, 0.004], jnp.float32)[:, None, None] / math.sqrt(SEEDS)


def scale_head():
    return 0.015 / math.sqrt(SEEDS)


def draw_links_first(key, part):
    key = jax.random.fold_in(key, 1)
    return neighbor_block(key, SEEDS // SEED_DEV * ROWS2, FAN_C, ROWS2, ROWS3 // ROWS2)


def draw_links_second(key, part):
    key = jax.random.fold_in(key, 2)
    return neighbor_block(key, SEEDS // SEED_DEV * ROWS1, FAN_B, ROWS1, ROWS2 // ROWS1)


def draw_links_third(key, part):
    key = jax.random.fold_in(key, 3)
    return neighbor_block(key, SEEDS, FAN_A, SEED_DEV, ROWS1 // SEED_DEV)


def draw_valid(key, part):
    key = jax.random.fold_in(key, 4)
    position = jnp.arange(SEEDS)
    ticket = jax.random.randint(key, (SEEDS,), 0, 4 * SEEDS)
    chosen = (ticket < SEEDS + 2 * position) | (position == 0)
    return chosen.astype(jnp.int32)


def draw_moment_first(key, part):
    key = jax.random.fold_in(key, 5)
    return signed_moment(key, (2 * IN, HID), scale_first())


def draw_square_first(key, part):
    key = jax.random.fold_in(key, 6)
    return second_moment(key, (2 * IN, HID), scale_first())


def draw_moment_stack(key, part):
    key = jax.random.fold_in(key, 7)
    return signed_moment(key, (2, 2 * HID, HID), scale_stack())


def draw_square_stack(key, part):
    key = jax.random.fold_in(key, 8)
    return second_moment(key, (2, 2 * HID, HID), scale_stack())


def draw_moment_head(key, part):
    key = jax.random.fold_in(key, 9)
    return signed_moment(key, (HID, CLS), scale_head())


def draw_square_head(key, part):
    key = jax.random.fold_in(key, 10)
    return second_moment(key, (HID, CLS), scale_head())


def with_ends(values, stream_key, least, largest):
    spot = [jax.random.randint(jax.random.fold_in(stream_key, axis), (), 0, length) for axis, length in enumerate(values.shape)]
    main_axis = values.shape.index(max(values.shape))
    beside = spot[:main_axis] + [(spot[main_axis] + 1) % values.shape[main_axis]] + spot[main_axis + 1:]
    return values.at[tuple(spot)].set(least).at[tuple(beside)].set(largest)


def steps_of(stream_key, dims, cuts, low, top_value):
    level, own = 1.0, jax.random.fold_in(stream_key, 6)
    for axis_at, parts in cuts:
        draws = jnp.exp(jax.random.uniform(jax.random.fold_in(own, axis_at), (parts,), jnp.float32, low / len(cuts), top_value / len(cuts)))
        level = level * jnp.repeat(draws, dims[axis_at] // parts).reshape([-1 if axis == axis_at else 1 for axis in range(len(dims))])
    return level


def normal_values(stream_key, shape, scale, bound, shards=(), dtype=jnp.bfloat16):
    values = jax.random.normal(stream_key, shape, jnp.float32) * scale
    if len(shards) > 0:
        values = steps_of(stream_key, shape, shards, -0.22, 0.18) * values
    return jnp.clip(values, min=-bound, max=bound).astype(dtype)


def setup_inputs(seed: int = 0) -> dict:
    key_list = jax.random.split(jax.random.key(seed), 16)
    return {
        "features": normal_values(key_list[0], (N_SEED * ROWS3, IN), 1.0, 6.0, ((0, 8),)),
        "links_first": draw_links_first(jax.random.fold_in(key_list[15], 71), 0),
        "links_second": draw_links_second(jax.random.fold_in(key_list[15], 71), 0),
        "links_third": draw_links_third(jax.random.fold_in(key_list[15], 71), 0),
        "labels": with_ends(jax.random.randint(key_list[4], (SEEDS,), 0, CLS), jax.random.fold_in(key_list[4], 1), 0, CLS - 1).astype(jnp.int32),
        "valid": draw_valid(jax.random.fold_in(key_list[15], 71), 0),
        "weight_first": normal_values(key_list[6], (2 * IN, HID), 0.3, 1.5, ((1, 4),), jnp.float32),
        "moment_first": draw_moment_first(jax.random.fold_in(key_list[15], 71), 0),
        "square_first": draw_square_first(jax.random.fold_in(key_list[15], 71), 0),
        "weight_stack": normal_values(key_list[9], (2, 2 * HID, HID), 0.7, 4.0, ((1, 8), (2, 4)), jnp.float32),
        "moment_stack": draw_moment_stack(jax.random.fold_in(key_list[15], 71), 0),
        "square_stack": draw_square_stack(jax.random.fold_in(key_list[15], 71), 0),
        "weight_head": normal_values(key_list[12], (HID, CLS), 1.2, 6.0, ((0, 4),), jnp.float32),
        "moment_head": draw_moment_head(jax.random.fold_in(key_list[15], 71), 0),
        "square_head": draw_square_head(jax.random.fold_in(key_list[15], 71), 0),
    }


@jax.custom_vjp
def low(v):
    return lax.optimization_barrier(v.astype(jnp.bfloat16)).astype(jnp.float32)

@jax.custom_vjp
def low_back(v):
    return v

def low_keep(v):
    return (low(v), None)

def low_pass(kept, grad):
    return (grad,)

def back_keep(v):
    return (v, None)

def back_low(kept, grad):
    return (low(grad),)
low.defvjp(low_keep, low_pass)
low_back.defvjp(back_keep, back_low)
epsilon_norm = 1e-06
epsilon_adam = 1e-08
learn_rate = 0.6
decay_rate = 0.01
beta_first = 0.5
beta_second = 0.5

def local_mean(source_rows, neighbors):
    present = (neighbors >= 0).astype(jnp.float32)
    picked = source_rows[jnp.maximum(neighbors, 0)]
    totals = lax.optimization_barrier(jnp.sum(picked * present[:, :, None], axis=1))
    degree = jnp.maximum(lax.optimization_barrier(jnp.sum(present, axis=1)), 1.0)
    return totals / degree[:, None]

def sage_layer(source_rows, neighbors, weight, rows_in, rows_out):
    width = source_rows.shape[1]
    blocks = source_rows.reshape(-1, rows_in, width)
    groups = neighbors.reshape(blocks.shape[0], rows_out, -1)
    merged = low(jax.vmap(local_mean)(blocks, groups).reshape(-1, width))
    itself = blocks[:, :rows_out].reshape(-1, width)
    joined = jnp.concatenate([itself, merged], axis=1)
    preact = low_back(jnp.dot(joined, weight, precision=lax.Precision.HIGHEST))
    active = jax.nn.silu(preact)
    scaled = active * lax.rsqrt(lax.optimization_barrier(jnp.sum(active * active, axis=1, keepdims=True)) + epsilon_norm)
    return low(scaled)

def adamw(weight, moment, square, grad):
    new_moment = beta_first * moment + (1.0 - beta_first) * grad
    new_square = beta_second * square + (1.0 - beta_second) * grad * grad
    moment_hat = new_moment / (1.0 - beta_first ** STEP)
    square_hat = new_square / (1.0 - beta_second ** STEP)
    new_weight = weight - learn_rate * (moment_hat / (jnp.sqrt(square_hat) + epsilon_adam) + decay_rate * weight)
    return (new_moment, new_square, new_weight)

def reference(features, links_first, links_second, links_third, labels, valid, weight_first, moment_first, square_first, weight_stack, moment_stack, square_stack, weight_head, moment_head, square_head):
    inputs = features.astype(jnp.float32)
    present = valid.astype(jnp.float32)
    count = jnp.sum(present)

    def forward(first, stack, head):
        first_low = low(first)
        stack_low = low(stack)
        head_low = low(head)
        level_two = sage_layer(inputs, links_first, first_low, ROWS3, ROWS2)
        level_one = sage_layer(level_two, links_second, stack_low[0], ROWS2, ROWS1)
        level_zero = sage_layer(level_one, links_third, stack_low[1], ROWS1, SEED_DEV)
        logits = low_back(jnp.dot(level_zero, head_low, precision=lax.Precision.HIGHEST))
        totals = jax.nn.logsumexp(logits, axis=1)
        target = jnp.take_along_axis(logits, labels[:, None], axis=1)[:, 0]
        summed = jnp.sum((totals - target) * present)
        return (summed / jnp.maximum(count, 1.0), summed)
    loss, pullback, loss_sum = jax.vjp(forward, weight_first, weight_stack, weight_head, has_aux=True)
    grad_first, grad_stack, grad_head = pullback(jnp.ones_like(loss))
    moment_a, square_a, weight_a = adamw(weight_first, moment_first, square_first, grad_first)
    moment_b, square_b, weight_b = adamw(weight_stack, moment_stack, square_stack, grad_stack)
    moment_c, square_c, weight_c = adamw(weight_head, moment_head, square_head, grad_head)
    return (loss_sum, count, moment_a, square_a, weight_a, moment_b, square_b, weight_b, moment_c, square_c, weight_c)
```

```python
import functools

import jax
import jax.numpy as jnp
from jax import lax
from jax.experimental import pallas as pl
from jax.experimental.pallas import tpu as pltpu
from jax.sharding import PartitionSpec as P

STEP = 5
LANES = 128


epsilon_norm = 1e-06
epsilon_adam = 1e-08
learn_rate = 0.6
decay_rate = 0.01
beta_first = 0.5
beta_second = 0.5

f32, bf16, i32 = jnp.float32, jnp.bfloat16, jnp.int32
NT = (((1,), (1,)), ((), ()))
TN = (((0,), (0,)), ((), ()))


def dot(a, b):
    return jnp.dot(a, b, preferred_element_type=f32)


def dot_nt(a, b):
    return lax.dot_general(a, b, NT, preferred_element_type=f32)


def dot_tn(a, b):
    return lax.dot_general(a, b, TN, preferred_element_type=f32)


def iota(shape, axis):
    return lax.broadcasted_iota(i32, shape, axis)


def slot_counts(links, first_row, ratio):
    lanes = links.shape[1]
    base = (first_row + iota((1, lanes), 1)) * ratio
    offsets = links - base
    counts = [
        jnp.sum(jnp.where(offsets == r, 1.0, 0.0), axis=0, keepdims=True) for r in range(ratio)
    ]
    degree = jnp.maximum(
        jnp.sum(jnp.where(links >= 0, 1.0, 0.0), axis=0, keepdims=True), 1.0
    )
    return counts, degree


def stripes(counts):
    ratio, lanes = len(counts), counts[0].shape[1]
    which = iota((8, lanes), 0) % ratio
    out = jnp.zeros((8, lanes), f32)
    for r in range(ratio):
        out = jnp.where(which == r, counts[r], out)
    return out


def spread(mask, stripe):
    rows = mask.shape[0]
    values = mask.reshape(rows // 8, 8, LANES) * stripe[None]
    return values.reshape(rows, LANES).astype(bf16)


def window_mask(rows, ratio):
    return jnp.where(iota((rows, LANES), 0) // ratio == iota((rows, LANES), 1), 1.0, 0.0)


def activate(preact):
    logistic = 1.0 / (1.0 + jnp.exp(-preact))
    active = preact * logistic
    slope = logistic * (1.0 + preact * (1.0 - logistic))
    scaling = lax.rsqrt(jnp.sum(active * active, axis=0, keepdims=True) + epsilon_norm)
    return (active * scaling).astype(bf16), active, slope, scaling


def activate_back(grad_out, active, slope, scaling):
    inner = jnp.sum(active * grad_out, axis=0, keepdims=True)
    grad_active = scaling * grad_out - active * (scaling * scaling * scaling * inner)
    return (grad_active * slope).astype(bf16)


def placement(rows, classes, width):
    gap = LANES - width
    row, col = iota((rows, classes), 0), iota((rows, classes), 1)
    target = jnp.where(col < gap, width + col, LANES + width + col - gap)
    return jnp.where(row == target, 1.0, 0.0).astype(bf16)


def compute_kernel(
    sizes,
    features, links_first, links_second, links_third,
    labels, valid, count, first_ref, low_two, low_three, head_ref,
    grad_first, grad_two, grad_three, loss_ref,
    own_rows, child_rows, own_lead, links_a, links_b, links_a_lead, links_b_lead,
    mean_one, hidden_one, active_one, slope_one, scale_one, degree_rows, stripe_rows,
    joined_two, joined_three, spread_two, mask_four, mask_eight, pre_one, sems,
):
    n3, n2, n1, n0, parts, width, classes = sizes
    q2, q1, q0 = n2 // parts, n1 // parts, n0 // parts
    r3, r2, r1 = n3 // n2, n2 // n1, n1 // n0
    z = lax.axis_index("hid")
    two = q2 + q1 + LANES
    hid = 256

    def at(unit):
        return pl.ds(pl.multiple_of(z * unit, LANES), unit)

    copies = [
        (links_first.at[:, at(q2)], links_a.at[:, pl.ds(0, q2)]),
        (links_first.at[:, at(q1)], links_a.at[:, pl.ds(q2, q1)]),
        (links_first.at[:, pl.ds(0, LANES)], links_a_lead),
        (links_second.at[:, at(q1)], links_b),
        (links_second.at[:, pl.ds(0, LANES)], links_b_lead),
        (features.at[:, pl.ds(0, LANES)], own_lead),
        (features.at[:, at(q2)], own_rows.at[:, pl.ds(0, q2)]),
        (features.at[:, at(q1)], own_rows.at[:, pl.ds(q2, q1)]),
        (features.at[:, at(q2 * r3)], child_rows.at[:, pl.ds(0, q2 * r3)]),
        (features.at[:, at(q1 * r3)], child_rows.at[:, pl.ds(q2 * r3, q1 * r3)]),
        (
            features.at[:, pl.ds(pl.multiple_of(z * q0 * r3, LANES), LANES * r3)],
            child_rows.at[:, pl.ds((q2 + q1) * r3, LANES * r3)],
        ),
    ]
    started = [pltpu.make_async_copy(src, dst, sems.at[i]) for i, (src, dst) in enumerate(copies)]
    for copy in started:
        copy.start()
    mask_four[...] = window_mask(LANES * r3, r3)
    mask_eight[...] = window_mask(LANES * r2, r2)
    mean_one[...] = jnp.zeros_like(mean_one)
    for copy in started:
        copy.wait()

    counts_a, degree_a = slot_counts(links_a_lead[...], 0, r3)
    counts_b, degree_b = slot_counts(links_b_lead[...], 0, r2)
    counts_c, degree_c = slot_counts(links_third[...], 0, r1)
    lead = [*counts_a, degree_a, *counts_b, degree_b, *counts_c, degree_c]
    lead += [labels[...].astype(f32), valid[...].astype(f32)]
    packed = jnp.zeros((32, LANES), f32)
    for k, row in enumerate(lead):
        packed = jnp.where(iota((32, LANES), 0) == k, row, packed)
    source, target = iota((LANES, LANES), 0), iota((LANES, LANES), 1)
    mine = jnp.where((source == target + z * q0) & (target < q0), 1.0, 0.0).astype(bf16)
    packed = dot(packed.astype(bf16), mine)
    take = [packed[k : k + 1] for k in range(len(lead))]
    counts_a, degree_a = take[:r3], jnp.maximum(take[r3], 1.0)
    take = take[r3 + 1 :]
    counts_b, degree_b = take[:r2], jnp.maximum(take[r2], 1.0)
    take = take[r2 + 1 :]
    counts_c, degree_c = take[:r1], jnp.maximum(take[r1], 1.0)
    label, present = take[r1 + 1], take[r1 + 2]
    own_rows[:, pl.ds(q2 + q1, LANES)] = dot(own_lead[...], mine).astype(bf16)

    counts, degree = slot_counts(links_a[:, pl.ds(0, q2)], z * q2, r3)
    for t in range(q2 // LANES):
        stripe_rows[t] = stripes([c[:, t * LANES : (t + 1) * LANES] for c in counts])
    degree_rows[:, pl.ds(0, q2)] = degree
    counts, degree = slot_counts(links_a[:, pl.ds(q2, q1)], z * q1, r3)
    for t in range(q1 // LANES):
        stripe_rows[q2 // LANES + t] = stripes([c[:, t * LANES : (t + 1) * LANES] for c in counts])
    degree_rows[:, pl.ds(q2, q1)] = degree
    stripe_rows[two // LANES - 1] = stripes(counts_a)
    degree_rows[:, pl.ds(q2 + q1, LANES)] = degree_a

    def layer_one(tile, tiles):
        for t in range(tiles):
            lanes = pl.ds(pl.multiple_of((tile + t) * LANES, LANES), LANES)
            kids = pl.ds(pl.multiple_of((tile + t) * LANES * r3, LANES), LANES * r3)
            matrix = spread(mask_four[...], stripe_rows[tile + t])
            mean = dot(child_rows[:, kids], matrix) / degree_rows[:, lanes]
            mean_one[0:width, lanes] = mean.astype(bf16)
        lanes = pl.ds(pl.multiple_of(tile * LANES, LANES), LANES * tiles)
        preact = dot(first_ref[:, 0:width], own_rows[:, lanes])
        preact += dot(first_ref[:, LANES : 2 * LANES], mean_one[:, lanes])
        output, active, slope, scaling = activate(preact)
        hidden_one[:, lanes] = output
        active_one[:, lanes] = active
        slope_one[:, lanes] = slope
        scale_one[:, lanes] = scaling

    per = 4
    lax.fori_loop(0, q2 // LANES // per, lambda i, c: (layer_one(i * per, per), c)[1], 0)
    layer_one(q2 // LANES, q1 // LANES + 1)

    counts, degree_t = slot_counts(links_b[...], z * q1, r2)
    joined_two[0:hid, :] = hidden_one[:, pl.ds(q2, q1 + LANES)]
    for t in range(q1 // LANES):
        stripe = stripes([c[:, t * LANES : (t + 1) * LANES] for c in counts])
        rows = pl.ds(t * LANES * r2, LANES * r2)
        spread_two[rows, :] = spread(mask_eight[...], stripe)
        mean = dot(hidden_one[:, rows], spread_two[rows, :])
        lanes = slice(t * LANES, (t + 1) * LANES)
        joined_two[hid:, lanes] = (mean / degree_t[:, lanes]).astype(bf16)
    spread_lead = spread(mask_eight[0 : q0 * r2, :], stripes(counts_b))
    mean = dot(hidden_one[:, pl.ds(q2, q1)], spread_lead)
    joined_two[hid:, pl.ds(q1, LANES)] = (mean / degree_b).astype(bf16)
    preact = dot_tn(low_two[...], joined_two[...])
    output, active_two, slope_two, scale_two = activate(preact)

    joined_three[0:hid, :] = output[:, q1:]
    spread_three = spread(mask_eight[0 : q0 * r1, :], stripes(counts_c))
    mean = dot(output[:, 0:q1], spread_three)
    joined_three[hid:, :] = (mean / degree_c).astype(bf16)
    preact = dot_tn(low_three[...], joined_three[...])
    seeds, active_three, slope_three, scale_three = activate(preact)

    logits = dot(head_ref[...], seeds)
    row = iota(logits.shape, 0)
    logits = jnp.where(row < classes, logits, -1e30)
    peak = jnp.max(logits, axis=0, keepdims=True)
    shifted = jnp.exp(logits - peak)
    totals = jnp.sum(shifted, axis=0, keepdims=True)
    hot = jnp.where(row.astype(f32) == label, 1.0, 0.0)
    nll = peak + jnp.log(totals) - jnp.sum(jnp.where(hot > 0, logits, 0.0), axis=0, keepdims=True)
    loss = jnp.sum(jnp.where(present > 0, nll, 0.0), axis=1, keepdims=True)
    loss_ref[...] = jnp.broadcast_to(loss, loss_ref.shape)
    share = present / jnp.maximum(count[0, 0], 1.0)
    grad_logits = ((shifted / totals - hot) * share).astype(bf16)
    placed = dot(placement(2 * LANES, grad_logits.shape[0], width), grad_logits).astype(bf16)
    grad_first[...] = dot_nt(seeds, placed)
    grad_out = dot_tn(head_ref[...], grad_logits)

    grad_pre = activate_back(grad_out, active_three, slope_three, scale_three)
    grad_three[...] = dot_nt(joined_three[...], grad_pre)
    grad_joined = dot(low_three[...], grad_pre)
    grad_mean = (grad_joined[hid:] / degree_c).astype(bf16)
    grad_out = jnp.concatenate([dot_nt(grad_mean, spread_three), grad_joined[0:hid]], axis=1)

    grad_pre = activate_back(grad_out, active_two, slope_two, scale_two)
    grad_two[...] = dot_nt(joined_two[...], grad_pre)
    grad_joined = dot(low_two[...], grad_pre)
    grad_mean = (grad_joined[hid:, 0:q1] / degree_t).astype(bf16)
    lead_mean = (grad_joined[hid:, q1:] / degree_b).astype(bf16)

    pieces = q2 // LANES // per
    for i in range(pieces):
        tile = i * per * LANES
        lanes = pl.ds(tile, per * LANES)
        group = tile // (LANES * r2) * LANES
        grad_out = dot_nt(grad_mean[:, group : group + LANES], spread_two[lanes, :])
        pre_one[:, lanes] = activate_back(
            grad_out, active_one[:, lanes], slope_one[:, lanes], scale_one[:, lanes]
        )
    own = grad_joined[0:hid]
    lanes = pl.ds(q2, q1)
    pre_one[:, lanes] = activate_back(
        own[:, 0:q1] + dot_nt(lead_mean, spread_lead),
        active_one[:, lanes], slope_one[:, lanes], scale_one[:, lanes],
    )
    lanes = pl.ds(q2 + q1, LANES)
    pre_one[:, lanes] = activate_back(
        own[:, q1:], active_one[:, lanes], slope_one[:, lanes], scale_one[:, lanes]
    )
    grad_first[:, 0:width] = dot_nt(pre_one[...], own_rows[...])
    grad_first[:, LANES : LANES + width] = dot_nt(pre_one[...], mean_one[0:width, :])


def compute(sizes, *operands):
    n3, n2, n1, n0, parts, width, classes = sizes
    q2, q1 = n2 // parts, n1 // parts
    r3, r2 = n3 // n2, n2 // n1
    two = q2 + q1 + LANES
    slots = operands[1].shape[0]
    slots_b = operands[2].shape[0]
    hbm, vmem = pl.BlockSpec(memory_space=pl.ANY), pl.BlockSpec(memory_space=pltpu.VMEM)
    smem = pl.BlockSpec(memory_space=pltpu.SMEM)
    shape = jax.ShapeDtypeStruct
    return pl.pallas_call(
        functools.partial(compute_kernel, sizes),
        out_shape=(
            shape((256, 256), f32), shape((512, 256), f32), shape((512, 256), f32), shape((8, LANES), f32),
        ),
        in_specs=[hbm, hbm, hbm, vmem, vmem, vmem, smem, vmem, vmem, vmem, vmem],
        out_specs=(vmem,) * 4,
        scratch_shapes=[
            pltpu.VMEM((width, two), bf16),
            pltpu.VMEM((width, two * r3), bf16),
            pltpu.VMEM((width, LANES), bf16),
            pltpu.VMEM((slots, q2 + q1), i32),
            pltpu.VMEM((slots_b, q1), i32),
            pltpu.VMEM((slots, LANES), i32),
            pltpu.VMEM((slots_b, LANES), i32),
            pltpu.VMEM((LANES, two), bf16),
            pltpu.VMEM((256, two), bf16),
            pltpu.VMEM((256, two), f32),
            pltpu.VMEM((256, two), f32),
            pltpu.VMEM((1, two), f32),
            pltpu.VMEM((1, two), f32),
            pltpu.VMEM((two // LANES, 8, LANES), f32),
            pltpu.VMEM((512, q1 + LANES), bf16),
            pltpu.VMEM((512, LANES), bf16),
            pltpu.VMEM((q2, LANES), bf16),
            pltpu.VMEM((LANES * r3, LANES), f32),
            pltpu.VMEM((LANES * r2, LANES), f32),
            pltpu.VMEM((256, two), bf16),
            pltpu.SemaphoreType.DMA((11,)),
        ],
        compiler_params=pltpu.CompilerParams(vmem_limit_bytes=56 * 2**20),
    )(*operands)


def adamw(weight, moment, square, grad):
    new_moment = beta_first * moment + (1.0 - beta_first) * grad
    new_square = beta_second * square + (1.0 - beta_second) * grad * grad
    moment_hat = new_moment / (1.0 - beta_first**STEP)
    square_hat = new_square / (1.0 - beta_second**STEP)
    new_weight = weight - learn_rate * (
        moment_hat / (jnp.sqrt(square_hat) + epsilon_adam) + decay_rate * weight
    )
    return (new_moment, new_square, new_weight)


def per_device(
    features,
    links_first,
    links_second,
    links_third,
    labels,
    valid,
    weight_first,
    moment_first,
    square_first,
    weight_stack,
    moment_stack,
    square_stack,
    weight_head,
    moment_head,
    square_head,
):
    parts = lax.axis_size("hid")
    width, classes = features.shape[1], weight_head.shape[1]
    sizes = (
        features.shape[0], links_first.shape[0], links_second.shape[0], links_third.shape[0],
        parts, width, classes,
    )
    stack_low = lax.all_gather(weight_stack.astype(bf16), "seed", axis=1, tiled=True)
    stack_low = lax.all_gather(stack_low, "hid", axis=2, tiled=True)
    first_low = weight_first.T.astype(bf16)
    first_low = jnp.pad(first_low.reshape(-1, 2, width), ((0, 0), (0, 0), (0, LANES - width)))
    first_low = lax.all_gather(first_low.reshape(-1, 2 * LANES), "hid", axis=0, tiled=True)
    head_low = jnp.pad(weight_head.T.astype(bf16), ((0, 48 - classes), (0, 0)))
    head_low = lax.all_gather(head_low, "hid", axis=1, tiled=True)
    count = lax.psum(jnp.sum(valid.astype(f32)), "seed")
    grad_first, grad_two, grad_three, loss = compute(
        sizes,
        features.T, links_first.T, links_second.T, links_third.T,
        labels.reshape(1, -1), valid.reshape(1, -1), count.reshape(1, 1),
        first_low, stack_low[0], stack_low[1], head_low,
    )
    loss_sum = lax.psum(loss[0, 0], ("seed", "hid"))
    grad_stack = jnp.stack([grad_two, grad_three]).astype(bf16)
    grad_stack = lax.psum_scatter(grad_stack, "seed", scatter_dimension=1, tiled=True)
    grad_stack = lax.psum_scatter(grad_stack, "hid", scatter_dimension=2, tiled=True).astype(f32)
    grad_first = lax.psum_scatter(grad_first, "hid", scatter_dimension=0, tiled=True)
    grad_first = lax.psum(grad_first, "seed")
    gap = LANES - width
    grad_head = jnp.concatenate(
        [grad_first[:, width:LANES], grad_first[:, LANES + width : LANES + width + classes - gap]], axis=1
    )
    grad_first = jnp.concatenate(
        [grad_first[:, :width], grad_first[:, LANES : LANES + width]], axis=1
    ).T
    moment_a, square_a, weight_a = adamw(weight_first, moment_first, square_first, grad_first)
    moment_b, square_b, weight_b = adamw(weight_stack, moment_stack, square_stack, grad_stack)
    moment_c, square_c, weight_c = adamw(weight_head, moment_head, square_head, grad_head)
    return (
        loss_sum,
        count,
        moment_a,
        square_a,
        weight_a,
        moment_b,
        square_b,
        weight_b,
        moment_c,
        square_c,
        weight_c,
    )


def solution(mesh):
    placed = (
        P("seed", None),
        P("seed", None),
        P("seed", None),
        P("seed", None),
        P("seed"),
        P("seed"),
        P(None, "hid"),
        P(None, "hid"),
        P(None, "hid"),
        P(None, "seed", "hid"),
        P(None, "seed", "hid"),
        P(None, "seed", "hid"),
        P("hid", None),
        P("hid", None),
        P("hid", None),
    )
    return jax.shard_map(
        per_device,
        mesh=mesh,
        in_specs=placed,
        out_specs=(P(), P()) + placed[6:],
        check_vma=False,
    )
```

```python
import functools

import jax
import jax.numpy as jnp
from jax import lax
from jax.experimental import pallas as pl
from jax.experimental.pallas import tpu as pltpu
from jax.sharding import PartitionSpec as P

STEP = 5
LANES = 128


epsilon_norm = 1e-06
epsilon_adam = 1e-08
learn_rate = 0.6
decay_rate = 0.01
beta_first = 0.5
beta_second = 0.5

f32, bf16, i32 = jnp.float32, jnp.bfloat16, jnp.int32
MESH = pl.DeviceIdType.MESH
NT = (((1,), (1,)), ((), ()))
TN = (((0,), (0,)), ((), ()))


def dot(a, b):
    return jnp.dot(a, b, preferred_element_type=f32)


def dot_nt(a, b):
    return lax.dot_general(a, b, NT, preferred_element_type=f32)


def dot_tn(a, b):
    return lax.dot_general(a, b, TN, preferred_element_type=f32)


def iota(shape, axis):
    return lax.broadcasted_iota(i32, shape, axis)


def slot_counts(links, first_row, ratio):
    lanes = links.shape[1]
    base = (first_row + iota((1, lanes), 1)) * ratio
    offsets = links - base
    counts = [
        jnp.sum(jnp.where(offsets == r, 1.0, 0.0), axis=0, keepdims=True) for r in range(ratio)
    ]
    degree = jnp.maximum(
        jnp.sum(jnp.where(links >= 0, 1.0, 0.0), axis=0, keepdims=True), 1.0
    )
    return counts, degree


def stripes(counts):
    ratio, lanes = len(counts), counts[0].shape[1]
    which = iota((8, lanes), 0) % ratio
    out = jnp.zeros((8, lanes), f32)
    for r in range(ratio):
        out = jnp.where(which == r, counts[r], out)
    return out


def spread(mask, stripe):
    rows = mask.shape[0]
    values = mask.reshape(rows // 8, 8, LANES) * stripe[None]
    return values.reshape(rows, LANES).astype(bf16)


def window_mask(rows, ratio):
    return jnp.where(iota((rows, LANES), 0) // ratio == iota((rows, LANES), 1), 1.0, 0.0)


def activate(preact):
    logistic = 1.0 / (1.0 + jnp.exp(-preact))
    active = preact * logistic
    slope = logistic * (1.0 + preact * (1.0 - logistic))
    scaling = lax.rsqrt(jnp.sum(active * active, axis=0, keepdims=True) + epsilon_norm)
    return (active * scaling).astype(bf16), active, slope, scaling


def activate_back(grad_out, active, slope, scaling):
    inner = jnp.sum(active * grad_out, axis=0, keepdims=True)
    grad_active = scaling * grad_out - active * (scaling * scaling * scaling * inner)
    return (grad_active * slope).astype(bf16)


def placement_rows(classes, columns, width):
    gap = LANES - width
    row, col = iota((classes, columns), 0), iota((classes, columns), 1)
    target = jnp.where(row < gap, width + row, LANES + width + row - gap)
    return jnp.where(col == target, 1.0, 0.0).astype(bf16)


def placement(rows, classes, width):
    gap = LANES - width
    row, col = iota((rows, classes), 0), iota((rows, classes), 1)
    target = jnp.where(col < gap, width + col, LANES + width + col - gap)
    return jnp.where(row == target, 1.0, 0.0).astype(bf16)


def shift_half(x):
    return pltpu.roll(x, LANES // 2, 1)


def step_kernel(
    sizes,
    features, links_first, links_second, links_third, labels, valid, weight_first, weight_stack, weight_head,
    first_out, stack_out, count_out,
    own_rows, child_rows, own_lead, links_a, links_b, links_a_lead, links_b_lead,
    mean_one, hidden_one, active_one, slope_one, scale_one, degree_rows, stripe_rows,
    joined_two, joined_three, spread_two, mask_four, mask_eight, pre_one,
    first_all, stack_all, valid_all, low_two, low_three,
    core_send, core_recv, stack_send, stack_recv, grad_one, first_send, first_recv, first_piece,
    local_sems, first_ssem, first_rsem, block_ssem, block_rsem, pair_ssem, pair_rsem, valid_ssem, valid_rsem,
    core_ssem, core_rsem, back_ssem, back_rsem, piece_ssem, piece_rsem, share_ssem, share_rsem,
):
    n3, n2, n1, n0, parts, seeds_axis, width, classes = sizes
    q2, q1, q0 = n2 // parts, n1 // parts, n0 // parts
    r3, r2, r1 = n3 // n2, n2 // n1, n1 // n0
    s, z = lax.axis_index("seed"), lax.axis_index("hid")
    core, chip = lax.rem(s, 2), s // 2
    chips = seeds_axis // 2
    sibling = s + 1 - 2 * core
    two = q2 + q1 + LANES
    hid = 256
    unit = hid // parts
    own_units = pl.ds(pl.multiple_of(z * unit, unit), unit)
    everyone = [(k, d) for d in range(parts) for k in range(seeds_axis) if (k, d) != (0, 0)]

    def place(k, d):
        return (lax.rem(s + k, seeds_axis), lax.rem(z + d, parts))

    barrier = pltpu.get_barrier_semaphore()
    for k, d in everyone:
        pl.semaphore_signal(barrier, inc=1, device_id=place(k, d), device_id_type=MESH)

    def at(size):
        return pl.ds(pl.multiple_of(z * size, LANES), size)

    copies = [
        (links_first.at[:, at(q2)], links_a.at[:, pl.ds(0, q2)]),
        (links_first.at[:, at(q1)], links_a.at[:, pl.ds(q2, q1)]),
        (links_first.at[:, pl.ds(0, LANES)], links_a_lead),
        (links_second.at[:, at(q1)], links_b),
        (links_second.at[:, pl.ds(0, LANES)], links_b_lead),
        (features.at[:, pl.ds(0, LANES)], own_lead),
        (features.at[:, at(q2)], own_rows.at[:, pl.ds(0, q2)]),
        (features.at[:, at(q1)], own_rows.at[:, pl.ds(q2, q1)]),
        (features.at[:, at(q2 * r3)], child_rows.at[:, pl.ds(0, q2 * r3)]),
        (features.at[:, at(q1 * r3)], child_rows.at[:, pl.ds(q2 * r3, q1 * r3)]),
        (
            features.at[:, pl.ds(pl.multiple_of(z * q0 * r3, LANES), LANES * r3)],
            child_rows.at[:, pl.ds((q2 + q1) * r3, LANES * r3)],
        ),
    ]
    started = [pltpu.make_async_copy(src, dst, local_sems.at[i]) for i, (src, dst) in enumerate(copies)]
    for copy in started:
        copy.start()

    row, col = iota((2 * width, hid), 0), iota((2 * width, hid), 1)
    columns = jnp.where(row < width, row, row - width + LANES)
    lift = jnp.where(columns == col, 1.0, 0.0).astype(bf16)
    seat = placement(hid, classes, width)
    shard = dot(weight_first[...].astype(bf16), lift)
    shard += dot_tn(weight_head[...].astype(bf16), placement_rows(classes, hid, width))
    first_all[own_units, :] = shard.astype(bf16)
    half = unit
    row, col = iota((half, LANES), 0), iota((half, LANES), 1)
    block = dot(weight_stack[0].astype(bf16), jnp.where(row == col, 1.0, 0.0).astype(bf16))
    block += dot(weight_stack[1].astype(bf16), jnp.where(row + half == col, 1.0, 0.0).astype(bf16))
    stack_all[core, z, chip] = block.astype(bf16)
    valid_all[s] = jnp.broadcast_to(valid[...].astype(f32), valid_all.shape[1:])

    pl.semaphore_wait(barrier, len(everyone))

    def send(src, dst, ssem, rsem, device):
        copy = pltpu.make_async_remote_copy(
            src_ref=src, dst_ref=dst, send_sem=ssem, recv_sem=rsem, device_id=device, device_id_type=MESH
        )
        copy.start()
        return copy

    first_moves = [
        send(first_all.at[own_units], first_all.at[own_units], first_ssem.at[d], first_rsem.at[d], place(0, d))
        for d in range(1, parts)
    ]
    others = [(k, d) for d in range(parts) for k in range(chips) if (k, d) != (0, 0)]
    mine_block = stack_all.at[core, z, chip]
    block_moves = [
        send(mine_block, mine_block, block_ssem.at[i], block_rsem.at[i], place(2 * k, d))
        for i, (k, d) in enumerate(others)
    ]
    valid_moves = [
        send(valid_all.at[s], valid_all.at[s], valid_ssem.at[k], valid_rsem.at[k], place(k, 0))
        for k in range(1, seeds_axis)
    ]

    mask_four[...] = window_mask(LANES * r3, r3)
    mask_eight[...] = window_mask(LANES * r2, r2)
    mean_one[...] = jnp.zeros_like(mean_one)
    for copy in started:
        copy.wait()

    counts_a, degree_a = slot_counts(links_a_lead[...], 0, r3)
    counts_b, degree_b = slot_counts(links_b_lead[...], 0, r2)
    counts_c, degree_c = slot_counts(links_third[...], 0, r1)
    lead = [*counts_a, degree_a, *counts_b, degree_b, *counts_c, degree_c]
    lead += [labels[...].astype(f32), valid[...].astype(f32)]
    packed = jnp.zeros((32, LANES), f32)
    for k, line in enumerate(lead):
        packed = jnp.where(iota((32, LANES), 0) == k, line, packed)
    source, target = iota((LANES, LANES), 0), iota((LANES, LANES), 1)
    mine = jnp.where((source == target + z * q0) & (target < q0), 1.0, 0.0).astype(bf16)
    packed = dot(packed.astype(bf16), mine)
    take = [packed[k : k + 1] for k in range(len(lead))]
    counts_a, degree_a = take[:r3], jnp.maximum(take[r3], 1.0)
    take = take[r3 + 1 :]
    counts_b, degree_b = take[:r2], jnp.maximum(take[r2], 1.0)
    take = take[r2 + 1 :]
    counts_c, degree_c = take[:r1], jnp.maximum(take[r1], 1.0)
    label, present = take[r1 + 1], take[r1 + 2]
    own_rows[:, pl.ds(q2 + q1, LANES)] = dot(own_lead[...], mine).astype(bf16)

    counts, degree = slot_counts(links_a[:, pl.ds(0, q2)], z * q2, r3)
    for t in range(q2 // LANES):
        stripe_rows[t] = stripes([c[:, t * LANES : (t + 1) * LANES] for c in counts])
    degree_rows[:, pl.ds(0, q2)] = degree
    counts, degree = slot_counts(links_a[:, pl.ds(q2, q1)], z * q1, r3)
    for t in range(q1 // LANES):
        stripe_rows[q2 // LANES + t] = stripes([c[:, t * LANES : (t + 1) * LANES] for c in counts])
    degree_rows[:, pl.ds(q2, q1)] = degree
    stripe_rows[two // LANES - 1] = stripes(counts_a)
    degree_rows[:, pl.ds(q2 + q1, LANES)] = degree_a

    def mean_tiles(tile, tiles):
        for t in range(tiles):
            lanes = pl.ds(pl.multiple_of((tile + t) * LANES, LANES), LANES)
            kids = pl.ds(pl.multiple_of((tile + t) * LANES * r3, LANES), LANES * r3)
            matrix = spread(mask_four[...], stripe_rows[tile + t])
            mean = dot(child_rows[:, kids], matrix) / degree_rows[:, lanes]
            mean_one[0:width, lanes] = mean.astype(bf16)

    def layer_one(tile, tiles):
        lanes = pl.ds(pl.multiple_of(tile * LANES, LANES), LANES * tiles)
        preact = dot(first_all[:, 0:width], own_rows[:, lanes])
        preact += dot(first_all[:, LANES : 2 * LANES], mean_one[:, lanes])
        output, active, slope, scaling = activate(preact)
        hidden_one[:, lanes] = output
        active_one[:, lanes] = active
        slope_one[:, lanes] = slope
        scale_one[:, lanes] = scaling

    per = 4
    tail = q1 // LANES + 1
    lax.fori_loop(0, q2 // LANES // per, lambda i, c: (mean_tiles(i * per, per), c)[1], 0)
    mean_tiles(q2 // LANES, tail)

    counts, degree_t = slot_counts(links_b[...], z * q1, r2)
    for t in range(q1 // LANES):
        stripe = stripes([c[:, t * LANES : (t + 1) * LANES] for c in counts])
        spread_two[pl.ds(t * LANES * r2, LANES * r2), :] = spread(mask_eight[...], stripe)
    spread_lead = spread(mask_eight[0 : q0 * r2, :], stripes(counts_b))
    spread_three = spread(mask_eight[0 : q0 * r1, :], stripes(counts_c))

    for copy in first_moves:
        copy.wait_recv()
    lax.fori_loop(0, q2 // LANES // per, lambda i, c: (layer_one(i * per, per), c)[1], 0)

    for copy in block_moves:
        copy.wait_recv()
    pair = stack_all.at[core]
    pair_move = send(pair, pair, pair_ssem, pair_rsem, (sibling, z))
    layer_one(q2 // LANES, tail)

    joined_two[0:hid, :] = hidden_one[:, pl.ds(q2, q1 + LANES)]
    for t in range(q1 // LANES):
        rows = pl.ds(t * LANES * r2, LANES * r2)
        mean = dot(hidden_one[:, rows], spread_two[rows, :])
        lanes = slice(t * LANES, (t + 1) * LANES)
        joined_two[hid:, lanes] = (mean / degree_t[:, lanes]).astype(bf16)
    mean = dot(hidden_one[:, pl.ds(q2, q1)], spread_lead)
    joined_two[hid:, pl.ds(q1, LANES)] = (mean / degree_b).astype(bf16)

    pair_move.wait_recv()
    low_half = iota((1, 1, LANES), 2) < half
    for b in range(2):
        for c in range(2):
            left = stack_all[c, 2 * b].astype(f32)
            right = stack_all[c, 2 * b + 1].astype(f32)
            lanes = slice(b * LANES, (b + 1) * LANES)
            swap = lambda v: shift_half(v.reshape(-1, LANES)).reshape(v.shape)
            low_two[:, c, :, lanes] = jnp.where(low_half, left, swap(right)).astype(bf16)
            low_three[:, c, :, lanes] = jnp.where(low_half, swap(left), right).astype(bf16)
    weight_two = low_two[...].reshape(2 * hid, hid)
    weight_three = low_three[...].reshape(2 * hid, hid)

    preact = dot_tn(weight_two, joined_two[...])
    output, active_two, slope_two, scale_two = activate(preact)

    joined_three[0:hid, :] = output[:, q1:]
    mean = dot(output[:, 0:q1], spread_three)
    joined_three[hid:, :] = (mean / degree_c).astype(bf16)
    preact = dot_tn(weight_three, joined_three[...])
    seeds, active_three, slope_three, scale_three = activate(preact)

    head = dot(first_all[...], seat).astype(bf16)
    for copy in valid_moves:
        copy.wait_recv()
    every_valid = jnp.sum(valid_all[...], axis=0)[0:1]
    count = jnp.sum(every_valid, axis=1, keepdims=True)
    count_out[...] = jnp.broadcast_to(count, count_out.shape)
    logits = dot_tn(head, seeds)
    line = iota(logits.shape, 0)
    peak = jnp.max(logits, axis=0, keepdims=True)
    shifted = jnp.exp(logits - peak)
    totals = jnp.sum(shifted, axis=0, keepdims=True)
    hot = jnp.where(line.astype(f32) == label, 1.0, 0.0)
    nll = peak + jnp.log(totals) - jnp.sum(hot * logits, axis=0, keepdims=True)
    loss = jnp.sum(jnp.where(present > 0, nll, 0.0), axis=1, keepdims=True)
    share = present / jnp.maximum(count, 1.0)
    grad_logits = ((shifted / totals - hot) * share).astype(bf16)
    placed = dot(seat, grad_logits).astype(bf16)
    grad_one[...] = dot_nt(seeds, placed)
    grad_out = dot(head, grad_logits)
    free = 2 * LANES - 3
    part_a = loss.astype(bf16).astype(f32)
    part_b = (loss - part_a).astype(bf16).astype(f32)
    part_c = loss - part_a - part_b
    row, col = iota((hid, LANES), 0), iota((hid, LANES), 1) + LANES
    notes = jnp.where(col == free, part_a, jnp.where(col == free + 1, part_b, part_c))
    notes = jnp.where((col >= free) & (lax.rem(row, unit) == 0), notes, 0.0)
    grad_one[:, LANES:] += notes

    grad_pre = activate_back(grad_out, active_three, slope_three, scale_three)
    grad_weight = dot_nt(joined_three[...], grad_pre).astype(bf16).reshape(chips, 2, -1, hid)
    for c in range(2):
        core_send[1, c] = grad_weight[:, c]
    core_moves = [
        send(core_send.at[1, 1 - core], core_recv.at[1], core_ssem.at[1], core_rsem.at[1], (sibling, z))
    ]
    grad_joined = dot(weight_three, grad_pre)
    grad_mean = (grad_joined[hid:] / degree_c).astype(bf16)
    grad_out = jnp.concatenate([dot_nt(grad_mean, spread_three), grad_joined[0:hid]], axis=1)

    grad_pre = activate_back(grad_out, active_two, slope_two, scale_two)
    grad_weight = dot_nt(joined_two[...], grad_pre).astype(bf16).reshape(chips, 2, -1, hid)
    for c in range(2):
        core_send[0, c] = grad_weight[:, c]
    core_moves += [
        send(core_send.at[0, 1 - core], core_recv.at[0], core_ssem.at[0], core_rsem.at[0], (sibling, z))
    ]
    grad_joined = dot(weight_two, grad_pre)
    grad_mean = (grad_joined[hid:, 0:q1] / degree_t).astype(bf16)
    lead_mean = (grad_joined[hid:, q1:] / degree_b).astype(bf16)

    def back_one(tile, grad_out):
        lanes = pl.ds(tile, grad_out.shape[1])
        pre_one[:, lanes] = activate_back(
            grad_out, active_one[:, lanes], slope_one[:, lanes], scale_one[:, lanes]
        )

    def back_piece(i):
        tile = i * per * LANES
        group = tile // (LANES * r2) * LANES
        back_one(tile, dot_nt(grad_mean[:, group : group + LANES], spread_two[pl.ds(tile, per * LANES), :]))

    own = grad_joined[0:hid]
    back_one(q2, own[:, 0:q1] + dot_nt(lead_mean, spread_lead))
    back_one(q2 + q1, own[:, q1:])
    pieces = q2 // LANES // per
    for i in range(pieces // 2):
        back_piece(i)

    for copy in core_moves:
        copy.wait_recv()
    sums = [core_send[l, core].astype(f32) + core_recv[l].astype(f32) for l in range(2)]
    low_half = iota((1, LANES), 1) < half
    for b in range(2):
        lanes = slice(b * LANES, (b + 1) * LANES)
        left, right = [v[:, :, lanes].reshape(-1, LANES) for v in sums]
        shape = stack_send.shape[1:]
        stack_send[2 * b] = jnp.where(low_half, left, shift_half(right)).astype(bf16).reshape(shape)
        stack_send[2 * b + 1] = jnp.where(low_half, shift_half(left), right).astype(bf16).reshape(shape)
    back_moves = [
        send(
            stack_send.at[lax.rem(z + d, parts), lax.rem(chip + k, chips)], stack_recv.at[i],
            back_ssem.at[i], back_rsem.at[i], place(2 * k, d),
        )
        for i, (k, d) in enumerate(others)
    ]

    for i in range(pieces // 2, pieces):
        back_piece(i)
    grad_one[:, 0:width] += dot_nt(pre_one[...], own_rows[...])
    grad_one[:, LANES : LANES + width] += dot_nt(pre_one[...], mean_one[0:width, :])
    first_send[...] = grad_one[...].astype(bf16)

    group = 2 * unit // 16

    def piece(owner, part):
        slot = lax.rem(owner, group)
        rows = pl.ds(pl.multiple_of(part * unit + slot // 2 * 16, 16), 16)
        return rows, pl.ds(pl.multiple_of(lax.rem(slot, 2) * LANES, LANES), LANES)

    piece_moves = []
    for i, (k, d) in enumerate(everyone):
        owner, part = place(k, d)
        rows, lanes = piece(owner, part)
        piece_moves.append(
            send(first_send.at[rows, lanes], first_recv.at[i], piece_ssem.at[i], piece_rsem.at[i], (owner, part))
        )

    for copy in back_moves:
        copy.wait_recv()
    total = stack_send[z, chip].astype(f32)
    for i in range(len(others)):
        total += stack_recv[i].astype(f32)
    stack_out[...] = total

    for copy in piece_moves:
        copy.wait_recv()
    rows, lanes = piece(s, z)
    total = first_send[rows, lanes].astype(f32)
    for i in range(len(everyone)):
        total += first_recv[i].astype(f32)
    rows, lanes = piece(s, 0)
    first_piece[rows, lanes] = total
    held = first_piece.at[rows, lanes]
    base = s // group * group
    share_moves = []
    for k in range(1, group):
        friend = base + lax.rem(s + k, group)
        share_moves.append(send(held, held, share_ssem.at[k], share_rsem.at[k], (friend, z)))
    for copy in share_moves:
        copy.wait_recv()
    first_out[...] = first_piece[...]

    moves = first_moves + block_moves + valid_moves + [pair_move] + core_moves
    for copy in moves + back_moves + piece_moves + share_moves:
        copy.wait_send()


def step(sizes, *operands):
    n3, n2, n1, n0, parts, seeds_axis, width, classes = sizes
    q2, q1 = n2 // parts, n1 // parts
    r3, r2 = n3 // n2, n2 // n1
    two = q2 + q1 + LANES
    hid = 256
    unit = hid // parts
    chips = seeds_axis // 2
    rows = 2 * hid // seeds_axis
    slots, slots_b = operands[1].shape[0], operands[2].shape[0]
    everyone, others = seeds_axis * parts - 1, chips * parts - 1
    group = 2 * unit // 16
    hbm, vmem = pl.BlockSpec(memory_space=pl.ANY), pl.BlockSpec(memory_space=pltpu.VMEM)
    shape = jax.ShapeDtypeStruct
    dma = pltpu.SemaphoreType.DMA
    return pl.pallas_call(
        functools.partial(step_kernel, sizes),
        out_shape=(shape((unit, hid), f32), shape((rows, LANES), f32), shape((8, LANES), f32)),
        in_specs=[hbm] * 3 + [vmem] * 6,
        out_specs=(vmem,) * 3,
        scratch_shapes=[
            pltpu.VMEM((width, two), bf16),
            pltpu.VMEM((width, two * r3), bf16),
            pltpu.VMEM((width, LANES), bf16),
            pltpu.VMEM((slots, q2 + q1), i32),
            pltpu.VMEM((slots_b, q1), i32),
            pltpu.VMEM((slots, LANES), i32),
            pltpu.VMEM((slots_b, LANES), i32),
            pltpu.VMEM((LANES, two), bf16),
            pltpu.VMEM((hid, two), bf16),
            pltpu.VMEM((hid, two), f32),
            pltpu.VMEM((hid, two), f32),
            pltpu.VMEM((1, two), f32),
            pltpu.VMEM((1, two), f32),
            pltpu.VMEM((two // LANES, 8, LANES), f32),
            pltpu.VMEM((2 * hid, q1 + LANES), bf16),
            pltpu.VMEM((2 * hid, LANES), bf16),
            pltpu.VMEM((q2, LANES), bf16),
            pltpu.VMEM((LANES * r3, LANES), f32),
            pltpu.VMEM((LANES * r2, LANES), f32),
            pltpu.VMEM((hid, two), bf16),
            pltpu.VMEM((hid, hid), bf16),
            pltpu.VMEM((2, parts, chips, rows, LANES), bf16),
            pltpu.VMEM((seeds_axis, 8, LANES), f32),
            pltpu.VMEM((chips, 2, rows, hid), bf16),
            pltpu.VMEM((chips, 2, rows, hid), bf16),
            pltpu.VMEM((2, 2, chips, rows, hid), bf16),
            pltpu.VMEM((2, chips, rows, hid), bf16),
            pltpu.VMEM((parts, chips, rows, LANES), bf16),
            pltpu.VMEM((others, rows, LANES), bf16),
            pltpu.VMEM((hid, hid), f32),
            pltpu.VMEM((hid, hid), bf16),
            pltpu.VMEM((everyone, 16, LANES), bf16),
            pltpu.VMEM((unit, hid), f32),
            dma((11,)),
            dma((parts,)), dma((parts,)),
            dma((others,)), dma((others,)),
            dma(()), dma(()),
            dma((seeds_axis,)), dma((seeds_axis,)),
            dma((2,)), dma((2,)),
            dma((others,)), dma((others,)),
            dma((everyone,)), dma((everyone,)),
            dma((group,)), dma((group,)),
        ],
        compiler_params=pltpu.CompilerParams(
            vmem_limit_bytes=56 * 2**20, collective_id=0, has_side_effects=True
        ),
    )(*operands)


def adamw(weight, moment, square, grad):
    new_moment = beta_first * moment + (1.0 - beta_first) * grad
    new_square = beta_second * square + (1.0 - beta_second) * grad * grad
    moment_hat = new_moment / (1.0 - beta_first**STEP)
    square_hat = new_square / (1.0 - beta_second**STEP)
    new_weight = weight - learn_rate * (
        moment_hat / (jnp.sqrt(square_hat) + epsilon_adam) + decay_rate * weight
    )
    return (new_moment, new_square, new_weight)


def update_kernel(
    width, classes,
    grad_first, grad_stack, count,
    w_a, m_a, s_a, w_b, m_b, s_b, w_c, m_c, s_c,
    loss_out, count_out, om_a, os_a, ow_a, om_b, os_b, ow_b, om_c, os_c, ow_c,
):
    def put(refs, where, values):
        for ref, value in zip(refs, values):
            ref[where] = value

    half = LANES // 2
    for l in range(2):
        grad = grad_stack[:, l * half : (l + 1) * half]
        put((om_b, os_b, ow_b), l, adamw(w_b[l], m_b[l], s_b[l], grad))
    for part in range(2):
        grad = grad_first[:, part * LANES : part * LANES + width]
        lanes = (slice(None), slice(part * width, (part + 1) * width))
        put((om_a, os_a, ow_a), lanes, adamw(w_a[lanes], m_a[lanes], s_a[lanes], grad))
    gap = LANES - width
    flipped = grad_first[...].T
    for start, stop, place in ((0, gap, width), (gap, classes, LANES + width)):
        rows = (slice(start, stop), slice(None))
        grad = flipped[place : place + stop - start]
        put((om_c, os_c, ow_c), rows, adamw(w_c[rows], m_c[rows], s_c[rows], grad))
    free = grad_first.shape[1] - 3
    loss_out[...] = jnp.sum(grad_first[0:1, free:], axis=1, keepdims=True)
    count_out[...] = count[0:1, 0:1]


def update(width, classes, *operands):
    vmem = pl.BlockSpec(memory_space=pltpu.VMEM)
    shape = jax.ShapeDtypeStruct
    outs = [shape((1, 1), f32)] * 2 + [shape(v.shape, f32) for v in operands[3:]]
    return pl.pallas_call(
        functools.partial(update_kernel, width, classes),
        out_shape=tuple(outs),
        in_specs=[vmem] * len(operands),
        out_specs=(vmem,) * len(outs),
    )(*operands)


def per_device(
    features,
    links_first,
    links_second,
    links_third,
    labels,
    valid,
    weight_first,
    moment_first,
    square_first,
    weight_stack,
    moment_stack,
    square_stack,
    weight_head,
    moment_head,
    square_head,
):
    width, classes = features.shape[1], weight_head.shape[1]
    sizes = (
        features.shape[0], links_first.shape[0], links_second.shape[0], links_third.shape[0],
        lax.axis_size("hid"), lax.axis_size("seed"), width, classes,
    )
    grad_first, grad_stack, count = step(
        sizes,
        features.T, links_first.T, links_second.T, links_third.T,
        labels.reshape(1, -1), valid.reshape(1, -1), weight_first.T, weight_stack, weight_head.T,
    )
    loss_sum, count, m_a, s_a, w_a, m_b, s_b, w_b, m_c, s_c, w_c = update(
        width, classes, grad_first, grad_stack, count,
        weight_first.T, moment_first.T, square_first.T,
        weight_stack, moment_stack, square_stack,
        weight_head.T, moment_head.T, square_head.T,
    )
    return (
        loss_sum.reshape(()), count.reshape(()),
        m_a.T, s_a.T, w_a.T,
        m_b, s_b, w_b,
        m_c.T, s_c.T, w_c.T,
    )


def solution(mesh):
    placed = (
        P("seed", None),
        P("seed", None),
        P("seed", None),
        P("seed", None),
        P("seed"),
        P("seed"),
        P(None, "hid"),
        P(None, "hid"),
        P(None, "hid"),
        P(None, "seed", "hid"),
        P(None, "seed", "hid"),
        P(None, "seed", "hid"),
        P("hid", None),
        P("hid", None),
        P("hid", None),
    )
    return jax.shard_map(
        per_device,
        mesh=mesh,
        in_specs=placed,
        out_specs=(P(), P()) + placed[6:],
        check_vma=False,
    )
```

```python
import functools

import jax
import jax.numpy as jnp
from jax import lax
from jax.experimental import pallas as pl
from jax.experimental.pallas import tpu as pltpu
from jax.sharding import PartitionSpec as P

STEP = 5
LANES = 128


epsilon_norm = 1e-06
epsilon_adam = 1e-08
learn_rate = 0.6
decay_rate = 0.01
beta_first = 0.5
beta_second = 0.5

f32, bf16, i32 = jnp.float32, jnp.bfloat16, jnp.int32
MESH = pl.DeviceIdType.MESH
NT = (((1,), (1,)), ((), ()))
TN = (((0,), (0,)), ((), ()))


def dot(a, b):
    return jnp.dot(a, b, preferred_element_type=f32)


def dot_nt(a, b):
    return lax.dot_general(a, b, NT, preferred_element_type=f32)


def dot_tn(a, b):
    return lax.dot_general(a, b, TN, preferred_element_type=f32)


def iota(shape, axis):
    return lax.broadcasted_iota(i32, shape, axis)


def slot_counts(links, first_row, ratio):
    lanes = links.shape[1]
    base = (first_row + iota((1, lanes), 1)) * ratio
    offsets = links - base
    counts = [
        jnp.sum(jnp.where(offsets == r, 1.0, 0.0), axis=0, keepdims=True) for r in range(ratio)
    ]
    degree = jnp.maximum(
        jnp.sum(jnp.where(links >= 0, 1.0, 0.0), axis=0, keepdims=True), 1.0
    )
    return counts, degree


def stripes(counts):
    ratio, lanes = len(counts), counts[0].shape[1]
    which = iota((8, lanes), 0) % ratio
    out = jnp.zeros((8, lanes), f32)
    for r in range(ratio):
        out = jnp.where(which == r, counts[r], out)
    return out


def spread(mask, stripe):
    rows = mask.shape[0]
    values = mask.reshape(rows // 8, 8, LANES) * stripe[None]
    return values.reshape(rows, LANES).astype(bf16)


def window_mask(rows, ratio):
    return jnp.where(iota((rows, LANES), 0) // ratio == iota((rows, LANES), 1), 1.0, 0.0)


def activate(preact):
    logistic = 1.0 / (1.0 + jnp.exp(-preact))
    active = preact * logistic
    slope = logistic * (1.0 + preact * (1.0 - logistic))
    scaling = lax.rsqrt(jnp.sum(active * active, axis=0, keepdims=True) + epsilon_norm)
    return (active * scaling).astype(bf16), active, slope, scaling


def activate_back(grad_out, active, slope, scaling):
    inner = jnp.sum(active * grad_out, axis=0, keepdims=True)
    grad_active = scaling * grad_out - active * (scaling * scaling * scaling * inner)
    return (grad_active * slope).astype(bf16)


def placement_rows(classes, columns, width):
    gap = LANES - width
    row, col = iota((classes, columns), 0), iota((classes, columns), 1)
    target = jnp.where(row < gap, width + row, LANES + width + row - gap)
    return jnp.where(col == target, 1.0, 0.0).astype(bf16)


def placement(rows, classes, width):
    gap = LANES - width
    row, col = iota((rows, classes), 0), iota((rows, classes), 1)
    target = jnp.where(col < gap, width + col, LANES + width + col - gap)
    return jnp.where(row == target, 1.0, 0.0).astype(bf16)


def shift_half(x):
    return pltpu.roll(x, LANES // 2, 1)


def step_kernel(
    sizes,
    features, links_first, links_second, links_third, labels, valid, weight_first, weight_stack, weight_head,
    first_out, stack_out, count_out,
    own_rows, child_rows, own_lead, links_a, links_b, links_a_lead, links_b_lead,
    mean_one, hidden_one, active_one, slope_one, scale_one, degree_rows, stripe_rows,
    joined_two, joined_three, spread_two, mask_four, mask_eight, pre_one,
    first_all, stack_all, valid_all, low_stack,
    core_send, core_recv, plane_send, plane_recv, turn_send, turn_recv,
    grad_one, first_send, first_recv, first_piece, first_own, stack_own, head_own,
    local_sems, first_sems, block_sems, chips_sems, pair_sems, valid_sems,
    core_sems, plane_sems, turn_sems, piece_sems, share_sems,
):
    n3, n2, n1, n0, parts, seeds_axis, width, classes = sizes
    q2, q1, q0 = n2 // parts, n1 // parts, n0 // parts
    r3, r2, r1 = n3 // n2, n2 // n1, n1 // n0
    s, z = lax.axis_index("seed"), lax.axis_index("hid")
    core, chip = lax.rem(s, 2), s // 2
    chips = seeds_axis // 2
    sibling = s + 1 - 2 * core
    two = q2 + q1 + LANES
    hid = 256
    unit = hid // parts
    own_units = pl.ds(pl.multiple_of(z * unit, unit), unit)
    everyone = [(k, d) for d in range(parts) for k in range(seeds_axis) if (k, d) != (0, 0)]
    near = [(k, d) for k, d in everyone if k == 0 or d == 0]

    def place(k, d):
        return (lax.rem(s + k, seeds_axis), lax.rem(z + d, parts))

    barrier = pltpu.get_barrier_semaphore()
    for k, d in near:
        pl.semaphore_signal(barrier, inc=1, device_id=place(k, d), device_id_type=MESH)

    def at(size):
        return pl.ds(pl.multiple_of(z * size, LANES), size)

    copies = [
        (weight_stack, stack_own),
        (weight_first, first_own),
        (weight_head, head_own),
        (links_first.at[:, at(q2)], links_a.at[:, pl.ds(0, q2)]),
        (links_first.at[:, at(q1)], links_a.at[:, pl.ds(q2, q1)]),
        (links_first.at[:, pl.ds(0, LANES)], links_a_lead),
        (links_second.at[:, at(q1)], links_b),
        (links_second.at[:, pl.ds(0, LANES)], links_b_lead),
        (features.at[:, pl.ds(0, LANES)], own_lead),
        (features.at[:, at(q2)], own_rows.at[:, pl.ds(0, q2)]),
        (features.at[:, at(q1)], own_rows.at[:, pl.ds(q2, q1)]),
        (features.at[:, at(q2 * r3)], child_rows.at[:, pl.ds(0, q2 * r3)]),
        (features.at[:, at(q1 * r3)], child_rows.at[:, pl.ds(q2 * r3, q1 * r3)]),
        (
            features.at[:, pl.ds(pl.multiple_of(z * q0 * r3, LANES), LANES * r3)],
            child_rows.at[:, pl.ds((q2 + q1) * r3, LANES * r3)],
        ),
    ]
    started = [pltpu.make_async_copy(src, dst, local_sems.at[i]) for i, (src, dst) in enumerate(copies)]
    for copy in started:
        copy.start()

    for copy in started[:3]:
        copy.wait()
    half = unit
    depth = stack_own.shape[1]
    short = depth // 2
    row, col = iota((half, LANES), 0), iota((half, LANES), 1)
    to_left = jnp.where(row == col, 1.0, 0.0).astype(bf16)
    to_right = jnp.where(row + half == col, 1.0, 0.0).astype(bf16)
    for l in range(2):
        block = dot(stack_own[l, 0:short].astype(bf16), to_left)
        block += dot(stack_own[l, short:].astype(bf16), to_right)
        stack_all[l, core, z, chip] = block.astype(bf16)
    row, col = iota((2 * width, hid), 0), iota((2 * width, hid), 1)
    columns = jnp.where(row < width, row, row - width + LANES)
    lift = jnp.where(columns == col, 1.0, 0.0).astype(bf16)
    seat = placement(hid, classes, width)
    shard = dot(first_own[...].astype(bf16), lift)
    shard += dot_tn(head_own[...].astype(bf16), placement_rows(classes, hid, width))
    first_all[own_units, :] = shard.astype(bf16)
    valid_all[s] = jnp.broadcast_to(valid[...].astype(f32), valid_all.shape[1:])

    pl.semaphore_wait(barrier, len(near))

    moves = []

    def send(src, dst, sems, where, device):
        copy = pltpu.make_async_remote_copy(
            src_ref=src, dst_ref=dst, send_sem=sems.at[(0, *where)], recv_sem=sems.at[(1, *where)],
            device_id=device, device_id_type=MESH,
        )
        copy.start()
        moves.append(copy)
        return copy

    def arrive(copies):
        for copy in copies:
            copy.wait_recv()

    def send_blocks(l):
        mine = stack_all.at[l, core, z, chip]
        return [send(mine, mine, block_sems, (l, d), place(0, d)) for d in range(1, parts)]

    def send_chips(l):
        mine = stack_all.at[l, core, :, chip]
        return [send(mine, mine, chips_sems, (l, k), place(2 * k, 0)) for k in range(1, chips)]

    def send_pair(l):
        mine = stack_all.at[l, core]
        return [send(mine, mine, pair_sems, (l,), (sibling, z))]

    block_moves = [send_blocks(0)]
    first_moves = [
        send(first_all.at[own_units], first_all.at[own_units], first_sems, (d,), place(0, d))
        for d in range(1, parts)
    ]
    block_moves += [send_blocks(1)]
    valid_moves = [
        send(valid_all.at[s], valid_all.at[s], valid_sems, (k,), place(k, 0)) for k in range(1, seeds_axis)
    ]

    mask_four[...] = window_mask(LANES * r3, r3)
    mask_eight[...] = window_mask(LANES * r2, r2)
    mean_one[...] = jnp.zeros_like(mean_one)
    for copy in started[3:]:
        copy.wait()

    counts_a, degree_a = slot_counts(links_a_lead[...], 0, r3)
    counts_b, degree_b = slot_counts(links_b_lead[...], 0, r2)
    counts_c, degree_c = slot_counts(links_third[...], 0, r1)
    lead = [*counts_a, degree_a, *counts_b, degree_b, *counts_c, degree_c]
    lead += [labels[...].astype(f32), valid[...].astype(f32)]
    packed = jnp.zeros((32, LANES), f32)
    for k, line in enumerate(lead):
        packed = jnp.where(iota((32, LANES), 0) == k, line, packed)
    source, target = iota((LANES, LANES), 0), iota((LANES, LANES), 1)
    mine = jnp.where((source == target + z * q0) & (target < q0), 1.0, 0.0).astype(bf16)
    packed = dot(packed.astype(bf16), mine)
    take = [packed[k : k + 1] for k in range(len(lead))]
    counts_a, degree_a = take[:r3], jnp.maximum(take[r3], 1.0)
    take = take[r3 + 1 :]
    counts_b, degree_b = take[:r2], jnp.maximum(take[r2], 1.0)
    take = take[r2 + 1 :]
    counts_c, degree_c = take[:r1], jnp.maximum(take[r1], 1.0)
    label, present = take[r1 + 1], take[r1 + 2]
    own_rows[:, pl.ds(q2 + q1, LANES)] = dot(own_lead[...], mine).astype(bf16)

    counts, degree = slot_counts(links_a[:, pl.ds(0, q2)], z * q2, r3)
    for t in range(q2 // LANES):
        stripe_rows[t] = stripes([c[:, t * LANES : (t + 1) * LANES] for c in counts])
    degree_rows[:, pl.ds(0, q2)] = degree
    counts, degree = slot_counts(links_a[:, pl.ds(q2, q1)], z * q1, r3)
    for t in range(q1 // LANES):
        stripe_rows[q2 // LANES + t] = stripes([c[:, t * LANES : (t + 1) * LANES] for c in counts])
    degree_rows[:, pl.ds(q2, q1)] = degree
    stripe_rows[two // LANES - 1] = stripes(counts_a)
    degree_rows[:, pl.ds(q2 + q1, LANES)] = degree_a

    def mean_tiles(tile, tiles):
        for t in range(tiles):
            lanes = pl.ds(pl.multiple_of((tile + t) * LANES, LANES), LANES)
            kids = pl.ds(pl.multiple_of((tile + t) * LANES * r3, LANES), LANES * r3)
            matrix = spread(mask_four[...], stripe_rows[tile + t])
            mean = dot(child_rows[:, kids], matrix) / degree_rows[:, lanes]
            mean_one[0:width, lanes] = mean.astype(bf16)

    def layer_one(tile, tiles):
        lanes = pl.ds(pl.multiple_of(tile * LANES, LANES), LANES * tiles)
        preact = dot(first_all[:, 0:width], own_rows[:, lanes])
        preact += dot(first_all[:, LANES : 2 * LANES], mean_one[:, lanes])
        output, active, slope, scaling = activate(preact)
        hidden_one[:, lanes] = output
        active_one[:, lanes] = active
        slope_one[:, lanes] = slope
        scale_one[:, lanes] = scaling

    per = 4
    tail = q1 // LANES + 1
    lax.fori_loop(0, q2 // LANES // per, lambda i, c: (mean_tiles(i * per, per), c)[1], 0)
    mean_tiles(q2 // LANES, tail)

    counts, degree_t = slot_counts(links_b[...], z * q1, r2)
    for t in range(q1 // LANES):
        stripe = stripes([c[:, t * LANES : (t + 1) * LANES] for c in counts])
        spread_two[pl.ds(t * LANES * r2, LANES * r2), :] = spread(mask_eight[...], stripe)
    spread_lead = spread(mask_eight[0 : q0 * r2, :], stripes(counts_b))
    spread_three = spread(mask_eight[0 : q0 * r1, :], stripes(counts_c))

    arrive(block_moves[0])
    chips_moves = [send_chips(0)]
    arrive(first_moves)
    arrive(block_moves[1])
    chips_moves += [send_chips(1)]
    lax.fori_loop(0, q2 // LANES // per, lambda i, c: (layer_one(i * per, per), c)[1], 0)
    layer_one(q2 // LANES, tail)
    arrive(chips_moves[0])
    pair_moves = [send_pair(0)]

    joined_two[0:hid, :] = hidden_one[:, pl.ds(q2, q1 + LANES)]
    for t in range(q1 // LANES):
        rows = pl.ds(t * LANES * r2, LANES * r2)
        mean = dot(hidden_one[:, rows], spread_two[rows, :])
        lanes = slice(t * LANES, (t + 1) * LANES)
        joined_two[hid:, lanes] = (mean / degree_t[:, lanes]).astype(bf16)
    mean = dot(hidden_one[:, pl.ds(q2, q1)], spread_lead)
    joined_two[hid:, pl.ds(q1, LANES)] = (mean / degree_b).astype(bf16)

    low_half = iota((1, LANES), 1) < half

    def interleave(left, right):
        return jnp.where(low_half, left, shift_half(right)), jnp.where(low_half, shift_half(left), right)

    def gathered(l):
        for b in range(parts // 2):
            for c in range(2):
                left = stack_all[l, c, 2 * b].astype(f32).reshape(-1, LANES)
                right = stack_all[l, c, 2 * b + 1].astype(f32).reshape(-1, LANES)
                for h, value in enumerate(interleave(left, right)):
                    lanes = slice(b * LANES, (b + 1) * LANES)
                    low_stack[l, :, c, h, :, lanes] = value.astype(bf16).reshape(chips, short, LANES)
        return low_stack[l].reshape(2 * hid, hid)

    arrive(pair_moves[0])
    weight_two = gathered(0)
    preact = dot_tn(weight_two, joined_two[...])
    output, active_two, slope_two, scale_two = activate(preact)

    arrive(chips_moves[1])
    pair_moves += [send_pair(1)]

    joined_three[0:hid, :] = output[:, q1:]
    mean = dot(output[:, 0:q1], spread_three)
    joined_three[hid:, :] = (mean / degree_c).astype(bf16)
    arrive(pair_moves[1])
    weight_three = gathered(1)
    preact = dot_tn(weight_three, joined_three[...])
    seeds, active_three, slope_three, scale_three = activate(preact)

    head = dot(first_all[...], seat).astype(bf16)
    arrive(valid_moves)
    every_valid = jnp.sum(valid_all[...], axis=0)[0:1]
    count = jnp.sum(every_valid, axis=1, keepdims=True)
    count_out[...] = jnp.broadcast_to(count, count_out.shape)
    logits = dot_tn(head, seeds)
    line = iota(logits.shape, 0)
    peak = jnp.max(logits, axis=0, keepdims=True)
    shifted = jnp.exp(logits - peak)
    totals = jnp.sum(shifted, axis=0, keepdims=True)
    hot = jnp.where(line.astype(f32) == label, 1.0, 0.0)
    nll = peak + jnp.log(totals) - jnp.sum(hot * logits, axis=0, keepdims=True)
    loss = jnp.sum(jnp.where(present > 0, nll, 0.0), axis=1, keepdims=True)
    share = present / jnp.maximum(count, 1.0)
    grad_logits = ((shifted / totals - hot) * share).astype(bf16)
    placed = dot(seat, grad_logits).astype(bf16)
    grad_one[...] = dot_nt(seeds, placed)
    grad_out = dot(head, grad_logits)
    free = 2 * LANES - 3
    part_a = loss.astype(bf16).astype(f32)
    part_b = (loss - part_a).astype(bf16).astype(f32)
    part_c = loss - part_a - part_b
    row, col = iota((hid, LANES), 0), iota((hid, LANES), 1) + LANES
    notes = jnp.where(col == free, part_a, jnp.where(col == free + 1, part_b, part_c))
    notes = jnp.where((col >= free) & (lax.rem(row, unit) == 0), notes, 0.0)
    grad_one[:, LANES:] += notes

    def keep_grad(l, value):
        value = value.astype(bf16).reshape(chips, 2, depth, hid)
        for c in range(2):
            core_send[l, c] = value[:, c]

    def send_core(l):
        return [send(core_send.at[l, 1 - core], core_recv.at[l], core_sems, (l,), (sibling, z))]

    def send_plane(l):
        plane_send[l] = (core_send[l, core].astype(f32) + core_recv[l].astype(f32)).astype(bf16)
        return [
            send(plane_send.at[l, lax.rem(chip + k, chips)], plane_recv.at[l, k], plane_sems, (l, k), place(2 * k, 0))
            for k in range(1, chips)
        ]

    def send_turn(l):
        total = plane_send[l, chip].astype(f32)
        for k in range(1, chips):
            total += plane_recv[l, k].astype(f32)
        for b in range(parts // 2):
            lanes = slice(b * LANES, (b + 1) * LANES)
            for h, value in enumerate(interleave(total[0:short, lanes], total[short:, lanes])):
                turn_send[l, 2 * b + h] = value.astype(bf16)
        return [
            send(turn_send.at[l, lax.rem(z + d, parts)], turn_recv.at[l, d], turn_sems, (l, d), place(0, d))
            for d in range(1, parts)
        ]

    def finish_stack(l):
        total = turn_send[l, z].astype(f32)
        for d in range(1, parts):
            total += turn_recv[l, d].astype(f32)
        stack_out[l] = total

    grad_pre = activate_back(grad_out, active_three, slope_three, scale_three)
    keep_grad(1, dot_nt(joined_three[...], grad_pre))
    grad_joined = dot(weight_three, grad_pre)
    grad_mean = (grad_joined[hid:] / degree_c).astype(bf16)
    grad_out = jnp.concatenate([dot_nt(grad_mean, spread_three), grad_joined[0:hid]], axis=1)
    core_moves = [None, send_core(1)]

    grad_pre = activate_back(grad_out, active_two, slope_two, scale_two)
    keep_grad(0, dot_nt(joined_two[...], grad_pre))
    grad_joined = dot(weight_two, grad_pre)
    grad_mean = (grad_joined[hid:, 0:q1] / degree_t).astype(bf16)
    lead_mean = (grad_joined[hid:, q1:] / degree_b).astype(bf16)
    core_moves[0] = send_core(0)

    def back_one(tile, grad_out):
        lanes = pl.ds(tile, grad_out.shape[1])
        pre_one[:, lanes] = activate_back(
            grad_out, active_one[:, lanes], slope_one[:, lanes], scale_one[:, lanes]
        )

    def back_piece(i):
        tile = i * per * LANES
        group = tile // (LANES * r2) * LANES
        back_one(tile, dot_nt(grad_mean[:, group : group + LANES], spread_two[pl.ds(tile, per * LANES), :]))

    own = grad_joined[0:hid]
    back_one(q2, own[:, 0:q1] + dot_nt(lead_mean, spread_lead))
    back_one(q2 + q1, own[:, q1:])
    for i in range(q2 // LANES // per):
        back_piece(i)
    grad_one[:, 0:width] += dot_nt(pre_one[...], own_rows[...])
    grad_one[:, LANES : LANES + width] += dot_nt(pre_one[...], mean_one[0:width, :])
    first_send[...] = grad_one[...].astype(bf16)

    group = 2 * unit // 16

    def piece(owner, part):
        slot = lax.rem(owner, group)
        rows = pl.ds(pl.multiple_of(part * unit + slot // 2 * 16, 16), 16)
        return rows, pl.ds(pl.multiple_of(lax.rem(slot, 2) * LANES, LANES), LANES)

    piece_moves = []
    for i, (k, d) in enumerate(everyone):
        owner, part = place(k, d)
        rows, lanes = piece(owner, part)
        piece_moves.append(
            send(first_send.at[rows, lanes], first_recv.at[i], piece_sems, (i,), (owner, part))
        )

    plane_moves, turn_moves = [None, None], [None, None]
    for l in (1, 0):
        arrive(core_moves[l])
        plane_moves[l] = send_plane(l)
    for l in (1, 0):
        arrive(plane_moves[l])
        turn_moves[l] = send_turn(l)

    arrive(piece_moves)
    rows, lanes = piece(s, z)
    total = first_send[rows, lanes].astype(f32)
    for i in range(len(everyone)):
        total += first_recv[i].astype(f32)
    rows, lanes = piece(s, 0)
    first_piece[rows, lanes] = total
    held = first_piece.at[rows, lanes]
    base = s // group * group
    share_moves = []
    for k in range(1, group):
        friend = base + lax.rem(s + k, group)
        share_moves.append(send(held, held, share_sems, (k,), (friend, z)))
    for l in (1, 0):
        arrive(turn_moves[l])
        finish_stack(l)
    arrive(share_moves)
    first_out[...] = first_piece[...]

    for copy in moves:
        copy.wait_send()


def step(sizes, *operands):
    n3, n2, n1, n0, parts, seeds_axis, width, classes = sizes
    q2, q1 = n2 // parts, n1 // parts
    r3, r2 = n3 // n2, n2 // n1
    two = q2 + q1 + LANES
    hid = 256
    unit = hid // parts
    chips = seeds_axis // 2
    rows = 2 * hid // seeds_axis
    slots, slots_b = operands[1].shape[0], operands[2].shape[0]
    everyone = seeds_axis * parts - 1
    short = rows // 2
    group = 2 * unit // 16
    hbm, vmem = pl.BlockSpec(memory_space=pl.ANY), pl.BlockSpec(memory_space=pltpu.VMEM)
    shape = jax.ShapeDtypeStruct
    dma = pltpu.SemaphoreType.DMA
    return pl.pallas_call(
        functools.partial(step_kernel, sizes),
        out_shape=(shape((unit, hid), f32), shape((2, short, LANES), f32), shape((8, LANES), f32)),
        in_specs=[hbm] * 3 + [vmem] * 3 + [hbm] * 3,
        out_specs=(vmem,) * 3,
        scratch_shapes=[
            pltpu.VMEM((width, two), bf16),
            pltpu.VMEM((width, two * r3), bf16),
            pltpu.VMEM((width, LANES), bf16),
            pltpu.VMEM((slots, q2 + q1), i32),
            pltpu.VMEM((slots_b, q1), i32),
            pltpu.VMEM((slots, LANES), i32),
            pltpu.VMEM((slots_b, LANES), i32),
            pltpu.VMEM((LANES, two), bf16),
            pltpu.VMEM((hid, two), bf16),
            pltpu.VMEM((hid, two), f32),
            pltpu.VMEM((hid, two), f32),
            pltpu.VMEM((1, two), f32),
            pltpu.VMEM((1, two), f32),
            pltpu.VMEM((two // LANES, 8, LANES), f32),
            pltpu.VMEM((2 * hid, q1 + LANES), bf16),
            pltpu.VMEM((2 * hid, LANES), bf16),
            pltpu.VMEM((q2, LANES), bf16),
            pltpu.VMEM((LANES * r3, LANES), f32),
            pltpu.VMEM((LANES * r2, LANES), f32),
            pltpu.VMEM((hid, two), bf16),
            pltpu.VMEM((hid, hid), bf16),
            pltpu.VMEM((2, 2, parts, chips, short, LANES), bf16),
            pltpu.VMEM((seeds_axis, 8, LANES), f32),
            pltpu.VMEM((2, chips, 2, 2, short, hid), bf16),
            pltpu.VMEM((2, 2, chips, rows, hid), bf16),
            pltpu.VMEM((2, chips, rows, hid), bf16),
            pltpu.VMEM((2, chips, rows, hid), bf16),
            pltpu.VMEM((2, chips, rows, hid), bf16),
            pltpu.VMEM((2, parts, short, LANES), bf16),
            pltpu.VMEM((2, parts, short, LANES), bf16),
            pltpu.VMEM((hid, hid), f32),
            pltpu.VMEM((hid, hid), bf16),
            pltpu.VMEM((everyone, 16, LANES), bf16),
            pltpu.VMEM((unit, hid), f32),
            *[pltpu.VMEM(v.shape, f32) for v in operands[6:]],
            dma((14,)),
            dma((2, parts)),
            dma((2, 2, parts)),
            dma((2, 2, chips)),
            dma((2, 2)),
            dma((2, seeds_axis)),
            dma((2, 2)),
            dma((2, 2, chips)),
            dma((2, 2, parts)),
            dma((2, everyone)),
            dma((2, group)),
        ],
        compiler_params=pltpu.CompilerParams(
            vmem_limit_bytes=56 * 2**20, collective_id=0, has_side_effects=True
        ),
    )(*operands)


def adamw(weight, moment, square, grad):
    new_moment = beta_first * moment + (1.0 - beta_first) * grad
    new_square = beta_second * square + (1.0 - beta_second) * grad * grad
    moment_hat = new_moment / (1.0 - beta_first**STEP)
    square_hat = new_square / (1.0 - beta_second**STEP)
    new_weight = weight - learn_rate * (
        moment_hat / (jnp.sqrt(square_hat) + epsilon_adam) + decay_rate * weight
    )
    return (new_moment, new_square, new_weight)


def update_kernel(
    width, classes,
    grad_first, grad_stack, count,
    w_a, m_a, s_a, w_b, m_b, s_b, w_c, m_c, s_c,
    loss_out, count_out, om_a, os_a, ow_a, om_b, os_b, ow_b, om_c, os_c, ow_c,
):
    def put(refs, where, values):
        for ref, value in zip(refs, values):
            ref[where] = value

    half = LANES // 2
    short = grad_stack.shape[1]
    for l in range(2):
        for h in range(2):
            grad = grad_stack[l, :, h * half : (h + 1) * half]
            rows = (l, slice(h * short, (h + 1) * short))
            put((om_b, os_b, ow_b), rows, adamw(w_b[rows], m_b[rows], s_b[rows], grad))
    for part in range(2):
        grad = grad_first[:, part * LANES : part * LANES + width]
        lanes = (slice(None), slice(part * width, (part + 1) * width))
        put((om_a, os_a, ow_a), lanes, adamw(w_a[lanes], m_a[lanes], s_a[lanes], grad))
    gap = LANES - width
    flipped = grad_first[...].T
    for start, stop, place in ((0, gap, width), (gap, classes, LANES + width)):
        rows = (slice(start, stop), slice(None))
        grad = flipped[place : place + stop - start]
        put((om_c, os_c, ow_c), rows, adamw(w_c[rows], m_c[rows], s_c[rows], grad))
    free = grad_first.shape[1] - 3
    loss_out[...] = jnp.sum(grad_first[0:1, free:], axis=1, keepdims=True)
    count_out[...] = count[0:1, 0:1]


def update(width, classes, *operands):
    vmem = pl.BlockSpec(memory_space=pltpu.VMEM)
    shape = jax.ShapeDtypeStruct
    outs = [shape((1, 1), f32)] * 2 + [shape(v.shape, f32) for v in operands[3:]]
    return pl.pallas_call(
        functools.partial(update_kernel, width, classes),
        out_shape=tuple(outs),
        in_specs=[vmem] * len(operands),
        out_specs=(vmem,) * len(outs),
    )(*operands)


def per_device(
    features,
    links_first,
    links_second,
    links_third,
    labels,
    valid,
    weight_first,
    moment_first,
    square_first,
    weight_stack,
    moment_stack,
    square_stack,
    weight_head,
    moment_head,
    square_head,
):
    width, classes = features.shape[1], weight_head.shape[1]
    sizes = (
        features.shape[0], links_first.shape[0], links_second.shape[0], links_third.shape[0],
        lax.axis_size("hid"), lax.axis_size("seed"), width, classes,
    )
    grad_first, grad_stack, count = step(
        sizes,
        features.T, links_first.T, links_second.T, links_third.T,
        labels.reshape(1, -1), valid.reshape(1, -1), weight_first.T, weight_stack, weight_head.T,
    )
    loss_sum, count, m_a, s_a, w_a, m_b, s_b, w_b, m_c, s_c, w_c = update(
        width, classes, grad_first, grad_stack, count,
        weight_first.T, moment_first.T, square_first.T,
        weight_stack, moment_stack, square_stack,
        weight_head.T, moment_head.T, square_head.T,
    )
    return (
        loss_sum.reshape(()), count.reshape(()),
        m_a.T, s_a.T, w_a.T,
        m_b, s_b, w_b,
        m_c.T, s_c.T, w_c.T,
    )


def solution(mesh):
    placed = (
        P("seed", None),
        P("seed", None),
        P("seed", None),
        P("seed", None),
        P("seed"),
        P("seed"),
        P(None, "hid"),
        P(None, "hid"),
        P(None, "hid"),
        P(None, "seed", "hid"),
        P(None, "seed", "hid"),
        P(None, "seed", "hid"),
        P("hid", None),
        P("hid", None),
        P("hid", None),
    )
    return jax.shard_map(
        per_device,
        mesh=mesh,
        in_specs=placed,
        out_specs=(P(), P()) + placed[6:],
        check_vma=False,
    )
```

```python
import functools

import jax
import jax.numpy as jnp
from jax import lax
from jax.experimental import pallas as pl
from jax.experimental.pallas import tpu as pltpu
from jax.sharding import PartitionSpec as P

STEP = 5
LANES = 128


epsilon_norm = 1e-06
epsilon_adam = 1e-08
learn_rate = 0.6
decay_rate = 0.01
beta_first = 0.5
beta_second = 0.5

f32, bf16, i32 = jnp.float32, jnp.bfloat16, jnp.int32
MESH = pl.DeviceIdType.MESH
NT = (((1,), (1,)), ((), ()))
TN = (((0,), (0,)), ((), ()))


def dot(a, b):
    return jnp.dot(a, b, preferred_element_type=f32)


def dot_nt(a, b):
    return lax.dot_general(a, b, NT, preferred_element_type=f32)


def dot_tn(a, b):
    return lax.dot_general(a, b, TN, preferred_element_type=f32)


def iota(shape, axis):
    return lax.broadcasted_iota(i32, shape, axis)


def slot_counts(links, first_row, ratio):
    lanes = links.shape[1]
    base = (first_row + iota((1, lanes), 1)) * ratio
    offsets = links - base
    counts = [
        jnp.sum(jnp.where(offsets == r, 1.0, 0.0), axis=0, keepdims=True) for r in range(ratio)
    ]
    degree = jnp.maximum(
        jnp.sum(jnp.where(links >= 0, 1.0, 0.0), axis=0, keepdims=True), 1.0
    )
    return counts, degree


def stripes(counts):
    ratio, lanes = len(counts), counts[0].shape[1]
    which = iota((8, lanes), 0) % ratio
    out = jnp.zeros((8, lanes), f32)
    for r in range(ratio):
        out = jnp.where(which == r, counts[r], out)
    return out


def spread(mask, stripe):
    rows = mask.shape[0]
    values = mask.reshape(rows // 8, 8, LANES) * stripe[None]
    return values.reshape(rows, LANES).astype(bf16)


def window_mask(rows, ratio):
    return jnp.where(iota((rows, LANES), 0) // ratio == iota((rows, LANES), 1), 1.0, 0.0)


def activate(preact):
    logistic = 1.0 / (1.0 + jnp.exp(-preact))
    active = preact * logistic
    slope = logistic * (1.0 + preact * (1.0 - logistic))
    scaling = lax.rsqrt(jnp.sum(active * active, axis=0, keepdims=True) + epsilon_norm)
    return (active * scaling).astype(bf16), active, slope, scaling


def activate_back(grad_out, active, slope, scaling):
    inner = jnp.sum(active * grad_out, axis=0, keepdims=True)
    grad_active = scaling * grad_out - active * (scaling * scaling * scaling * inner)
    return (grad_active * slope).astype(bf16)


def placement_rows(classes, columns, width):
    gap = LANES - width
    row, col = iota((classes, columns), 0), iota((classes, columns), 1)
    target = jnp.where(row < gap, width + row, LANES + width + row - gap)
    return jnp.where(col == target, 1.0, 0.0).astype(bf16)


def placement(rows, classes, width):
    gap = LANES - width
    row, col = iota((rows, classes), 0), iota((rows, classes), 1)
    target = jnp.where(col < gap, width + col, LANES + width + col - gap)
    return jnp.where(row == target, 1.0, 0.0).astype(bf16)


def shift_half(x):
    return pltpu.roll(x, LANES // 2, 1)


def step_kernel(
    sizes,
    features, links_first, links_second, links_third, labels, valid, weight_first, weight_stack, weight_head,
    first_out, stack_out,
    own_rows, child_rows, own_lead, links_a, links_b, links_a_lead, links_b_lead,
    mean_one, hidden_one, active_one, slope_one, scale_one, degree_rows, stripe_rows,
    joined_two, joined_three, spread_two, mask_four, mask_eight, pre_one,
    first_all, stack_all, valid_all, low_stack,
    core_send, core_recv, plane_send, plane_recv, turn_send, turn_recv,
    grad_one, first_send, first_recv, first_piece, first_own, stack_own, head_own,
    links_c, labels_own, valid_own,
    local_sems, first_sems, block_sems, chips_sems, pair_sems, valid_sems,
    core_sems, plane_sems, turn_sems, piece_sems, share_sems,
):
    n3, n2, n1, n0, parts, seeds_axis, width, classes = sizes
    q2, q1, q0 = n2 // parts, n1 // parts, n0 // parts
    r3, r2, r1 = n3 // n2, n2 // n1, n1 // n0
    s, z = lax.axis_index("seed"), lax.axis_index("hid")
    core, chip = lax.rem(s, 2), s // 2
    chips = seeds_axis // 2
    sibling = s + 1 - 2 * core
    two = q2 + q1 + LANES
    hid = 256
    unit = hid // parts
    own_units = pl.ds(pl.multiple_of(z * unit, unit), unit)
    everyone = [(k, d) for d in range(parts) for k in range(seeds_axis) if (k, d) != (0, 0)]
    near = [(k, d) for k, d in everyone if k == 0 or d == 0]

    def place(k, d):
        return (lax.rem(s + k, seeds_axis), lax.rem(z + d, parts))

    barrier = pltpu.get_barrier_semaphore()
    for k, d in near:
        pl.semaphore_signal(barrier, inc=1, device_id=place(k, d), device_id_type=MESH)

    def at(size):
        return pl.ds(pl.multiple_of(z * size, LANES), size)

    copies = [
        (weight_stack, stack_own),
        (weight_first, first_own),
        (weight_head, head_own),
        (valid, valid_own),
        (labels, labels_own),
        (links_third, links_c),
        (links_first.at[:, at(q2)], links_a.at[:, pl.ds(0, q2)]),
        (links_first.at[:, at(q1)], links_a.at[:, pl.ds(q2, q1)]),
        (links_first.at[:, pl.ds(0, LANES)], links_a_lead),
        (links_second.at[:, at(q1)], links_b),
        (links_second.at[:, pl.ds(0, LANES)], links_b_lead),
        (features.at[:, pl.ds(0, LANES)], own_lead),
        (features.at[:, at(q2)], own_rows.at[:, pl.ds(0, q2)]),
        (features.at[:, at(q1)], own_rows.at[:, pl.ds(q2, q1)]),
        (features.at[:, at(q2 * r3)], child_rows.at[:, pl.ds(0, q2 * r3)]),
        (features.at[:, at(q1 * r3)], child_rows.at[:, pl.ds(q2 * r3, q1 * r3)]),
        (
            features.at[:, pl.ds(pl.multiple_of(z * q0 * r3, LANES), LANES * r3)],
            child_rows.at[:, pl.ds((q2 + q1) * r3, LANES * r3)],
        ),
    ]
    started = [pltpu.make_async_copy(src, dst, local_sems.at[i]) for i, (src, dst) in enumerate(copies)]
    for copy in started:
        copy.start()

    for copy in started[:4]:
        copy.wait()
    half = unit
    depth = stack_own.shape[1]
    short = depth // 2
    row, col = iota((half, LANES), 0), iota((half, LANES), 1)
    to_left = jnp.where(row == col, 1.0, 0.0).astype(bf16)
    to_right = jnp.where(row + half == col, 1.0, 0.0).astype(bf16)
    for l in range(2):
        block = dot(stack_own[l, 0:short].astype(bf16), to_left)
        block += dot(stack_own[l, short:].astype(bf16), to_right)
        stack_all[l, core, z, chip] = block.astype(bf16)
    row, col = iota((2 * width, hid), 0), iota((2 * width, hid), 1)
    columns = jnp.where(row < width, row, row - width + LANES)
    lift = jnp.where(columns == col, 1.0, 0.0).astype(bf16)
    seat = placement(hid, classes, width)
    shard = dot(first_own[...].astype(bf16), lift)
    shard += dot_tn(head_own[...].astype(bf16), placement_rows(classes, hid, width))
    first_all[own_units, :] = shard.astype(bf16)
    valid_all[s] = jnp.broadcast_to(valid_own[...].astype(f32), valid_all.shape[1:])

    pl.semaphore_wait(barrier, len(near))

    moves = []

    def send(src, dst, sems, where, device):
        copy = pltpu.make_async_remote_copy(
            src_ref=src, dst_ref=dst, send_sem=sems.at[(0, *where)], recv_sem=sems.at[(1, *where)],
            device_id=device, device_id_type=MESH,
        )
        copy.start()
        moves.append(copy)
        return copy

    def arrive(copies):
        for copy in copies:
            copy.wait_recv()

    def send_blocks(l):
        mine = stack_all.at[l, core, z, chip]
        return [send(mine, mine, block_sems, (l, d), place(0, d)) for d in range(1, parts)]

    def send_chips(l):
        mine = stack_all.at[l, core, :, chip]
        return [send(mine, mine, chips_sems, (l, k), place(2 * k, 0)) for k in range(1, chips)]

    def send_pair(l):
        mine = stack_all.at[l, core]
        return [send(mine, mine, pair_sems, (l,), (sibling, z))]

    block_moves = [send_blocks(0), send_blocks(1)]
    first_moves = [
        send(first_all.at[own_units], first_all.at[own_units], first_sems, (d,), place(0, d))
        for d in range(1, parts)
    ]
    valid_moves = [
        send(valid_all.at[s], valid_all.at[s], valid_sems, (k,), place(k, 0)) for k in range(1, seeds_axis)
    ]

    mask_four[...] = window_mask(LANES * r3, r3)
    mask_eight[...] = window_mask(LANES * r2, r2)
    mean_one[...] = jnp.zeros_like(mean_one)
    for copy in started[4:]:
        copy.wait()

    counts_a, degree_a = slot_counts(links_a_lead[...], 0, r3)
    counts_b, degree_b = slot_counts(links_b_lead[...], 0, r2)
    counts_c, degree_c = slot_counts(links_c[...], 0, r1)
    lead = [*counts_a, degree_a, *counts_b, degree_b, *counts_c, degree_c]
    lead += [labels_own[...].astype(f32), valid_own[...].astype(f32)]
    packed = jnp.zeros((32, LANES), f32)
    for k, line in enumerate(lead):
        packed = jnp.where(iota((32, LANES), 0) == k, line, packed)
    source, target = iota((LANES, LANES), 0), iota((LANES, LANES), 1)
    mine = jnp.where((source == target + z * q0) & (target < q0), 1.0, 0.0).astype(bf16)
    packed = dot(packed.astype(bf16), mine)
    take = [packed[k : k + 1] for k in range(len(lead))]
    counts_a, degree_a = take[:r3], jnp.maximum(take[r3], 1.0)
    take = take[r3 + 1 :]
    counts_b, degree_b = take[:r2], jnp.maximum(take[r2], 1.0)
    take = take[r2 + 1 :]
    counts_c, degree_c = take[:r1], jnp.maximum(take[r1], 1.0)
    label, present = take[r1 + 1], take[r1 + 2]
    own_rows[:, pl.ds(q2 + q1, LANES)] = dot(own_lead[...], mine).astype(bf16)

    counts, degree = slot_counts(links_a[:, pl.ds(0, q2)], z * q2, r3)
    for t in range(q2 // LANES):
        stripe_rows[t] = stripes([c[:, t * LANES : (t + 1) * LANES] for c in counts])
    degree_rows[:, pl.ds(0, q2)] = degree
    counts, degree = slot_counts(links_a[:, pl.ds(q2, q1)], z * q1, r3)
    for t in range(q1 // LANES):
        stripe_rows[q2 // LANES + t] = stripes([c[:, t * LANES : (t + 1) * LANES] for c in counts])
    degree_rows[:, pl.ds(q2, q1)] = degree
    stripe_rows[two // LANES - 1] = stripes(counts_a)
    degree_rows[:, pl.ds(q2 + q1, LANES)] = degree_a

    def mean_tiles(tile, tiles):
        for t in range(tiles):
            lanes = pl.ds(pl.multiple_of((tile + t) * LANES, LANES), LANES)
            kids = pl.ds(pl.multiple_of((tile + t) * LANES * r3, LANES), LANES * r3)
            matrix = spread(mask_four[...], stripe_rows[tile + t])
            mean = dot(child_rows[:, kids], matrix) / degree_rows[:, lanes]
            mean_one[0:width, lanes] = mean.astype(bf16)

    def layer_one(tile, tiles):
        lanes = pl.ds(pl.multiple_of(tile * LANES, LANES), LANES * tiles)
        preact = dot(first_all[:, 0:width], own_rows[:, lanes])
        preact += dot(first_all[:, LANES : 2 * LANES], mean_one[:, lanes])
        output, active, slope, scaling = activate(preact)
        hidden_one[:, lanes] = output
        active_one[:, lanes] = active
        slope_one[:, lanes] = slope
        scale_one[:, lanes] = scaling

    per = 4
    tail = q1 // LANES + 1
    lax.fori_loop(0, q2 // LANES // per, lambda i, c: (mean_tiles(i * per, per), c)[1], 0)
    mean_tiles(q2 // LANES, tail)

    counts, degree_t = slot_counts(links_b[...], z * q1, r2)
    for t in range(q1 // LANES):
        stripe = stripes([c[:, t * LANES : (t + 1) * LANES] for c in counts])
        spread_two[pl.ds(t * LANES * r2, LANES * r2), :] = spread(mask_eight[...], stripe)
    spread_lead = spread(mask_eight[0 : q0 * r2, :], stripes(counts_b))
    spread_three = spread(mask_eight[0 : q0 * r1, :], stripes(counts_c))

    chips_moves = []
    for l in range(2):
        arrive(block_moves[l])
        chips_moves.append(send_chips(l))
    arrive(first_moves)
    lax.fori_loop(0, q2 // LANES // per, lambda i, c: (layer_one(i * per, per), c)[1], 0)
    layer_one(q2 // LANES, tail)
    arrive(chips_moves[0])
    pair_moves = [send_pair(0)]

    joined_two[0:hid, :] = hidden_one[:, pl.ds(q2, q1 + LANES)]
    for t in range(q1 // LANES):
        rows = pl.ds(t * LANES * r2, LANES * r2)
        mean = dot(hidden_one[:, rows], spread_two[rows, :])
        lanes = slice(t * LANES, (t + 1) * LANES)
        joined_two[hid:, lanes] = (mean / degree_t[:, lanes]).astype(bf16)
    mean = dot(hidden_one[:, pl.ds(q2, q1)], spread_lead)
    joined_two[hid:, pl.ds(q1, LANES)] = (mean / degree_b).astype(bf16)

    low_half = iota((1, LANES), 1) < half

    def interleave(left, right):
        return jnp.where(low_half, left, shift_half(right)), jnp.where(low_half, shift_half(left), right)

    def gathered(l):
        for b in range(parts // 2):
            for c in range(2):
                left = stack_all[l, c, 2 * b].astype(f32).reshape(-1, LANES)
                right = stack_all[l, c, 2 * b + 1].astype(f32).reshape(-1, LANES)
                for h, value in enumerate(interleave(left, right)):
                    lanes = slice(b * LANES, (b + 1) * LANES)
                    low_stack[l, :, c, h, :, lanes] = value.astype(bf16).reshape(chips, short, LANES)
        return low_stack[l].reshape(2 * hid, hid)

    arrive(pair_moves[0])
    weight_two = gathered(0)
    preact = dot_tn(weight_two, joined_two[...])
    output, active_two, slope_two, scale_two = activate(preact)

    arrive(chips_moves[1])
    pair_moves += [send_pair(1)]

    joined_three[0:hid, :] = output[:, q1:]
    mean = dot(output[:, 0:q1], spread_three)
    joined_three[hid:, :] = (mean / degree_c).astype(bf16)
    arrive(pair_moves[1])
    weight_three = gathered(1)
    preact = dot_tn(weight_three, joined_three[...])
    seeds, active_three, slope_three, scale_three = activate(preact)

    head = dot(first_all[...], seat).astype(bf16)
    arrive(valid_moves)
    every_valid = jnp.sum(valid_all[...], axis=0)[0:1]
    count = jnp.sum(every_valid, axis=1, keepdims=True)
    logits = dot_tn(head, seeds)
    line = iota(logits.shape, 0)
    peak = jnp.max(logits, axis=0, keepdims=True)
    shifted = jnp.exp(logits - peak)
    totals = jnp.sum(shifted, axis=0, keepdims=True)
    hot = jnp.where(line.astype(f32) == label, 1.0, 0.0)
    nll = peak + jnp.log(totals) - jnp.sum(hot * logits, axis=0, keepdims=True)
    loss = jnp.sum(jnp.where(present > 0, nll, 0.0), axis=1, keepdims=True)
    share = present / jnp.maximum(count, 1.0)
    grad_logits = ((shifted / totals - hot) * share).astype(bf16)
    placed = dot(seat, grad_logits).astype(bf16)
    grad_one[...] = dot_nt(seeds, placed)
    grad_out = dot(head, grad_logits)
    free = 2 * LANES - 3
    part_a = loss.astype(bf16).astype(f32)
    part_b = (loss - part_a).astype(bf16).astype(f32)
    part_c = loss - part_a - part_b
    row, col = iota((hid, LANES), 0), iota((hid, LANES), 1) + LANES
    notes = jnp.where(col == free, part_a, jnp.where(col == free + 1, part_b, part_c))
    notes = jnp.where((col >= free) & (lax.rem(row, unit) == 0), notes, 0.0)
    grad_one[:, LANES:] += notes

    def keep_grad(l, value):
        value = value.astype(bf16).reshape(chips, 2, depth, hid)
        for c in range(2):
            core_send[l, c] = value[:, c]

    def send_core(l):
        return [send(core_send.at[l, 1 - core], core_recv.at[l], core_sems, (l,), (sibling, z))]

    def send_plane(l):
        plane_send[l] = (core_send[l, core].astype(f32) + core_recv[l].astype(f32)).astype(bf16)
        return [
            send(plane_send.at[l, lax.rem(chip + k, chips)], plane_recv.at[l, k], plane_sems, (l, k), place(2 * k, 0))
            for k in range(1, chips)
        ]

    def send_turn(l):
        total = plane_send[l, chip].astype(f32)
        for k in range(1, chips):
            total += plane_recv[l, k].astype(f32)
        for b in range(parts // 2):
            lanes = slice(b * LANES, (b + 1) * LANES)
            for h, value in enumerate(interleave(total[0:short, lanes], total[short:, lanes])):
                turn_send[l, 2 * b + h] = value.astype(bf16)
        return [
            send(turn_send.at[l, lax.rem(z + d, parts)], turn_recv.at[l, d], turn_sems, (l, d), place(0, d))
            for d in range(1, parts)
        ]

    def finish_stack(l):
        total = turn_send[l, z].astype(f32)
        for d in range(1, parts):
            total += turn_recv[l, d].astype(f32)
        stack_out[l] = total

    grad_pre = activate_back(grad_out, active_three, slope_three, scale_three)
    keep_grad(1, dot_nt(joined_three[...], grad_pre))
    grad_joined = dot(weight_three, grad_pre)
    grad_mean = (grad_joined[hid:] / degree_c).astype(bf16)
    grad_out = jnp.concatenate([dot_nt(grad_mean, spread_three), grad_joined[0:hid]], axis=1)
    core_moves = [None, send_core(1)]

    grad_pre = activate_back(grad_out, active_two, slope_two, scale_two)
    keep_grad(0, dot_nt(joined_two[...], grad_pre))
    grad_joined = dot(weight_two, grad_pre)
    grad_mean = (grad_joined[hid:, 0:q1] / degree_t).astype(bf16)
    lead_mean = (grad_joined[hid:, q1:] / degree_b).astype(bf16)
    core_moves[0] = send_core(0)

    def back_one(tile, grad_out):
        lanes = pl.ds(tile, grad_out.shape[1])
        pre_one[:, lanes] = activate_back(
            grad_out, active_one[:, lanes], slope_one[:, lanes], scale_one[:, lanes]
        )

    def back_piece(i):
        tile = i * per * LANES
        group = tile // (LANES * r2) * LANES
        back_one(tile, dot_nt(grad_mean[:, group : group + LANES], spread_two[pl.ds(tile, per * LANES), :]))

    own = grad_joined[0:hid]
    back_one(q2, own[:, 0:q1] + dot_nt(lead_mean, spread_lead))
    back_one(q2 + q1, own[:, q1:])
    plane_moves, turn_moves = [None, None], [None, None]
    pieces = q2 // LANES // per
    for i in range(pieces // 2):
        back_piece(i)
    arrive(core_moves[1])
    plane_moves[1] = send_plane(1)
    for i in range(pieces // 2, pieces):
        back_piece(i)
    grad_one[:, 0:width] += dot_nt(pre_one[...], own_rows[...])
    grad_one[:, LANES : LANES + width] += dot_nt(pre_one[...], mean_one[0:width, :])
    first_send[...] = grad_one[...].astype(bf16)

    group = 2 * unit // 16

    def piece(owner, part):
        slot = lax.rem(owner, group)
        rows = pl.ds(pl.multiple_of(part * unit + slot // 2 * 16, 16), 16)
        return rows, pl.ds(pl.multiple_of(lax.rem(slot, 2) * LANES, LANES), LANES)

    piece_moves = []
    for i, (k, d) in reversed(list(enumerate(everyone))):
        owner, part = place(k, d)
        rows, lanes = piece(owner, part)
        piece_moves.append(
            send(first_send.at[rows, lanes], first_recv.at[i], piece_sems, (i,), (owner, part))
        )

    arrive(core_moves[0])
    plane_moves[0] = send_plane(0)
    for l in (1, 0):
        arrive(plane_moves[l])
        turn_moves[l] = send_turn(l)

    arrive(piece_moves)
    rows, lanes = piece(s, z)
    total = first_send[rows, lanes].astype(f32)
    for i in range(len(everyone)):
        total += first_recv[i].astype(f32)
    rows, lanes = piece(s, 0)
    first_piece[rows, lanes] = total
    held = first_piece.at[rows, lanes]
    base = s // group * group
    share_moves = []
    for k in range(1, group):
        friend = base + lax.rem(s + k, group)
        share_moves.append(send(held, held, share_sems, (k,), (friend, z)))
    for l in (1, 0):
        arrive(turn_moves[l])
        finish_stack(l)
    arrive(share_moves)
    spare = (iota((unit, LANES), 0) == 0) & (iota((unit, LANES), 1) == LANES - 4)
    first_out[:, 0 : hid - LANES] = first_piece[:, 0 : hid - LANES]
    first_out[:, hid - LANES :] = jnp.where(spare, count, first_piece[:, hid - LANES :])

    for copy in moves:
        copy.wait_send()


def step(sizes, *operands):
    n3, n2, n1, n0, parts, seeds_axis, width, classes = sizes
    q2, q1 = n2 // parts, n1 // parts
    r3, r2 = n3 // n2, n2 // n1
    two = q2 + q1 + LANES
    hid = 256
    unit = hid // parts
    chips = seeds_axis // 2
    rows = 2 * hid // seeds_axis
    slots, slots_b = operands[1].shape[0], operands[2].shape[0]
    everyone = seeds_axis * parts - 1
    short = rows // 2
    group = 2 * unit // 16
    hbm, vmem = pl.BlockSpec(memory_space=pl.ANY), pl.BlockSpec(memory_space=pltpu.VMEM)
    shape = jax.ShapeDtypeStruct
    dma = pltpu.SemaphoreType.DMA
    return pl.pallas_call(
        functools.partial(step_kernel, sizes),
        out_shape=(shape((unit, hid), f32), shape((2, short, LANES), f32)),
        in_specs=[hbm] * 9,
        out_specs=(vmem,) * 2,
        scratch_shapes=[
            pltpu.VMEM((width, two), bf16),
            pltpu.VMEM((width, two * r3), bf16),
            pltpu.VMEM((width, LANES), bf16),
            pltpu.VMEM((slots, q2 + q1), i32),
            pltpu.VMEM((slots_b, q1), i32),
            pltpu.VMEM((slots, LANES), i32),
            pltpu.VMEM((slots_b, LANES), i32),
            pltpu.VMEM((LANES, two), bf16),
            pltpu.VMEM((hid, two), bf16),
            pltpu.VMEM((hid, two), f32),
            pltpu.VMEM((hid, two), f32),
            pltpu.VMEM((1, two), f32),
            pltpu.VMEM((1, two), f32),
            pltpu.VMEM((two // LANES, 8, LANES), f32),
            pltpu.VMEM((2 * hid, q1 + LANES), bf16),
            pltpu.VMEM((2 * hid, LANES), bf16),
            pltpu.VMEM((q2, LANES), bf16),
            pltpu.VMEM((LANES * r3, LANES), f32),
            pltpu.VMEM((LANES * r2, LANES), f32),
            pltpu.VMEM((hid, two), bf16),
            pltpu.VMEM((hid, hid), bf16),
            pltpu.VMEM((2, 2, parts, chips, short, LANES), bf16),
            pltpu.VMEM((seeds_axis, 8, LANES), f32),
            pltpu.VMEM((2, chips, 2, 2, short, hid), bf16),
            pltpu.VMEM((2, 2, chips, rows, hid), bf16),
            pltpu.VMEM((2, chips, rows, hid), bf16),
            pltpu.VMEM((2, chips, rows, hid), bf16),
            pltpu.VMEM((2, chips, rows, hid), bf16),
            pltpu.VMEM((2, parts, short, LANES), bf16),
            pltpu.VMEM((2, parts, short, LANES), bf16),
            pltpu.VMEM((hid, hid), f32),
            pltpu.VMEM((hid, hid), bf16),
            pltpu.VMEM((everyone, 16, LANES), bf16),
            pltpu.VMEM((unit, hid), f32),
            *[pltpu.VMEM(v.shape, f32) for v in operands[6:]],
            *[pltpu.VMEM(v.shape, i32) for v in operands[3:6]],
            dma((17,)),
            dma((2, parts)),
            dma((2, 2, parts)),
            dma((2, 2, chips)),
            dma((2, 2)),
            dma((2, seeds_axis)),
            dma((2, 2)),
            dma((2, 2, chips)),
            dma((2, 2, parts)),
            dma((2, everyone)),
            dma((2, group)),
        ],
        compiler_params=pltpu.CompilerParams(
            vmem_limit_bytes=56 * 2**20, collective_id=0, has_side_effects=True
        ),
    )(*operands)


def adamw(weight, moment, square, grad):
    new_moment = beta_first * moment + (1.0 - beta_first) * grad
    new_square = beta_second * square + (1.0 - beta_second) * grad * grad
    moment_hat = new_moment / (1.0 - beta_first**STEP)
    square_hat = new_square / (1.0 - beta_second**STEP)
    new_weight = weight - learn_rate * (
        moment_hat / (jnp.sqrt(square_hat) + epsilon_adam) + decay_rate * weight
    )
    return (new_moment, new_square, new_weight)


def update_kernel(
    width, classes,
    grad_first, grad_stack,
    w_a, m_a, s_a, w_b, m_b, s_b, w_c, m_c, s_c,
    loss_out, count_out, om_a, os_a, ow_a, om_b, os_b, ow_b, om_c, os_c, ow_c,
):
    def put(refs, where, values):
        for ref, value in zip(refs, values):
            ref[where] = value

    half = LANES // 2
    short = grad_stack.shape[1]
    for l in range(2):
        for h in range(2):
            grad = grad_stack[l, :, h * half : (h + 1) * half]
            rows = (l, slice(h * short, (h + 1) * short))
            put((om_b, os_b, ow_b), rows, adamw(w_b[rows], m_b[rows], s_b[rows], grad))
    for part in range(2):
        grad = grad_first[:, part * LANES : part * LANES + width]
        lanes = (slice(None), slice(part * width, (part + 1) * width))
        put((om_a, os_a, ow_a), lanes, adamw(w_a[lanes], m_a[lanes], s_a[lanes], grad))
    gap = LANES - width
    flipped = grad_first[...].T
    for start, stop, place in ((0, gap, width), (gap, classes, LANES + width)):
        rows = (slice(start, stop), slice(None))
        grad = flipped[place : place + stop - start]
        put((om_c, os_c, ow_c), rows, adamw(w_c[rows], m_c[rows], s_c[rows], grad))
    free = grad_first.shape[1] - 3
    loss_out[...] = jnp.sum(grad_first[0:1, free:], axis=1, keepdims=True)
    count_out[...] = grad_first[0:1, free - 1 : free]


def update(width, classes, *operands):
    vmem = pl.BlockSpec(memory_space=pltpu.VMEM)
    shape = jax.ShapeDtypeStruct
    outs = [shape((1, 1), f32)] * 2 + [shape(v.shape, f32) for v in operands[2:]]
    return pl.pallas_call(
        functools.partial(update_kernel, width, classes),
        out_shape=tuple(outs),
        in_specs=[vmem] * len(operands),
        out_specs=(vmem,) * len(outs),
    )(*operands)


def per_device(
    features,
    links_first,
    links_second,
    links_third,
    labels,
    valid,
    weight_first,
    moment_first,
    square_first,
    weight_stack,
    moment_stack,
    square_stack,
    weight_head,
    moment_head,
    square_head,
):
    width, classes = features.shape[1], weight_head.shape[1]
    sizes = (
        features.shape[0], links_first.shape[0], links_second.shape[0], links_third.shape[0],
        lax.axis_size("hid"), lax.axis_size("seed"), width, classes,
    )
    grad_first, grad_stack = step(
        sizes,
        features.T, links_first.T, links_second.T, links_third.T,
        labels.reshape(1, -1), valid.reshape(1, -1), weight_first.T, weight_stack, weight_head.T,
    )
    loss_sum, count, m_a, s_a, w_a, m_b, s_b, w_b, m_c, s_c, w_c = update(
        width, classes, grad_first, grad_stack,
        weight_first.T, moment_first.T, square_first.T,
        weight_stack, moment_stack, square_stack,
        weight_head.T, moment_head.T, square_head.T,
    )
    return (
        loss_sum.reshape(()), count.reshape(()),
        m_a.T, s_a.T, w_a.T,
        m_b, s_b, w_b,
        m_c.T, s_c.T, w_c.T,
    )


def solution(mesh):
    placed = (
        P("seed", None),
        P("seed", None),
        P("seed", None),
        P("seed", None),
        P("seed"),
        P("seed"),
        P(None, "hid"),
        P(None, "hid"),
        P(None, "hid"),
        P(None, "seed", "hid"),
        P(None, "seed", "hid"),
        P(None, "seed", "hid"),
        P("hid", None),
        P("hid", None),
        P("hid", None),
    )
    return jax.shard_map(
        per_device,
        mesh=mesh,
        in_specs=placed,
        out_specs=(P(), P()) + placed[6:],
        check_vma=False,
    )
```

```python
import functools

import jax
import jax.numpy as jnp
from jax import lax
from jax.experimental import pallas as pl
from jax.experimental.pallas import tpu as pltpu
from jax.sharding import PartitionSpec as P

STEP = 5
LANES = 128


epsilon_norm = 1e-06
epsilon_adam = 1e-08
learn_rate = 0.6
decay_rate = 0.01
beta_first = 0.5
beta_second = 0.5

f32, bf16, i32 = jnp.float32, jnp.bfloat16, jnp.int32
MESH = pl.DeviceIdType.MESH
NT = (((1,), (1,)), ((), ()))
TN = (((0,), (0,)), ((), ()))


def dot(a, b):
    return jnp.dot(a, b, preferred_element_type=f32)


def dot_nt(a, b):
    return lax.dot_general(a, b, NT, preferred_element_type=f32)


def dot_tn(a, b):
    return lax.dot_general(a, b, TN, preferred_element_type=f32)


def iota(shape, axis):
    return lax.broadcasted_iota(i32, shape, axis)


def slot_counts(links, first_row, ratio):
    lanes = links.shape[1]
    base = (first_row + iota((1, lanes), 1)) * ratio
    offsets = links - base
    counts = [
        jnp.sum(jnp.where(offsets == r, 1.0, 0.0), axis=0, keepdims=True) for r in range(ratio)
    ]
    degree = jnp.maximum(
        jnp.sum(jnp.where(links >= 0, 1.0, 0.0), axis=0, keepdims=True), 1.0
    )
    return counts, degree


def stripes(counts):
    ratio, lanes = len(counts), counts[0].shape[1]
    which = iota((8, lanes), 0) % ratio
    out = jnp.zeros((8, lanes), f32)
    for r in range(ratio):
        out = jnp.where(which == r, counts[r], out)
    return out


def spread(mask, stripe):
    rows = mask.shape[0]
    values = mask.reshape(rows // 8, 8, LANES) * stripe[None]
    return values.reshape(rows, LANES).astype(bf16)


def window_mask(rows, ratio):
    return jnp.where(iota((rows, LANES), 0) // ratio == iota((rows, LANES), 1), 1.0, 0.0)


def activate(preact):
    logistic = 0.5 * jnp.tanh(0.5 * preact) + 0.5
    active = preact * logistic
    slope = logistic + (active - active * logistic)
    scaling = lax.rsqrt(jnp.sum(active * active, axis=0, keepdims=True) + epsilon_norm)
    return (active * scaling).astype(bf16), active, slope, scaling


def activate_back(grad_out, active, slope, scaling):
    inner = jnp.sum(active * grad_out, axis=0, keepdims=True)
    grad_active = scaling * grad_out - active * (scaling * scaling * scaling * inner)
    return (grad_active * slope).astype(bf16)


def placement_rows(classes, columns, width):
    gap = LANES - width
    row, col = iota((classes, columns), 0), iota((classes, columns), 1)
    target = jnp.where(row < gap, width + row, LANES + width + row - gap)
    return jnp.where(col == target, 1.0, 0.0).astype(bf16)


def placement(rows, classes, width):
    gap = LANES - width
    row, col = iota((rows, classes), 0), iota((rows, classes), 1)
    target = jnp.where(col < gap, width + col, LANES + width + col - gap)
    return jnp.where(row == target, 1.0, 0.0).astype(bf16)


def shift_half(x):
    return pltpu.roll(x, LANES // 2, 1)


def step_kernel(
    sizes,
    features, links_first, links_second, links_third, labels, valid, weight_first, weight_stack, weight_head,
    first_out, stack_out, count_out,
    own_rows, child_rows, own_lead, links_a, links_b, links_a_lead, links_b_lead,
    joined_one, hidden_one, active_one, slope_one, scale_one, degree_rows, stripe_rows,
    joined_two, joined_three, spread_two, mask_four, mask_eight,
    first_all, stack_all, valid_all, low_stack,
    core_send, core_recv, plane_send, plane_recv, turn_send,
    grad_one, first_send, half_recv, half_send, part_recv, share, count_own, first_own, stack_own, head_own,
    links_c, labels_own, valid_own,
    local_sems, first_sems, block_sems, own_sems, chips_sems, pair_sems, valid_sems,
    core_sems, plane_sems, turn_sems, half_sems, part_sems, share_sems, out_sems,
):
    n3, n2, n1, n0, parts, seeds_axis, width, classes = sizes
    q2, q1, q0 = n2 // parts, n1 // parts, n0 // parts
    r3, r2, r1 = n3 // n2, n2 // n1, n1 // n0
    s, z = lax.axis_index("seed"), lax.axis_index("hid")
    core, chip = lax.rem(s, 2), s // 2
    chips = seeds_axis // 2
    sibling = s + 1 - 2 * core
    two = q2 + q1 + LANES
    hid = 256
    unit = hid // parts
    own_units = pl.ds(pl.multiple_of(z * unit, unit), unit)
    near = [(0, d) for d in range(1, parts)] + [(k, 0) for k in range(1, seeds_axis)]

    def place(k, d):
        return (lax.rem(s + k, seeds_axis), lax.rem(z + d, parts))

    barrier = pltpu.get_barrier_semaphore()
    for k, d in near:
        pl.semaphore_signal(barrier, inc=1, device_id=place(k, d), device_id_type=MESH)

    def at(size):
        return pl.ds(pl.multiple_of(z * size, LANES), size)

    copies = [
        (weight_stack, stack_own),
        (weight_first, first_own),
        (weight_head, head_own),
        (valid, valid_own),
        (labels, labels_own),
        (links_third, links_c),
        (links_first.at[:, at(q2)], links_a.at[:, pl.ds(0, q2)]),
        (links_first.at[:, at(q1)], links_a.at[:, pl.ds(q2, q1)]),
        (links_first.at[:, pl.ds(0, LANES)], links_a_lead),
        (links_second.at[:, at(q1)], links_b),
        (links_second.at[:, pl.ds(0, LANES)], links_b_lead),
        (features.at[:, pl.ds(0, LANES)], own_lead),
        (features.at[:, at(q2)], own_rows.at[:, pl.ds(0, q2)]),
        (features.at[:, at(q1)], own_rows.at[:, pl.ds(q2, q1)]),
        (features.at[:, at(q2 * r3)], child_rows.at[:, pl.ds(0, q2 * r3)]),
        (features.at[:, at(q1 * r3)], child_rows.at[:, pl.ds(q2 * r3, q1 * r3)]),
        (
            features.at[:, pl.ds(pl.multiple_of(z * q0 * r3, LANES), LANES * r3)],
            child_rows.at[:, pl.ds((q2 + q1) * r3, LANES * r3)],
        ),
    ]
    started = [pltpu.make_async_copy(src, dst, local_sems.at[i]) for i, (src, dst) in enumerate(copies)]
    for copy in started:
        copy.start()

    started[0].wait()
    depth = stack_own.shape[1]
    short = depth // 2
    row, col = iota((unit, LANES), 0), iota((unit, LANES), 1)
    to_left = jnp.where(row == col, 1.0, 0.0).astype(bf16)
    to_right = jnp.where(row + unit == col, 1.0, 0.0).astype(bf16)
    for l in range(2):
        block = dot(stack_own[l, 0:short].astype(bf16), to_left)
        block += dot(stack_own[l, short:].astype(bf16), to_right)
        stack_all[l, core, 0, chip] = block.astype(bf16)
    pl.semaphore_wait(barrier, len(near))

    moves = []

    def send(src, dst, sems, where, device):
        copy = pltpu.make_async_remote_copy(
            src_ref=src, dst_ref=dst, send_sem=sems.at[(0, *where)], recv_sem=sems.at[(1, *where)],
            device_id=device, device_id_type=MESH,
        )
        copy.start()
        moves.append(copy)
        return copy

    def arrive(copies):
        for copy in copies:
            copy.wait_recv()

    def send_blocks(l):
        mine = stack_all.at[l, core, 0, chip]
        return [
            send(mine, stack_all.at[l, core, d, chip], block_sems, (l, d), place(0, d)) for d in range(1, parts)
        ]

    def send_own(l):
        mine = stack_all.at[l, core, 0, chip]
        return [send(mine, mine, own_sems, (l, k), place(2 * k, 0)) for k in range(1, chips)]

    def send_chips(l):
        mine = stack_all.at[l, core, 1:parts, chip]
        return [send(mine, mine, chips_sems, (l, k), place(2 * k, 0)) for k in range(1, chips)]

    def send_pair(l):
        mine = stack_all.at[l, core]
        return [send(mine, mine, pair_sems, (l,), (sibling, z))]

    block_moves = [send_blocks(0), send_blocks(1)]
    own_moves = [send_own(0), send_own(1)]
    for copy in started[1:4]:
        copy.wait()
    row, col = iota((2 * width, hid), 0), iota((2 * width, hid), 1)
    columns = jnp.where(row < width, row, row - width + LANES)
    lift = jnp.where(columns == col, 1.0, 0.0).astype(bf16)
    seat = placement(hid, classes, width)
    shard = dot(first_own[...].astype(bf16), lift)
    shard += dot_tn(head_own[...].astype(bf16), placement_rows(classes, hid, width))
    first_all[own_units, :] = shard.astype(bf16)
    valid_all[s] = jnp.broadcast_to(valid_own[...].astype(f32), valid_all.shape[1:])

    first_moves = [
        send(first_all.at[own_units], first_all.at[own_units], first_sems, (d,), place(0, d))
        for d in range(1, parts)
    ]
    valid_moves = [
        send(valid_all.at[s], valid_all.at[s], valid_sems, (k,), place(k, 0)) for k in range(1, seeds_axis)
    ]

    mask_four[...] = window_mask(LANES * r3, r3)
    mask_eight[...] = window_mask(LANES * r2, r2)
    for part in range(2):
        joined_one[pl.ds((part + 1) * LANES - 32, 32), :] = jnp.zeros((32, two), bf16)
    for copy in started[4:]:
        copy.wait()

    counts_a, degree_a = slot_counts(links_a_lead[...], 0, r3)
    counts_b, degree_b = slot_counts(links_b_lead[...], 0, r2)
    counts_c, degree_c = slot_counts(links_c[...], 0, r1)
    lead = [*counts_a, degree_a, *counts_b, degree_b, *counts_c, degree_c]
    lead += [labels_own[...].astype(f32), valid_own[...].astype(f32)]
    packed = jnp.zeros((32, LANES), f32)
    for k, line in enumerate(lead):
        packed = jnp.where(iota((32, LANES), 0) == k, line, packed)
    source, target = iota((LANES, LANES), 0), iota((LANES, LANES), 1)
    mine = jnp.where((source == target + z * q0) & (target < q0), 1.0, 0.0).astype(bf16)
    packed = dot(packed.astype(bf16), mine)
    take = [packed[k : k + 1] for k in range(len(lead))]
    counts_a, degree_a = take[:r3], jnp.maximum(take[r3], 1.0)
    take = take[r3 + 1 :]
    counts_b, degree_b = take[:r2], jnp.maximum(take[r2], 1.0)
    take = take[r2 + 1 :]
    counts_c, degree_c = take[:r1], jnp.maximum(take[r1], 1.0)
    label, present = take[r1 + 1], take[r1 + 2]
    own_rows[:, pl.ds(q2 + q1, LANES)] = dot(own_lead[...], mine).astype(bf16)

    counts, degree = slot_counts(links_a[:, pl.ds(0, q2)], z * q2, r3)
    for t in range(q2 // LANES):
        stripe_rows[t] = stripes([c[:, t * LANES : (t + 1) * LANES] for c in counts])
    degree_rows[:, pl.ds(0, q2)] = degree
    counts, degree = slot_counts(links_a[:, pl.ds(q2, q1)], z * q1, r3)
    for t in range(q1 // LANES):
        stripe_rows[q2 // LANES + t] = stripes([c[:, t * LANES : (t + 1) * LANES] for c in counts])
    degree_rows[:, pl.ds(q2, q1)] = degree
    stripe_rows[two // LANES - 1] = stripes(counts_a)
    degree_rows[:, pl.ds(q2 + q1, LANES)] = degree_a

    def mean_tiles(tile, tiles):
        for t in range(tiles):
            lanes = pl.ds(pl.multiple_of((tile + t) * LANES, LANES), LANES)
            kids = pl.ds(pl.multiple_of((tile + t) * LANES * r3, LANES), LANES * r3)
            matrix = spread(mask_four[...], stripe_rows[tile + t])
            mean = dot(child_rows[:, kids], matrix) / degree_rows[:, lanes]
            joined_one[LANES : LANES + width, lanes] = mean.astype(bf16)
            joined_one[0:width, lanes] = own_rows[:, lanes]

    def layer_one(tile, tiles):
        lanes = pl.ds(pl.multiple_of(tile * LANES, LANES), LANES * tiles)
        preact = dot(first_all[...], joined_one[:, lanes])
        output, active, slope, scaling = activate(preact)
        hidden_one[:, lanes] = output
        active_one[:, lanes] = active
        slope_one[:, lanes] = slope
        scale_one[:, lanes] = scaling

    per = 4
    tail = q1 // LANES + 1
    lax.fori_loop(0, q2 // LANES // per, lambda i, c: (mean_tiles(i * per, per), c)[1], 0)
    mean_tiles(q2 // LANES, tail)

    counts, degree_t = slot_counts(links_b[...], z * q1, r2)
    for t in range(q1 // LANES):
        stripe = stripes([c[:, t * LANES : (t + 1) * LANES] for c in counts])
        spread_two[pl.ds(t * LANES * r2, LANES * r2), :] = spread(mask_eight[...], stripe)
    spread_lead = spread(mask_eight[0 : q0 * r2, :], stripes(counts_b))
    spread_three = spread(mask_eight[0 : q0 * r1, :], stripes(counts_c))

    chips_moves = []
    for l in range(2):
        arrive(block_moves[l])
        chips_moves.append(send_chips(l))
    arrive(first_moves)
    turns = q2 // LANES // per
    pair_moves = []
    for l in range(2):
        lax.fori_loop(l * turns // 2, (l + 1) * turns // 2, lambda i, c: (layer_one(i * per, per), c)[1], 0)
        arrive(own_moves[l] + chips_moves[l])
        pair_moves.append(send_pair(l))
    arrive(valid_moves)
    layer_one(q2 // LANES, tail)

    joined_two[0:hid, :] = hidden_one[:, pl.ds(q2, q1 + LANES)]
    for t in range(q1 // LANES):
        rows = pl.ds(t * LANES * r2, LANES * r2)
        mean = dot(hidden_one[:, rows], spread_two[rows, :])
        lanes = slice(t * LANES, (t + 1) * LANES)
        joined_two[hid:, lanes] = (mean / degree_t[:, lanes]).astype(bf16)
    mean = dot(hidden_one[:, pl.ds(q2, q1)], spread_lead)
    joined_two[hid:, pl.ds(q1, LANES)] = (mean / degree_b).astype(bf16)

    low_half = iota((1, LANES), 1) < unit

    def interleave(left, right):
        return jnp.where(low_half, left, shift_half(right)), jnp.where(low_half, shift_half(left), right)

    def gathered(l):
        for b in range(parts // 2):
            for c in range(2):
                left = stack_all[l, c, lax.rem(z - 2 * b + parts, parts)].astype(f32).reshape(-1, LANES)
                right = stack_all[l, c, lax.rem(z - 2 * b - 1 + parts, parts)].astype(f32).reshape(-1, LANES)
                for h, value in enumerate(interleave(left, right)):
                    lanes = slice(b * LANES, (b + 1) * LANES)
                    low_stack[l, :, c, h, :, lanes] = value.astype(bf16).reshape(chips, short, LANES)
        return low_stack[l].reshape(2 * hid, hid)

    arrive(pair_moves[0])
    weight_two = gathered(0)
    preact = dot_tn(weight_two, joined_two[...])
    output, active_two, slope_two, scale_two = activate(preact)

    joined_three[0:hid, :] = output[:, q1:]
    mean = dot(output[:, 0:q1], spread_three)
    joined_three[hid:, :] = (mean / degree_c).astype(bf16)
    arrive(pair_moves[1])
    weight_three = gathered(1)
    preact = dot_tn(weight_three, joined_three[...])
    seeds, active_three, slope_three, scale_three = activate(preact)

    head = dot(first_all[...], seat).astype(bf16)
    every_valid = jnp.sum(valid_all[...], axis=0)[0:1]
    count = jnp.sum(every_valid, axis=1, keepdims=True)
    logits = dot_tn(head, seeds)
    line = iota(logits.shape, 0)
    peak = jnp.max(logits, axis=0, keepdims=True)
    shifted = jnp.exp(logits - peak)
    totals = jnp.sum(shifted, axis=0, keepdims=True)
    hot = jnp.where(line.astype(f32) == label, 1.0, 0.0)
    nll = peak + jnp.log(totals) - jnp.sum(hot * logits, axis=0, keepdims=True)
    loss = jnp.sum(jnp.where(present > 0, nll, 0.0), axis=1, keepdims=True)
    count_own[...] = jnp.broadcast_to(count, count_own.shape)
    out_moves = [pltpu.make_async_copy(count_own, count_out, out_sems.at[0])]
    out_moves[0].start()
    weight = present / jnp.maximum(count, 1.0)
    grad_logits = ((shifted / totals - hot) * weight).astype(bf16)
    placed = dot(seat, grad_logits).astype(bf16)
    grad_one[...] = dot_nt(seeds, placed)
    grad_out = dot(head, grad_logits)
    free = 2 * LANES - 3
    part_a = loss.astype(bf16).astype(f32)
    part_b = (loss - part_a).astype(bf16).astype(f32)
    part_c = loss - part_a - part_b
    row, col = iota((hid, LANES), 0), iota((hid, LANES), 1) + LANES
    notes = jnp.where(col == free, part_a, jnp.where(col == free + 1, part_b, part_c))
    notes = jnp.where((col >= free) & (lax.rem(row, unit) == 2 * z + core), notes, 0.0)
    grad_one[:, LANES:] += notes

    def keep_grad(l, value):
        value = value.astype(bf16).reshape(chips, 2, depth, hid)
        for c in range(2):
            core_send[l, c] = value[:, c]

    def send_core(l):
        return [send(core_send.at[l, 1 - core], core_recv.at[l], core_sems, (l,), (sibling, z))]

    def send_plane(l):
        plane_send[l] = (core_send[l, core].astype(f32) + core_recv[l].astype(f32)).astype(bf16)
        return [
            send(plane_send.at[l, lax.rem(chip + k, chips)], plane_recv.at[l, k], plane_sems, (l, k), place(2 * k, 0))
            for k in range(1, chips)
        ]

    def send_turn(l):
        total = plane_send[l, chip].astype(f32)
        for k in range(1, chips):
            total += plane_recv[l, k].astype(f32)
        for b in range(parts // 2):
            lanes = slice(b * LANES, (b + 1) * LANES)
            for h, value in enumerate(interleave(total[0:short, lanes], total[short:, lanes])):
                turn_send[l, 2 * b + h] = value.astype(bf16)
        out_moves.append(pltpu.make_async_copy(turn_send.at[l, z], stack_out.at[l, 0], out_sems.at[1 + l]))
        out_moves[-1].start()
        return [
            send(turn_send.at[l, lax.rem(z + d, parts)], stack_out.at[l, d], turn_sems, (l, d), place(0, d))
            for d in range(1, parts)
        ]

    grad_pre = activate_back(grad_out, active_three, slope_three, scale_three)
    keep_grad(1, dot_nt(joined_three[...], grad_pre))
    core_moves = [None, send_core(1)]
    grad_joined = dot(weight_three, grad_pre)
    grad_mean = (grad_joined[hid:] / degree_c).astype(bf16)
    grad_out = jnp.concatenate([dot_nt(grad_mean, spread_three), grad_joined[0:hid]], axis=1)

    grad_pre = activate_back(grad_out, active_two, slope_two, scale_two)
    keep_grad(0, dot_nt(joined_two[...], grad_pre))
    grad_joined = dot(weight_two, grad_pre)
    grad_mean = (grad_joined[hid:, 0:q1] / degree_t).astype(bf16)
    lead_mean = (grad_joined[hid:, q1:] / degree_b).astype(bf16)
    core_moves[0] = send_core(0)

    def back_one(tile, grad_out):
        lanes = pl.ds(tile, grad_out.shape[1])
        grad_pre = activate_back(grad_out, active_one[:, lanes], slope_one[:, lanes], scale_one[:, lanes])
        return dot_nt(grad_pre, joined_one[:, lanes])

    own = grad_joined[0:hid]
    total = back_one(q2 + q1, own[:, q1:])
    total += back_one(q2, own[:, 0:q1] + dot_nt(lead_mean, spread_lead))
    plane_moves, turn_moves = [None, None], [None, None]
    for i in range(turns):
        if i == turns // 2:
            arrive(core_moves[1])
            plane_moves[1] = send_plane(1)
        tile = i * per * LANES
        group = tile // (LANES * r2) * LANES
        total += back_one(tile, dot_nt(grad_mean[:, group : group + LANES], spread_two[pl.ds(tile, per * LANES), :]))
    first_send[...] = (grad_one[...] + total).astype(bf16)

    def half(c):
        return pl.ds(pl.multiple_of(c * LANES, LANES), LANES)

    def part(d):
        return pl.ds(pl.multiple_of(lax.rem(z + d, parts) * unit, unit), unit)

    half_moves = [send(first_send.at[:, half(1 - core)], half_recv, half_sems, (0,), (sibling, z))]
    arrive(core_moves[0])
    plane_moves[0] = send_plane(0)

    arrive(half_moves)
    half_send[...] = (first_send[:, half(core)].astype(f32) + half_recv[...].astype(f32)).astype(bf16)
    part_moves = [
        send(half_send.at[part(d)], part_recv.at[d], part_sems, (d,), place(0, d)) for d in range(1, parts)
    ]
    arrive(plane_moves[1])
    turn_moves[1] = send_turn(1)
    arrive(part_moves)
    total = half_send[part(0), :].astype(f32)
    for d in range(1, parts):
        total += part_recv[d].astype(f32)
    share[...] = total.astype(bf16)
    held = first_out.at[chip, :, half(core)]
    out_moves.append(pltpu.make_async_copy(share, held, out_sems.at[3]))
    out_moves[-1].start()
    share_moves = [send(share, held, share_sems, (k,), place(k, 0)) for k in range(1, seeds_axis)]
    arrive(plane_moves[0])
    turn_moves[0] = send_turn(0)

    for copies in turn_moves:
        arrive(copies)
    arrive(share_moves)
    for copy in out_moves:
        copy.wait()
    for copy in moves:
        copy.wait_send()


def step(sizes, *operands):
    n3, n2, n1, n0, parts, seeds_axis, width, classes = sizes
    q2, q1 = n2 // parts, n1 // parts
    r3, r2 = n3 // n2, n2 // n1
    two = q2 + q1 + LANES
    hid = 256
    unit = hid // parts
    chips = seeds_axis // 2
    rows = 2 * hid // seeds_axis
    slots, slots_b = operands[1].shape[0], operands[2].shape[0]
    short = rows // 2
    hbm = pl.BlockSpec(memory_space=pl.ANY)
    shape = jax.ShapeDtypeStruct
    dma = pltpu.SemaphoreType.DMA
    return pl.pallas_call(
        functools.partial(step_kernel, sizes),
        out_shape=(shape((chips, unit, hid), bf16), shape((2, parts, short, LANES), bf16), shape((8, LANES), f32)),
        in_specs=[hbm] * 9,
        out_specs=(hbm,) * 3,
        scratch_shapes=[
            pltpu.VMEM((width, two), bf16),
            pltpu.VMEM((width, two * r3), bf16),
            pltpu.VMEM((width, LANES), bf16),
            pltpu.VMEM((slots, q2 + q1), i32),
            pltpu.VMEM((slots_b, q1), i32),
            pltpu.VMEM((slots, LANES), i32),
            pltpu.VMEM((slots_b, LANES), i32),
            pltpu.VMEM((2 * LANES, two), bf16),
            pltpu.VMEM((hid, two), bf16),
            pltpu.VMEM((hid, two), f32),
            pltpu.VMEM((hid, two), f32),
            pltpu.VMEM((1, two), f32),
            pltpu.VMEM((1, two), f32),
            pltpu.VMEM((two // LANES, 8, LANES), f32),
            pltpu.VMEM((2 * hid, q1 + LANES), bf16),
            pltpu.VMEM((2 * hid, LANES), bf16),
            pltpu.VMEM((q2, LANES), bf16),
            pltpu.VMEM((LANES * r3, LANES), f32),
            pltpu.VMEM((LANES * r2, LANES), f32),
            pltpu.VMEM((hid, hid), bf16),
            pltpu.VMEM((2, 2, parts, chips, short, LANES), bf16),
            pltpu.VMEM((seeds_axis, 8, LANES), f32),
            pltpu.VMEM((2, chips, 2, 2, short, hid), bf16),
            pltpu.VMEM((2, 2, chips, rows, hid), bf16),
            pltpu.VMEM((2, chips, rows, hid), bf16),
            pltpu.VMEM((2, chips, rows, hid), bf16),
            pltpu.VMEM((2, chips, rows, hid), bf16),
            pltpu.VMEM((2, parts, short, LANES), bf16),
            pltpu.VMEM((hid, hid), f32),
            pltpu.VMEM((hid, hid), bf16),
            pltpu.VMEM((hid, LANES), bf16),
            pltpu.VMEM((hid, LANES), bf16),
            pltpu.VMEM((parts, unit, LANES), bf16),
            pltpu.VMEM((unit, LANES), bf16),
            pltpu.VMEM((8, LANES), f32),
            *[pltpu.VMEM(v.shape, f32) for v in operands[6:]],
            *[pltpu.VMEM(v.shape, i32) for v in operands[3:6]],
            dma((17,)),
            dma((2, parts)),
            dma((2, 2, parts)),
            dma((2, 2, chips)),
            dma((2, 2, chips)),
            dma((2, 2)),
            dma((2, seeds_axis)),
            dma((2, 2)),
            dma((2, 2, chips)),
            dma((2, 2, parts)),
            dma((2, 1)),
            dma((2, parts)),
            dma((2, seeds_axis)),
            dma((4,)),
        ],
        compiler_params=pltpu.CompilerParams(
            vmem_limit_bytes=56 * 2**20, collective_id=0, has_side_effects=True
        ),
    )(*operands)


def adamw(weight, moment, square, grad):
    new_moment = beta_first * moment + (1.0 - beta_first) * grad
    new_square = beta_second * square + (1.0 - beta_second) * grad * grad
    moment_hat = new_moment / (1.0 - beta_first**STEP)
    square_hat = new_square / (1.0 - beta_second**STEP)
    new_weight = weight - learn_rate * (
        moment_hat / (jnp.sqrt(square_hat) + epsilon_adam) + decay_rate * weight
    )
    return (new_moment, new_square, new_weight)


def update_kernel(
    width, classes,
    first_parts, stack_parts, count,
    w_a, m_a, s_a, w_b, m_b, s_b, w_c, m_c, s_c,
    loss_out, count_out, om_a, os_a, ow_a, om_b, os_b, ow_b, om_c, os_c, ow_c,
):
    def put(refs, where, values):
        for ref, value in zip(refs, values):
            ref[where] = value

    half = LANES // 2
    grad_first = jnp.sum(first_parts[...].astype(f32), axis=0)
    grad_stack = jnp.sum(stack_parts[...].astype(f32), axis=1)
    short = grad_stack.shape[1]
    for l in range(2):
        for h in range(2):
            grad = grad_stack[l, :, h * half : (h + 1) * half]
            rows = (l, slice(h * short, (h + 1) * short))
            put((om_b, os_b, ow_b), rows, adamw(w_b[rows], m_b[rows], s_b[rows], grad))
    for part in range(2):
        grad = grad_first[:, part * LANES : part * LANES + width]
        lanes = (slice(None), slice(part * width, (part + 1) * width))
        put((om_a, os_a, ow_a), lanes, adamw(w_a[lanes], m_a[lanes], s_a[lanes], grad))
    gap = LANES - width
    flipped = grad_first.T
    for start, stop, place in ((0, gap, width), (gap, classes, LANES + width)):
        rows = (slice(start, stop), slice(None))
        grad = flipped[place : place + stop - start]
        put((om_c, os_c, ow_c), rows, adamw(w_c[rows], m_c[rows], s_c[rows], grad))
    losses = jnp.where(iota((8, LANES), 1) >= LANES - 3, grad_first[0:8, LANES:], 0.0)
    loss_out[...] = jnp.sum(losses, keepdims=True)
    count_out[...] = count[0:1, 0:1]


def update(width, classes, *operands):
    vmem = pl.BlockSpec(memory_space=pltpu.VMEM)
    shape = jax.ShapeDtypeStruct
    outs = [shape((1, 1), f32)] * 2 + [shape(v.shape, f32) for v in operands[3:]]
    return pl.pallas_call(
        functools.partial(update_kernel, width, classes),
        out_shape=tuple(outs),
        in_specs=[vmem] * len(operands),
        out_specs=(vmem,) * len(outs),
    )(*operands)


def per_device(
    features,
    links_first,
    links_second,
    links_third,
    labels,
    valid,
    weight_first,
    moment_first,
    square_first,
    weight_stack,
    moment_stack,
    square_stack,
    weight_head,
    moment_head,
    square_head,
):
    width, classes = features.shape[1], weight_head.shape[1]
    sizes = (
        features.shape[0], links_first.shape[0], links_second.shape[0], links_third.shape[0],
        lax.axis_size("hid"), lax.axis_size("seed"), width, classes,
    )
    grad_first, grad_stack, count = step(
        sizes,
        features.T, links_first.T, links_second.T, links_third.T,
        labels.reshape(1, -1), valid.reshape(1, -1), weight_first.T, weight_stack, weight_head.T,
    )
    loss_sum, count, m_a, s_a, w_a, m_b, s_b, w_b, m_c, s_c, w_c = update(
        width, classes, grad_first, grad_stack, count,
        weight_first.T, moment_first.T, square_first.T,
        weight_stack, moment_stack, square_stack,
        weight_head.T, moment_head.T, square_head.T,
    )
    return (
        loss_sum.reshape(()), count.reshape(()),
        m_a.T, s_a.T, w_a.T,
        m_b, s_b, w_b,
        m_c.T, s_c.T, w_c.T,
    )


def solution(mesh):
    placed = (
        P("seed", None),
        P("seed", None),
        P("seed", None),
        P("seed", None),
        P("seed"),
        P("seed"),
        P(None, "hid"),
        P(None, "hid"),
        P(None, "hid"),
        P(None, "seed", "hid"),
        P(None, "seed", "hid"),
        P(None, "seed", "hid"),
        P("hid", None),
        P("hid", None),
        P("hid", None),
    )
    return jax.shard_map(
        per_device,
        mesh=mesh,
        in_specs=placed,
        out_specs=(P(), P()) + placed[6:],
        check_vma=False,
    )
```

```python
import functools

import jax
import jax.numpy as jnp
from jax import lax
from jax.experimental import pallas as pl
from jax.experimental.pallas import tpu as pltpu
from jax.sharding import PartitionSpec as P

STEP = 5
LANES = 128


epsilon_norm = 1e-06
epsilon_adam = 1e-08
learn_rate = 0.6
decay_rate = 0.01
beta_first = 0.5
beta_second = 0.5

f32, bf16, i32 = jnp.float32, jnp.bfloat16, jnp.int32
MESH = pl.DeviceIdType.MESH
NT = (((1,), (1,)), ((), ()))
TN = (((0,), (0,)), ((), ()))


def dot(a, b):
    return jnp.dot(a, b, preferred_element_type=f32)


def dot_nt(a, b):
    return lax.dot_general(a, b, NT, preferred_element_type=f32)


def dot_tn(a, b):
    return lax.dot_general(a, b, TN, preferred_element_type=f32)


def iota(shape, axis):
    return lax.broadcasted_iota(i32, shape, axis)


def slot_counts(links, first_row, ratio):
    lanes = links.shape[1]
    base = (first_row + iota((1, lanes), 1)) * ratio
    offsets = links - base
    counts = [
        jnp.sum(jnp.where(offsets == r, 1.0, 0.0), axis=0, keepdims=True) for r in range(ratio)
    ]
    degree = jnp.maximum(
        jnp.sum(jnp.where(links >= 0, 1.0, 0.0), axis=0, keepdims=True), 1.0
    )
    return counts, degree


def stripes(counts):
    ratio, lanes = len(counts), counts[0].shape[1]
    which = iota((8, lanes), 0) % ratio
    out = jnp.zeros((8, lanes), f32)
    for r in range(ratio):
        out = jnp.where(which == r, counts[r], out)
    return out


def spread(mask, stripe):
    rows = mask.shape[0]
    values = mask.reshape(rows // 8, 8, LANES) * stripe[None]
    return values.reshape(rows, LANES).astype(bf16)


def window_mask(rows, ratio):
    return jnp.where(iota((rows, LANES), 0) // ratio == iota((rows, LANES), 1), 1.0, 0.0)


def activate(preact):
    logistic = 0.5 * jnp.tanh(0.5 * preact) + 0.5
    active = preact * logistic
    slope = logistic + (active - active * logistic)
    scaling = lax.rsqrt(jnp.sum(active * active, axis=0, keepdims=True) + epsilon_norm)
    return (active * scaling).astype(bf16), active, slope, scaling


def activate_back(grad_out, active, slope, scaling):
    inner = jnp.sum(active * grad_out, axis=0, keepdims=True)
    grad_active = scaling * grad_out - active * (scaling * scaling * scaling * inner)
    return (grad_active * slope).astype(bf16)


def placement_rows(classes, columns, width):
    gap = LANES - width
    row, col = iota((classes, columns), 0), iota((classes, columns), 1)
    target = jnp.where(row < gap, width + row, LANES + width + row - gap)
    return jnp.where(col == target, 1.0, 0.0).astype(bf16)


def placement(rows, classes, width):
    gap = LANES - width
    row, col = iota((rows, classes), 0), iota((rows, classes), 1)
    target = jnp.where(col < gap, width + col, LANES + width + col - gap)
    return jnp.where(row == target, 1.0, 0.0).astype(bf16)


def shift_half(x):
    return pltpu.roll(x, LANES // 2, 1)


def step_kernel(
    sizes,
    features, links_first, links_second, links_third, labels, valid, weight_first, weight_stack, weight_head,
    first_out, stack_out, count_out,
    own_rows, child_rows, own_lead, links_a, links_b, links_a_lead, links_b_lead,
    joined_one, hidden_one, active_one, slope_one, scale_one, degree_rows, stripe_rows,
    joined_two, joined_three, spread_two, mask_four, mask_eight,
    first_all, stack_all, valid_all, low_stack,
    core_send, core_recv, plane_send, plane_recv, turn_send,
    grad_one, first_send, half_recv, half_send, part_recv, share, count_own, first_own, stack_own, head_own,
    links_c, labels_own, valid_own,
    local_sems, first_sems, block_sems, chips_sems, pair_sems, valid_sems,
    core_sems, plane_sems, turn_sems, half_sems, part_sems, share_sems, out_sems,
):
    n3, n2, n1, n0, parts, seeds_axis, width, classes = sizes
    q2, q1, q0 = n2 // parts, n1 // parts, n0 // parts
    r3, r2, r1 = n3 // n2, n2 // n1, n1 // n0
    s, z = lax.axis_index("seed"), lax.axis_index("hid")
    core, chip = lax.rem(s, 2), s // 2
    chips = seeds_axis // 2
    sibling = s + 1 - 2 * core
    two = q2 + q1 + LANES
    hid = 256
    unit = hid // parts
    own_units = pl.ds(pl.multiple_of(z * unit, unit), unit)
    near = [(0, d) for d in range(1, parts)] + [(k, 0) for k in range(1, seeds_axis)]

    def place(k, d):
        return (lax.rem(s + k, seeds_axis), lax.rem(z + d, parts))

    barrier = pltpu.get_barrier_semaphore()
    for k, d in near:
        pl.semaphore_signal(barrier, inc=1, device_id=place(k, d), device_id_type=MESH)

    def at(size):
        return pl.ds(pl.multiple_of(z * size, LANES), size)

    copies = [
        (weight_stack, stack_own),
        (weight_first, first_own),
        (weight_head, head_own),
        (valid, valid_own),
        (labels, labels_own),
        (links_third, links_c),
        (links_first.at[:, at(q2)], links_a.at[:, pl.ds(0, q2)]),
        (links_first.at[:, at(q1)], links_a.at[:, pl.ds(q2, q1)]),
        (links_first.at[:, pl.ds(0, LANES)], links_a_lead),
        (links_second.at[:, at(q1)], links_b),
        (links_second.at[:, pl.ds(0, LANES)], links_b_lead),
        (features.at[:, pl.ds(0, LANES)], own_lead),
        (features.at[:, at(q2)], own_rows.at[:, pl.ds(0, q2)]),
        (features.at[:, at(q1)], own_rows.at[:, pl.ds(q2, q1)]),
        (features.at[:, at(q2 * r3)], child_rows.at[:, pl.ds(0, q2 * r3)]),
        (features.at[:, at(q1 * r3)], child_rows.at[:, pl.ds(q2 * r3, q1 * r3)]),
        (
            features.at[:, pl.ds(pl.multiple_of(z * q0 * r3, LANES), LANES * r3)],
            child_rows.at[:, pl.ds((q2 + q1) * r3, LANES * r3)],
        ),
    ]
    started = [pltpu.make_async_copy(src, dst, local_sems.at[i]) for i, (src, dst) in enumerate(copies)]
    for copy in started:
        copy.start()

    started[0].wait()
    depth = stack_own.shape[1]
    short = depth // 2
    row, col = iota((unit, LANES), 0), iota((unit, LANES), 1)
    to_left = jnp.where(row == col, 1.0, 0.0).astype(bf16)
    to_right = jnp.where(row + unit == col, 1.0, 0.0).astype(bf16)
    for l in range(2):
        block = dot(stack_own[l, 0:short].astype(bf16), to_left)
        block += dot(stack_own[l, short:].astype(bf16), to_right)
        stack_all[core, 0, chip, l] = block.astype(bf16)
    pl.semaphore_wait(barrier, len(near))

    moves = []

    def send(src, dst, sems, where, device):
        copy = pltpu.make_async_remote_copy(
            src_ref=src, dst_ref=dst, send_sem=sems.at[(0, *where)], recv_sem=sems.at[(1, *where)],
            device_id=device, device_id_type=MESH,
        )
        copy.start()
        moves.append(copy)
        return copy

    def arrive(copies):
        for copy in copies:
            copy.wait_recv()

    flip = 1 - 2 * z // parts
    distances = [0] + [i + flip * (parts - 2 * i) for i in range(1, parts)]

    def send_chips(d):
        block = stack_all.at[core, d, chip]
        return [send(block, block, chips_sems, (d, k), place(2 * k, 0)) for k in range(1, chips)]

    def send_pair(d):
        block = stack_all.at[core, d]
        return send(block, block, pair_sems, (d,), (sibling, z))

    block_moves = [
        send(stack_all.at[core, 0, chip], stack_all.at[core, d, chip], block_sems, (d,), place(0, d))
        for d in distances[1:]
    ]
    chips_moves = [send_chips(0)]
    for copy in started[1:4]:
        copy.wait()
    row, col = iota((2 * width, hid), 0), iota((2 * width, hid), 1)
    columns = jnp.where(row < width, row, row - width + LANES)
    lift = jnp.where(columns == col, 1.0, 0.0).astype(bf16)
    seat = placement(hid, classes, width)
    shard = dot(first_own[...].astype(bf16), lift)
    shard += dot_tn(head_own[...].astype(bf16), placement_rows(classes, hid, width))
    first_all[own_units, :] = shard.astype(bf16)
    valid_all[s] = jnp.broadcast_to(valid_own[...].astype(f32), valid_all.shape[1:])

    first_moves = [
        send(first_all.at[own_units], first_all.at[own_units], first_sems, (d,), place(0, d))
        for d in range(1, parts)
    ]
    valid_moves = [
        send(valid_all.at[s], valid_all.at[s], valid_sems, (k,), place(k, 0)) for k in range(1, seeds_axis)
    ]

    mask_four[...] = window_mask(LANES * r3, r3)
    mask_eight[...] = window_mask(LANES * r2, r2)
    for part in range(2):
        joined_one[pl.ds((part + 1) * LANES - 32, 32), :] = jnp.zeros((32, two), bf16)
    for copy in started[4:]:
        copy.wait()

    counts_a, degree_a = slot_counts(links_a_lead[...], 0, r3)
    counts_b, degree_b = slot_counts(links_b_lead[...], 0, r2)
    counts_c, degree_c = slot_counts(links_c[...], 0, r1)
    lead = [*counts_a, degree_a, *counts_b, degree_b, *counts_c, degree_c]
    lead += [labels_own[...].astype(f32), valid_own[...].astype(f32)]
    packed = jnp.zeros((32, LANES), f32)
    for k, line in enumerate(lead):
        packed = jnp.where(iota((32, LANES), 0) == k, line, packed)
    source, target = iota((LANES, LANES), 0), iota((LANES, LANES), 1)
    mine = jnp.where((source == target + z * q0) & (target < q0), 1.0, 0.0).astype(bf16)
    packed = dot(packed.astype(bf16), mine)
    take = [packed[k : k + 1] for k in range(len(lead))]
    counts_a, degree_a = take[:r3], jnp.maximum(take[r3], 1.0)
    take = take[r3 + 1 :]
    counts_b, degree_b = take[:r2], jnp.maximum(take[r2], 1.0)
    take = take[r2 + 1 :]
    counts_c, degree_c = take[:r1], jnp.maximum(take[r1], 1.0)
    label, present = take[r1 + 1], take[r1 + 2]
    own_rows[:, pl.ds(q2 + q1, LANES)] = dot(own_lead[...], mine).astype(bf16)

    counts, degree = slot_counts(links_a[:, pl.ds(0, q2)], z * q2, r3)
    for t in range(q2 // LANES):
        stripe_rows[t] = stripes([c[:, t * LANES : (t + 1) * LANES] for c in counts])
    degree_rows[:, pl.ds(0, q2)] = degree
    counts, degree = slot_counts(links_a[:, pl.ds(q2, q1)], z * q1, r3)
    for t in range(q1 // LANES):
        stripe_rows[q2 // LANES + t] = stripes([c[:, t * LANES : (t + 1) * LANES] for c in counts])
    degree_rows[:, pl.ds(q2, q1)] = degree
    stripe_rows[two // LANES - 1] = stripes(counts_a)
    degree_rows[:, pl.ds(q2 + q1, LANES)] = degree_a

    def mean_tiles(tile, tiles):
        for t in range(tiles):
            lanes = pl.ds(pl.multiple_of((tile + t) * LANES, LANES), LANES)
            kids = pl.ds(pl.multiple_of((tile + t) * LANES * r3, LANES), LANES * r3)
            matrix = spread(mask_four[...], stripe_rows[tile + t])
            mean = dot(child_rows[:, kids], matrix) / degree_rows[:, lanes]
            joined_one[LANES : LANES + width, lanes] = mean.astype(bf16)
            joined_one[0:width, lanes] = own_rows[:, lanes]

    def layer_one(tile, tiles):
        lanes = pl.ds(pl.multiple_of(tile * LANES, LANES), LANES * tiles)
        preact = dot(first_all[...], joined_one[:, lanes])
        output, active, slope, scaling = activate(preact)
        hidden_one[:, lanes] = output
        active_one[:, lanes] = active
        slope_one[:, lanes] = slope
        scale_one[:, lanes] = scaling

    per = 4
    tail = q1 // LANES + 1
    lax.fori_loop(0, q2 // LANES // per, lambda i, c: (mean_tiles(i * per, per), c)[1], 0)
    mean_tiles(q2 // LANES, tail)

    counts, degree_t = slot_counts(links_b[...], z * q1, r2)
    for t in range(q1 // LANES):
        stripe = stripes([c[:, t * LANES : (t + 1) * LANES] for c in counts])
        spread_two[pl.ds(t * LANES * r2, LANES * r2), :] = spread(mask_eight[...], stripe)
    spread_lead = spread(mask_eight[0 : q0 * r2, :], stripes(counts_b))
    spread_three = spread(mask_eight[0 : q0 * r1, :], stripes(counts_c))

    for d, copy in zip(distances[1:], block_moves):
        arrive([copy])
        chips_moves.append(send_chips(d))
    arrive(chips_moves[0])
    pair_moves = [send_pair(0)]
    arrive(first_moves)
    turns = q2 // LANES // per
    at_turn = lambda i, c: (layer_one(i * per, per), c)[1]
    lax.fori_loop(0, turns // 2, at_turn, 0)
    for i in range(1, parts // 2):
        arrive(chips_moves[i])
        pair_moves.append(send_pair(distances[i]))
    lax.fori_loop(turns // 2, turns, at_turn, 0)
    for i in range(parts // 2, parts):
        arrive(chips_moves[i])
        pair_moves.append(send_pair(distances[i]))
    arrive(valid_moves)
    layer_one(q2 // LANES, tail)
    head = dot(first_all[...], seat).astype(bf16)
    every_valid = jnp.sum(valid_all[...], axis=0)[0:1]
    count = jnp.sum(every_valid, axis=1, keepdims=True)
    count_own[...] = jnp.broadcast_to(count, count_own.shape)
    out_moves = [pltpu.make_async_copy(count_own, count_out, out_sems.at[0])]
    out_moves[0].start()

    joined_two[0:hid, :] = hidden_one[:, pl.ds(q2, q1 + LANES)]
    for t in range(q1 // LANES):
        rows = pl.ds(t * LANES * r2, LANES * r2)
        mean = dot(hidden_one[:, rows], spread_two[rows, :])
        lanes = slice(t * LANES, (t + 1) * LANES)
        joined_two[hid:, lanes] = (mean / degree_t[:, lanes]).astype(bf16)
    mean = dot(hidden_one[:, pl.ds(q2, q1)], spread_lead)
    joined_two[hid:, pl.ds(q1, LANES)] = (mean / degree_b).astype(bf16)

    low_half = iota((1, LANES), 1) < unit

    def interleave(left, right):
        return jnp.where(low_half, left, shift_half(right)), jnp.where(low_half, shift_half(left), right)

    def gathered(l):
        for b in range(parts // 2):
            for c in range(2):
                left = stack_all[c, lax.rem(z - 2 * b + parts, parts), :, l].astype(f32).reshape(-1, LANES)
                right = stack_all[c, lax.rem(z - 2 * b - 1 + parts, parts), :, l].astype(f32).reshape(-1, LANES)
                for h, value in enumerate(interleave(left, right)):
                    lanes = slice(b * LANES, (b + 1) * LANES)
                    low_stack[l, :, c, h, :, lanes] = value.astype(bf16).reshape(chips, short, LANES)
        return low_stack[l].reshape(2 * hid, hid)

    arrive(pair_moves)
    weight_two = gathered(0)
    preact = dot_tn(weight_two, joined_two[...])
    output, active_two, slope_two, scale_two = activate(preact)

    joined_three[0:hid, :] = output[:, q1:]
    mean = dot(output[:, 0:q1], spread_three)
    joined_three[hid:, :] = (mean / degree_c).astype(bf16)
    weight_three = gathered(1)
    preact = dot_tn(weight_three, joined_three[...])
    seeds, active_three, slope_three, scale_three = activate(preact)

    logits = dot_tn(head, seeds)
    line = iota(logits.shape, 0)
    peak = jnp.max(logits, axis=0, keepdims=True)
    shifted = jnp.exp(logits - peak)
    totals = jnp.sum(shifted, axis=0, keepdims=True)
    hot = jnp.where(line.astype(f32) == label, 1.0, 0.0)
    weight = present / jnp.maximum(count, 1.0)
    grad_logits = ((shifted / totals - hot) * weight).astype(bf16)
    grad_out = dot(head, grad_logits)

    def keep_grad(l, value):
        value = value.astype(bf16).reshape(chips, 2, depth, hid)
        for c in range(2):
            core_send[l, c] = value[:, c]

    def send_core(l):
        return [send(core_send.at[l, 1 - core], core_recv.at[l], core_sems, (l,), (sibling, z))]

    def send_plane(l):
        plane_send[l] = (core_send[l, core].astype(f32) + core_recv[l].astype(f32)).astype(bf16)
        return [
            send(plane_send.at[l, lax.rem(chip + k, chips)], plane_recv.at[l, k], plane_sems, (l, k), place(2 * k, 0))
            for k in range(1, chips)
        ]

    def send_turn(l):
        total = plane_send[l, chip].astype(f32)
        for k in range(1, chips):
            total += plane_recv[l, k].astype(f32)
        for b in range(parts // 2):
            lanes = slice(b * LANES, (b + 1) * LANES)
            for h, value in enumerate(interleave(total[0:short, lanes], total[short:, lanes])):
                turn_send[l, 2 * b + h] = value.astype(bf16)
        out_moves.append(pltpu.make_async_copy(turn_send.at[l, z], stack_out.at[l, 0], out_sems.at[1 + l]))
        out_moves[-1].start()
        return [
            send(turn_send.at[l, lax.rem(z + d, parts)], stack_out.at[l, d], turn_sems, (l, d), place(0, d))
            for d in range(1, parts)
        ]

    grad_pre = activate_back(grad_out, active_three, slope_three, scale_three)
    keep_grad(1, dot_nt(joined_three[...], grad_pre))
    grad_joined = dot(weight_three, grad_pre)
    grad_mean = (grad_joined[hid:] / degree_c).astype(bf16)
    grad_out = jnp.concatenate([dot_nt(grad_mean, spread_three), grad_joined[0:hid]], axis=1)

    grad_pre = activate_back(grad_out, active_two, slope_two, scale_two)
    core_one = send_core(1)
    keep_grad(0, dot_nt(joined_two[...], grad_pre))
    grad_joined = dot(weight_two, grad_pre)
    grad_mean = (grad_joined[hid:, 0:q1] / degree_t).astype(bf16)
    lead_mean = (grad_joined[hid:, q1:] / degree_b).astype(bf16)
    core_moves = [send_core(0), core_one]

    nll = peak + jnp.log(totals) - jnp.sum(hot * logits, axis=0, keepdims=True)
    loss = jnp.sum(jnp.where(present > 0, nll, 0.0), axis=1, keepdims=True)
    placed = dot(seat, grad_logits).astype(bf16)
    grad_one[...] = dot_nt(seeds, placed)
    free = 2 * LANES - 3
    part_a = loss.astype(bf16).astype(f32)
    part_b = (loss - part_a).astype(bf16).astype(f32)
    part_c = loss - part_a - part_b
    row, col = iota((hid, LANES), 0), iota((hid, LANES), 1) + LANES
    notes = jnp.where(col == free, part_a, jnp.where(col == free + 1, part_b, part_c))
    notes = jnp.where((col >= free) & (lax.rem(row, unit) == 2 * z + core), notes, 0.0)
    grad_one[:, LANES:] += notes

    own = grad_joined[0:hid]
    plane_moves, turn_moves = [None, None], [None, None]
    step_lanes = 2 * LANES

    def named(tile):
        group = tile // (LANES * r2) * LANES
        return dot_nt(grad_mean[:, group : group + LANES], spread_two[pl.ds(tile, step_lanes), :])

    pieces = [(q2 + q1, lambda tile: own[:, q1:]), (q2, lambda tile: own[:, 0:q1] + dot_nt(lead_mean, spread_lead))]
    pieces += [(tile, named) for tile in range(0, q2, step_lanes)]
    grad_out = pieces[0][1](pieces[0][0])
    total, waiting = None, None
    for i, (tile, _) in enumerate(pieces):
        ahead = pieces[i + 1][1](pieces[i + 1][0]) if i + 1 < len(pieces) else None
        lanes = pl.ds(tile, grad_out.shape[1])
        grad_pre = activate_back(grad_out, active_one[:, lanes], slope_one[:, lanes], scale_one[:, lanes])
        if waiting is not None:
            total = waiting() if total is None else total + waiting()
        waiting = functools.partial(lambda g, v: dot_nt(g, joined_one[:, v]), grad_pre, lanes)
        grad_out = ahead
    total += waiting()
    first_send[...] = (grad_one[...] + total).astype(bf16)

    def half(c):
        return pl.ds(pl.multiple_of(c * LANES, LANES), LANES)

    def part(d):
        return pl.ds(pl.multiple_of(lax.rem(z + d, parts) * unit, unit), unit)

    half_moves = [send(first_send.at[:, half(1 - core)], half_recv, half_sems, (0,), (sibling, z))]
    for l in (1, 0):
        arrive(core_moves[l])
        plane_moves[l] = send_plane(l)

    arrive(half_moves)
    half_send[...] = (first_send[:, half(core)].astype(f32) + half_recv[...].astype(f32)).astype(bf16)
    part_moves = [
        send(half_send.at[part(d)], part_recv.at[d], part_sems, (d,), place(0, d)) for d in range(1, parts)
    ]
    arrive(plane_moves[1])
    turn_moves[1] = send_turn(1)
    arrive(part_moves)
    total = half_send[part(0), :].astype(f32)
    for d in range(1, parts):
        total += part_recv[d].astype(f32)
    share[...] = total.astype(bf16)
    held = first_out.at[chip, :, half(core)]
    out_moves.append(pltpu.make_async_copy(share, held, out_sems.at[3]))
    out_moves[-1].start()
    share_moves = [send(share, held, share_sems, (k,), place(k, 0)) for k in range(1, seeds_axis)]
    arrive(plane_moves[0])
    turn_moves[0] = send_turn(0)

    for copies in turn_moves:
        arrive(copies)
    arrive(share_moves)
    for copy in out_moves:
        copy.wait()
    for copy in moves:
        copy.wait_send()


def step(sizes, *operands):
    n3, n2, n1, n0, parts, seeds_axis, width, classes = sizes
    q2, q1 = n2 // parts, n1 // parts
    r3, r2 = n3 // n2, n2 // n1
    two = q2 + q1 + LANES
    hid = 256
    unit = hid // parts
    chips = seeds_axis // 2
    rows = 2 * hid // seeds_axis
    slots, slots_b = operands[1].shape[0], operands[2].shape[0]
    short = rows // 2
    hbm = pl.BlockSpec(memory_space=pl.ANY)
    shape = jax.ShapeDtypeStruct
    dma = pltpu.SemaphoreType.DMA
    return pl.pallas_call(
        functools.partial(step_kernel, sizes),
        out_shape=(shape((chips, unit, hid), bf16), shape((2, parts, short, LANES), bf16), shape((8, LANES), f32)),
        in_specs=[hbm] * 9,
        out_specs=(hbm,) * 3,
        scratch_shapes=[
            pltpu.VMEM((width, two), bf16),
            pltpu.VMEM((width, two * r3), bf16),
            pltpu.VMEM((width, LANES), bf16),
            pltpu.VMEM((slots, q2 + q1), i32),
            pltpu.VMEM((slots_b, q1), i32),
            pltpu.VMEM((slots, LANES), i32),
            pltpu.VMEM((slots_b, LANES), i32),
            pltpu.VMEM((2 * LANES, two), bf16),
            pltpu.VMEM((hid, two), bf16),
            pltpu.VMEM((hid, two), f32),
            pltpu.VMEM((hid, two), f32),
            pltpu.VMEM((1, two), f32),
            pltpu.VMEM((1, two), f32),
            pltpu.VMEM((two // LANES, 8, LANES), f32),
            pltpu.VMEM((2 * hid, q1 + LANES), bf16),
            pltpu.VMEM((2 * hid, LANES), bf16),
            pltpu.VMEM((q2, LANES), bf16),
            pltpu.VMEM((LANES * r3, LANES), f32),
            pltpu.VMEM((LANES * r2, LANES), f32),
            pltpu.VMEM((hid, hid), bf16),
            pltpu.VMEM((2, parts, chips, 2, short, LANES), bf16),
            pltpu.VMEM((seeds_axis, 8, LANES), f32),
            pltpu.VMEM((2, chips, 2, 2, short, hid), bf16),
            pltpu.VMEM((2, 2, chips, rows, hid), bf16),
            pltpu.VMEM((2, chips, rows, hid), bf16),
            pltpu.VMEM((2, chips, rows, hid), bf16),
            pltpu.VMEM((2, chips, rows, hid), bf16),
            pltpu.VMEM((2, parts, short, LANES), bf16),
            pltpu.VMEM((hid, hid), f32),
            pltpu.VMEM((hid, hid), bf16),
            pltpu.VMEM((hid, LANES), bf16),
            pltpu.VMEM((hid, LANES), bf16),
            pltpu.VMEM((parts, unit, LANES), bf16),
            pltpu.VMEM((unit, LANES), bf16),
            pltpu.VMEM((8, LANES), f32),
            *[pltpu.VMEM(v.shape, f32) for v in operands[6:]],
            *[pltpu.VMEM(v.shape, i32) for v in operands[3:6]],
            dma((17,)),
            dma((2, parts)),
            dma((2, parts)),
            dma((2, parts, chips)),
            dma((2, parts)),
            dma((2, seeds_axis)),
            dma((2, 2)),
            dma((2, 2, chips)),
            dma((2, 2, parts)),
            dma((2, 1)),
            dma((2, parts)),
            dma((2, seeds_axis)),
            dma((4,)),
        ],
        compiler_params=pltpu.CompilerParams(
            vmem_limit_bytes=56 * 2**20, collective_id=0, has_side_effects=True
        ),
    )(*operands)


def adamw(weight, moment, square, grad):
    new_moment = beta_first * moment + (1.0 - beta_first) * grad
    new_square = beta_second * square + (1.0 - beta_second) * grad * grad
    moment_hat = new_moment / (1.0 - beta_first**STEP)
    square_hat = new_square / (1.0 - beta_second**STEP)
    new_weight = weight - learn_rate * (
        moment_hat / (jnp.sqrt(square_hat) + epsilon_adam) + decay_rate * weight
    )
    return (new_moment, new_square, new_weight)


def update_kernel(
    width, classes,
    first_parts, stack_parts, count,
    w_a, m_a, s_a, w_b, m_b, s_b, w_c, m_c, s_c,
    loss_out, count_out, om_a, os_a, ow_a, om_b, os_b, ow_b, om_c, os_c, ow_c,
):
    def put(refs, where, values):
        for ref, value in zip(refs, values):
            ref[where] = value

    half = LANES // 2
    grad_first = jnp.sum(first_parts[...].astype(f32), axis=0)
    grad_stack = jnp.sum(stack_parts[...].astype(f32), axis=1)
    short = grad_stack.shape[1]
    for l in range(2):
        for h in range(2):
            grad = grad_stack[l, :, h * half : (h + 1) * half]
            rows = (l, slice(h * short, (h + 1) * short))
            put((om_b, os_b, ow_b), rows, adamw(w_b[rows], m_b[rows], s_b[rows], grad))
    for part in range(2):
        grad = grad_first[:, part * LANES : part * LANES + width]
        lanes = (slice(None), slice(part * width, (part + 1) * width))
        put((om_a, os_a, ow_a), lanes, adamw(w_a[lanes], m_a[lanes], s_a[lanes], grad))
    gap = LANES - width
    flipped = grad_first.T
    for start, stop, place in ((0, gap, width), (gap, classes, LANES + width)):
        rows = (slice(start, stop), slice(None))
        grad = flipped[place : place + stop - start]
        put((om_c, os_c, ow_c), rows, adamw(w_c[rows], m_c[rows], s_c[rows], grad))
    losses = jnp.where(iota((8, LANES), 1) >= LANES - 3, grad_first[0:8, LANES:], 0.0)
    loss_out[...] = jnp.sum(losses, keepdims=True)
    count_out[...] = count[0:1, 0:1]


def update(width, classes, *operands):
    vmem = pl.BlockSpec(memory_space=pltpu.VMEM)
    shape = jax.ShapeDtypeStruct
    outs = [shape((1, 1), f32)] * 2 + [shape(v.shape, f32) for v in operands[3:]]
    return pl.pallas_call(
        functools.partial(update_kernel, width, classes),
        out_shape=tuple(outs),
        in_specs=[vmem] * len(operands),
        out_specs=(vmem,) * len(outs),
    )(*operands)


def per_device(
    features,
    links_first,
    links_second,
    links_third,
    labels,
    valid,
    weight_first,
    moment_first,
    square_first,
    weight_stack,
    moment_stack,
    square_stack,
    weight_head,
    moment_head,
    square_head,
):
    width, classes = features.shape[1], weight_head.shape[1]
    sizes = (
        features.shape[0], links_first.shape[0], links_second.shape[0], links_third.shape[0],
        lax.axis_size("hid"), lax.axis_size("seed"), width, classes,
    )
    grad_first, grad_stack, count = step(
        sizes,
        features.T, links_first.T, links_second.T, links_third.T,
        labels.reshape(1, -1), valid.reshape(1, -1), weight_first.T, weight_stack, weight_head.T,
    )
    loss_sum, count, m_a, s_a, w_a, m_b, s_b, w_b, m_c, s_c, w_c = update(
        width, classes, grad_first, grad_stack, count,
        weight_first.T, moment_first.T, square_first.T,
        weight_stack, moment_stack, square_stack,
        weight_head.T, moment_head.T, square_head.T,
    )
    return (
        loss_sum.reshape(()), count.reshape(()),
        m_a.T, s_a.T, w_a.T,
        m_b, s_b, w_b,
        m_c.T, s_c.T, w_c.T,
    )


def solution(mesh):
    placed = (
        P("seed", None),
        P("seed", None),
        P("seed", None),
        P("seed", None),
        P("seed"),
        P("seed"),
        P(None, "hid"),
        P(None, "hid"),
        P(None, "hid"),
        P(None, "seed", "hid"),
        P(None, "seed", "hid"),
        P(None, "seed", "hid"),
        P("hid", None),
        P("hid", None),
        P("hid", None),
    )
    return jax.shard_map(
        per_device,
        mesh=mesh,
        in_specs=placed,
        out_specs=(P(), P()) + placed[6:],
        check_vma=False,
    )
```

```python
import functools

import jax
import jax.numpy as jnp
from jax import lax
from jax.experimental import pallas as pl
from jax.experimental.pallas import tpu as pltpu
from jax.sharding import PartitionSpec as P

STEP = 5
LANES = 128


epsilon_norm = 1e-06
epsilon_adam = 1e-08
learn_rate = 0.6
decay_rate = 0.01
beta_first = 0.5
beta_second = 0.5

f32, bf16, i32 = jnp.float32, jnp.bfloat16, jnp.int32
MESH = pl.DeviceIdType.MESH
NT = (((1,), (1,)), ((), ()))
TN = (((0,), (0,)), ((), ()))


def dot(a, b):
    return jnp.dot(a, b, preferred_element_type=f32)


def dot_nt(a, b):
    return lax.dot_general(a, b, NT, preferred_element_type=f32)


def dot_tn(a, b):
    return lax.dot_general(a, b, TN, preferred_element_type=f32)


def iota(shape, axis):
    return lax.broadcasted_iota(i32, shape, axis)


def slot_counts(links, first_row, ratio):
    lanes = links.shape[1]
    base = (first_row + iota((1, lanes), 1)) * ratio
    offsets = links - base
    counts = [
        jnp.sum(jnp.where(offsets == r, 1.0, 0.0), axis=0, keepdims=True) for r in range(ratio)
    ]
    degree = jnp.sum(jnp.where(links >= 0, 1.0, 0.0), axis=0, keepdims=True)
    return counts, degree


def stripes(counts):
    ratio, lanes = len(counts), counts[0].shape[1]
    which = iota((8, lanes), 0) % ratio
    out = jnp.zeros((8, lanes), f32)
    for r in range(ratio):
        out = jnp.where(which == r, counts[r], out)
    return out


def spread(mask, stripe):
    rows = mask.shape[0]
    values = mask.reshape(rows // 8, 8, LANES) * stripe[None]
    return values.reshape(rows, LANES).astype(bf16)


def window_mask(rows, ratio):
    return jnp.where(iota((rows, LANES), 0) // ratio == iota((rows, LANES), 1), 1.0, 0.0)


def sigmoid_parts(preact):
    logistic = 0.5 * jnp.tanh(0.5 * preact) + 0.5
    active = preact * logistic
    return active, logistic + (active - active * logistic)


def activate(preact):
    active, slope = sigmoid_parts(preact)
    scaling = lax.rsqrt(jnp.sum(active * active, axis=0, keepdims=True) + epsilon_norm)
    return (active * scaling).astype(bf16), active, slope, scaling


def activate_back(grad_out, active, slope, scaling):
    inner = jnp.sum(active * grad_out, axis=0, keepdims=True)
    grad_active = scaling * grad_out - active * (scaling * scaling * scaling * inner)
    return (grad_active * slope).astype(bf16)


def placement_rows(classes, columns, width):
    gap = LANES - width
    row, col = iota((classes, columns), 0), iota((classes, columns), 1)
    target = jnp.where(row < gap, width + row, LANES + width + row - gap)
    return jnp.where(col == target, 1.0, 0.0).astype(bf16)


def placement(rows, classes, width):
    gap = LANES - width
    row, col = iota((rows, classes), 0), iota((rows, classes), 1)
    target = jnp.where(col < gap, width + col, LANES + width + col - gap)
    return jnp.where(row == target, 1.0, 0.0).astype(bf16)


def shift_half(x):
    return pltpu.roll(x, LANES // 2, 1)


def step_kernel(
    sizes,
    features, links_first, links_second, links_third, labels, valid, weight_first, weight_stack, weight_head,
    first_out, stack_out, count_out,
    own_rows, child_rows, own_lead, links_a, links_b, links_a_lead, links_b_lead,
    joined_one, hidden_one, active_one, slope_one, scale_one, square_rows, degree_rows, stripe_rows,
    joined_two, joined_three, spread_two, mask_four, mask_eight,
    first_all, stack_all, valid_all, low_stack,
    core_send, core_recv, plane_send, plane_recv, turn_send,
    grad_one, first_send, half_recv, half_send, part_recv, share, count_own, first_own, stack_own, head_own,
    links_c, labels_own, valid_own,
    local_sems, first_sems, block_sems, chips_sems, wide_sems, pair_sems, valid_sems,
    core_sems, plane_sems, turn_sems, half_sems, part_sems, share_sems, out_sems,
):
    n3, n2, n1, n0, parts, seeds_axis, width, classes = sizes
    q2, q1, q0 = n2 // parts, n1 // parts, n0 // parts
    r3, r2, r1 = n3 // n2, n2 // n1, n1 // n0
    s, z = lax.axis_index("seed"), lax.axis_index("hid")
    core, chip = lax.rem(s, 2), s // 2
    chips = seeds_axis // 2
    sibling = s + 1 - 2 * core
    two = q2 + q1 + LANES
    hid = 256
    unit = hid // parts
    own_units = pl.ds(pl.multiple_of(z * unit, unit), unit)
    near = [(0, d) for d in range(1, parts)] + [(k, 0) for k in range(1, seeds_axis)]

    def place(k, d):
        return (lax.rem(s + k, seeds_axis), lax.rem(z + d, parts))

    barrier = pltpu.get_barrier_semaphore()
    for k, d in near:
        pl.semaphore_signal(barrier, inc=1, device_id=place(k, d), device_id_type=MESH)

    def at(size):
        return pl.ds(pl.multiple_of(z * size, LANES), size)

    copies = [
        (weight_stack, stack_own),
        (weight_first, first_own),
        (weight_head, head_own),
        (valid, valid_own),
        (labels, labels_own),
        (links_third, links_c),
        (links_first.at[:, at(q2)], links_a.at[:, pl.ds(0, q2)]),
        (links_first.at[:, at(q1)], links_a.at[:, pl.ds(q2, q1)]),
        (links_first.at[:, pl.ds(0, LANES)], links_a_lead),
        (links_second.at[:, at(q1)], links_b),
        (links_second.at[:, pl.ds(0, LANES)], links_b_lead),
        (features.at[:, pl.ds(0, LANES)], own_lead),
        (features.at[:, at(q2)], own_rows.at[:, pl.ds(0, q2)]),
        (features.at[:, at(q1)], own_rows.at[:, pl.ds(q2, q1)]),
        (features.at[:, at(q2 * r3)], child_rows.at[:, pl.ds(0, q2 * r3)]),
        (features.at[:, at(q1 * r3)], child_rows.at[:, pl.ds(q2 * r3, q1 * r3)]),
        (
            features.at[:, pl.ds(pl.multiple_of(z * q0 * r3, LANES), LANES * r3)],
            child_rows.at[:, pl.ds((q2 + q1) * r3, LANES * r3)],
        ),
    ]
    started = [pltpu.make_async_copy(src, dst, local_sems.at[i]) for i, (src, dst) in enumerate(copies)]
    for copy in started[:4]:
        copy.start()

    started[0].wait()
    depth = stack_own.shape[1]
    short = depth // 2
    row, col = iota((unit, LANES), 0), iota((unit, LANES), 1)
    to_left = jnp.where(row == col, 1.0, 0.0).astype(bf16)
    to_right = jnp.where(row + unit == col, 1.0, 0.0).astype(bf16)
    for l in range(2):
        block = dot(stack_own[l, 0:short].astype(bf16), to_left)
        block += dot(stack_own[l, short:].astype(bf16), to_right)
        stack_all[core, 0, chip, l] = block.astype(bf16)
    for copy in started[4:]:
        copy.start()
    pl.semaphore_wait(barrier, len(near))

    moves = []

    def send(src, dst, sems, where, device):
        copy = pltpu.make_async_remote_copy(
            src_ref=src, dst_ref=dst, send_sem=sems.at[(0, *where)], recv_sem=sems.at[(1, *where)],
            device_id=device, device_id_type=MESH,
        )
        copy.start()
        moves.append(copy)
        return copy

    def arrive(copies):
        for copy in copies:
            copy.wait_recv()

    flip = 1 - 2 * z // parts
    distances = [0] + [i + flip * (parts - 2 * i) for i in range(1, parts)]

    def send_chips(d):
        block = stack_all.at[core, d, chip]
        return [send(block, block, chips_sems, (d, k), place(2 * k, 0)) for k in range(1, chips)]

    def send_plane_wide(d):
        block = stack_all.at[core, d, chip]
        return [send(block, block, wide_sems, (k,), place(k, 0)) for k in range(1, seeds_axis)]

    def send_pair(d):
        block = stack_all.at[core, d]
        return send(block, block, pair_sems, (d,), (sibling, z))

    block_moves = [
        send(stack_all.at[core, 0, chip], stack_all.at[core, d, chip], block_sems, (d,), place(0, d))
        for d in distances[1:]
    ]
    chips_moves = [send_chips(0)]
    for copy in started[1:4]:
        copy.wait()
    row, col = iota((2 * width, hid), 0), iota((2 * width, hid), 1)
    columns = jnp.where(row < width, row, row - width + LANES)
    lift = jnp.where(columns == col, 1.0, 0.0).astype(bf16)
    seat = placement(hid, classes, width)
    shard = dot(first_own[...].astype(bf16), lift)
    shard += dot_tn(head_own[...].astype(bf16), placement_rows(classes, hid, width))
    first_all[own_units, :] = shard.astype(bf16)
    valid_all[s] = jnp.broadcast_to(valid_own[...].astype(f32), valid_all.shape[1:])

    first_moves = [
        send(first_all.at[own_units], first_all.at[own_units], first_sems, (d,), place(0, d)) for d in reversed(distances[1:])
    ][::-1]
    valid_moves = [
        send(valid_all.at[s], valid_all.at[s], valid_sems, (k,), place(k, 0)) for k in range(1, seeds_axis)
    ]

    mask_four[...] = window_mask(LANES * r3, r3)
    mask_eight[...] = window_mask(LANES * r2, r2)
    for part in range(2):
        joined_one[pl.ds((part + 1) * LANES - 32, 32), :] = jnp.zeros((32, two), bf16)
    for copy in started[4:]:
        copy.wait()

    counts_a, degree_a = slot_counts(links_a_lead[...], 0, r3)
    counts_b, degree_b = slot_counts(links_b_lead[...], 0, r2)
    counts_c, degree_c = slot_counts(links_c[...], 0, r1)
    lead = [*counts_a, degree_a, *counts_b, degree_b, *counts_c, degree_c]
    lead += [labels_own[...].astype(f32), valid_own[...].astype(f32)]
    packed = jnp.zeros((32, LANES), f32)
    for k, line in enumerate(lead):
        packed = jnp.where(iota((32, LANES), 0) == k, line, packed)
    source, target = iota((LANES, LANES), 0), iota((LANES, LANES), 1)
    mine = jnp.where((source == target + z * q0) & (target < q0), 1.0, 0.0).astype(bf16)
    packed = dot(packed.astype(bf16), mine)
    take = [packed[k : k + 1] for k in range(len(lead))]
    counts_a, degree_a = take[:r3], 1.0 / jnp.maximum(take[r3], 1.0)
    take = take[r3 + 1 :]
    counts_b, degree_b = take[:r2], 1.0 / jnp.maximum(take[r2], 1.0)
    take = take[r2 + 1 :]
    counts_c, degree_c = take[:r1], 1.0 / jnp.maximum(take[r1], 1.0)
    label, present = take[r1 + 1], take[r1 + 2]
    own_rows[:, pl.ds(q2 + q1, LANES)] = dot(own_lead[...], mine).astype(bf16)

    counts, degree = slot_counts(links_a[:, pl.ds(0, q2)], z * q2, r3)
    for t in range(q2 // LANES):
        stripe_rows[t] = stripes([c[:, t * LANES : (t + 1) * LANES] for c in counts])
    degree_rows[:, pl.ds(0, q2)] = 1.0 / jnp.maximum(degree, 1.0)
    counts, degree = slot_counts(links_a[:, pl.ds(q2, q1)], z * q1, r3)
    for t in range(q1 // LANES):
        stripe_rows[q2 // LANES + t] = stripes([c[:, t * LANES : (t + 1) * LANES] for c in counts])
    degree_rows[:, pl.ds(q2, q1)] = 1.0 / jnp.maximum(degree, 1.0)
    stripe_rows[two // LANES - 1] = stripes(counts_a)
    degree_rows[:, pl.ds(q2 + q1, LANES)] = degree_a

    def mean_tiles(tile, tiles):
        for t in range(tiles):
            lanes = pl.ds(pl.multiple_of((tile + t) * LANES, LANES), LANES)
            kids = pl.ds(pl.multiple_of((tile + t) * LANES * r3, LANES), LANES * r3)
            matrix = spread(mask_four[...], stripe_rows[tile + t])
            mean = dot(child_rows[:, kids], matrix) * degree_rows[:, lanes]
            joined_one[LANES : LANES + width, lanes] = mean.astype(bf16)
            joined_one[0:width, lanes] = own_rows[:, lanes]

    def layer_one(i):
        units = pl.ds(pl.multiple_of(lax.rem(z - distances[i] + parts, parts) * unit, unit), unit)

        def tile_units(tile, tiles):
            lanes = pl.ds(pl.multiple_of(tile * LANES, LANES), LANES * tiles)
            active, slope = sigmoid_parts(dot(first_all[units, :], joined_one[:, lanes]))
            active_one[units, lanes] = active
            slope_one[units, lanes] = slope
            square_rows[i : i + 1, lanes] = jnp.sum(active * active, axis=0, keepdims=True)

        tile_units(0, two // LANES)

    per = 4
    wide = 16
    tail = q1 // LANES + 1
    lax.fori_loop(0, q2 // LANES // per, lambda i, c: (mean_tiles(i * per, per), c)[1], 0)
    mean_tiles(q2 // LANES, tail)

    counts, degree_t = slot_counts(links_b[...], z * q1, r2)
    share_t = 1.0 / jnp.maximum(degree_t, 1.0)
    for t in range(q1 // LANES):
        stripe = stripes([c[:, t * LANES : (t + 1) * LANES] for c in counts])
        spread_two[pl.ds(t * LANES * r2, LANES * r2), :] = spread(mask_eight[...], stripe)
    spread_lead = spread(mask_eight[0 : q0 * r2, :], stripes(counts_b))
    spread_three = spread(mask_eight[0 : q0 * r1, :], stripes(counts_c))

    layer_one(0)
    for d, copy in zip(distances[1:], block_moves):
        arrive([copy])
        chips_moves.append((send_plane_wide if copy is block_moves[-1] else send_chips)(d))
    pair_moves = []
    arrive(chips_moves[0])
    pair_moves.append(send_pair(distances[0]))
    for i in range(1, parts):
        arrive(first_moves[i - 1 : i])
        layer_one(i)
    for i in range(1, parts - 1):
        arrive(chips_moves[i])
        pair_moves.append(send_pair(distances[i]))
    squares = jnp.sum(square_rows[0:parts, :], axis=0, keepdims=True)
    scale_one[...] = lax.rsqrt(squares + epsilon_norm)
    hidden_one[...] = (active_one[...] * scale_one[...]).astype(bf16)
    arrive(valid_moves)
    head = dot(first_all[...], seat).astype(bf16)
    every_valid = jnp.sum(valid_all[...], axis=0)[0:1]
    count = jnp.sum(every_valid, axis=1, keepdims=True)
    count_own[...] = jnp.broadcast_to(count, count_own.shape)
    out_moves = [pltpu.make_async_copy(count_own, count_out, out_sems.at[0])]
    out_moves[0].start()

    joined_two[0:hid, :] = hidden_one[:, pl.ds(q2, q1 + LANES)]
    for t in range(q1 // LANES):
        rows = pl.ds(t * LANES * r2, LANES * r2)
        mean = dot(hidden_one[:, rows], spread_two[rows, :])
        lanes = slice(t * LANES, (t + 1) * LANES)
        joined_two[hid:, lanes] = (mean * share_t[:, lanes]).astype(bf16)
    mean = dot(hidden_one[:, pl.ds(q2, q1)], spread_lead)
    joined_two[hid:, pl.ds(q1, LANES)] = (mean * degree_b).astype(bf16)

    low_half = iota((1, LANES), 1) < unit

    def interleave(left, right):
        return jnp.where(low_half, left, shift_half(right)), jnp.where(low_half, shift_half(left), right)

    def gathered(l):
        for b in range(parts // 2):
            for c in range(2):
                left = stack_all[c, lax.rem(z - 2 * b + parts, parts), :, l].reshape(-1, LANES)
                right = stack_all[c, lax.rem(z - 2 * b - 1 + parts, parts), :, l].reshape(-1, LANES)
                for h, value in enumerate(interleave(left, right)):
                    lanes = slice(b * LANES, (b + 1) * LANES)
                    low_stack[l, :, c, h, :, lanes] = value.astype(bf16).reshape(chips, short, LANES)
        return low_stack[l].reshape(2 * hid, hid)

    arrive(pair_moves + chips_moves[-1])
    weight_two = gathered(0)
    preact = dot_tn(weight_two, joined_two[...])
    output, active_two, slope_two, scale_two = activate(preact)

    joined_three[0:hid, :] = output[:, q1:]
    mean = dot(output[:, 0:q1], spread_three)
    joined_three[hid:, :] = (mean * degree_c).astype(bf16)
    weight_three = gathered(1)
    preact = dot_tn(weight_three, joined_three[...])
    seeds, active_three, slope_three, scale_three = activate(preact)

    logits = dot_tn(head, seeds)
    line = iota(logits.shape, 0)
    peak = jnp.max(logits, axis=0, keepdims=True)
    shifted = jnp.exp(logits - peak)
    totals = jnp.sum(shifted, axis=0, keepdims=True)
    hot = jnp.where(line.astype(f32) == label, 1.0, 0.0)
    weight = present / jnp.maximum(count, 1.0)
    grad_logits = ((shifted / totals - hot) * weight).astype(bf16)
    grad_out = dot(head, grad_logits)

    def keep_grad(l, value):
        value = value.astype(bf16).reshape(chips, 2, depth, hid)
        for c in range(2):
            core_send[l, c] = value[:, c]

    def send_core(l):
        return [send(core_send.at[l, 1 - core], core_recv.at[l], core_sems, (l,), (sibling, z))]

    def send_plane(l):
        plane_send[l] = (core_send[l, core].astype(f32) + core_recv[l].astype(f32)).astype(bf16)
        return [
            send(plane_send.at[l, lax.rem(chip + k, chips)], plane_recv.at[l, k], plane_sems, (l, k), place(2 * k, 0))
            for k in range(1, chips)
        ]

    def send_turn(l):
        total = plane_send[l, chip].astype(f32)
        for k in range(1, chips):
            total += plane_recv[l, k].astype(f32)
        for b in range(parts // 2):
            lanes = slice(b * LANES, (b + 1) * LANES)
            for h, value in enumerate(interleave(total[0:short, lanes], total[short:, lanes])):
                turn_send[l, 2 * b + h] = value.astype(bf16)
        out_moves.append(pltpu.make_async_copy(turn_send.at[l, z], stack_out.at[l, 0], out_sems.at[1 + l]))
        out_moves[-1].start()
        return [
            send(turn_send.at[l, lax.rem(z + d, parts)], stack_out.at[l, d], turn_sems, (l, d), place(0, d))
            for d in range(1, parts)
        ]

    grad_pre = activate_back(grad_out, active_three, slope_three, scale_three)
    keep_grad(1, dot_nt(joined_three[...], grad_pre))
    grad_joined = dot(weight_three, grad_pre)
    grad_mean = (grad_joined[hid:] * degree_c).astype(bf16)
    grad_out = jnp.concatenate([dot_nt(grad_mean, spread_three), grad_joined[0:hid]], axis=1)

    grad_pre = activate_back(grad_out, active_two, slope_two, scale_two)
    core_one = send_core(1)
    keep_grad(0, dot_nt(joined_two[...], grad_pre))
    grad_joined = dot(weight_two, grad_pre)
    grad_mean = (grad_joined[hid:, 0:q1] * share_t).astype(bf16)
    lead_mean = (grad_joined[hid:, q1:] * degree_b).astype(bf16)
    core_moves = [send_core(0), core_one]

    nll = peak + jnp.log(totals) - jnp.sum(hot * logits, axis=0, keepdims=True)
    loss = jnp.sum(jnp.where(present > 0, nll, 0.0), axis=1, keepdims=True)
    placed = dot(seat, grad_logits).astype(bf16)
    grad_one[...] = dot_nt(seeds, placed)
    free = 2 * LANES - 3
    part_a = loss.astype(bf16).astype(f32)
    part_b = (loss - part_a).astype(bf16).astype(f32)
    part_c = loss - part_a - part_b
    row, col = iota((hid, LANES), 0), iota((hid, LANES), 1) + LANES
    notes = jnp.where(col == free, part_a, jnp.where(col == free + 1, part_b, part_c))
    notes = jnp.where((col >= free) & (lax.rem(row, unit) == 2 * z + core), notes, 0.0)
    grad_one[:, LANES:] += notes

    own = grad_joined[0:hid]
    plane_moves, turn_moves = [None, None], [None, None]
    step_lanes = 2 * LANES

    def named(tile):
        group = tile // (LANES * r2) * LANES
        return dot_nt(grad_mean[:, group : group + LANES], spread_two[pl.ds(tile, step_lanes), :])

    pieces = [(q2 + q1, lambda tile: own[:, q1:]), (q2, lambda tile: own[:, 0:q1] + dot_nt(lead_mean, spread_lead))]
    pieces += [(tile, named) for tile in range(0, q2, step_lanes)]
    grad_out = pieces[0][1](pieces[0][0])
    total, waiting = None, None
    for i, (tile, _) in enumerate(pieces):
        ahead = pieces[i + 1][1](pieces[i + 1][0]) if i + 1 < len(pieces) else None
        lanes = pl.ds(tile, grad_out.shape[1])
        grad_pre = activate_back(grad_out, active_one[:, lanes], slope_one[:, lanes], scale_one[:, lanes])
        if waiting is not None:
            total = waiting() if total is None else total + waiting()
        waiting = functools.partial(lambda g, v: dot_nt(g, joined_one[:, v]), grad_pre, lanes)
        grad_out = ahead
    total += waiting()
    first_send[...] = (grad_one[...] + total).astype(bf16)

    def half(c):
        return pl.ds(pl.multiple_of(c * LANES, LANES), LANES)

    def part(d):
        return pl.ds(pl.multiple_of(lax.rem(z + d, parts) * unit, unit), unit)

    half_moves = [send(first_send.at[:, half(1 - core)], half_recv, half_sems, (0,), (sibling, z))]
    for l in (1, 0):
        arrive(core_moves[l])
        plane_moves[l] = send_plane(l)

    arrive(half_moves)
    half_send[...] = (first_send[:, half(core)].astype(f32) + half_recv[...].astype(f32)).astype(bf16)
    part_moves = [
        send(half_send.at[part(d)], part_recv.at[d], part_sems, (d,), place(0, d)) for d in distances[1:]
    ]
    arrive(plane_moves[1])
    turn_moves[1] = send_turn(1)
    arrive(part_moves)
    total = half_send[part(0), :].astype(f32)
    for d in range(1, parts):
        total += part_recv[d].astype(f32)
    share[...] = total.astype(bf16)
    held = first_out.at[chip, :, half(core)]
    out_moves.append(pltpu.make_async_copy(share, held, out_sems.at[3]))
    out_moves[-1].start()
    share_moves = [send(share, held, share_sems, (k,), place(k, 0)) for k in range(1, seeds_axis)]
    arrive(plane_moves[0])
    turn_moves[0] = send_turn(0)

    for copies in turn_moves:
        arrive(copies)
    arrive(share_moves)
    for copy in out_moves:
        copy.wait()
    for copy in moves:
        copy.wait_send()


def step(sizes, *operands):
    n3, n2, n1, n0, parts, seeds_axis, width, classes = sizes
    q2, q1 = n2 // parts, n1 // parts
    r3, r2 = n3 // n2, n2 // n1
    two = q2 + q1 + LANES
    hid = 256
    unit = hid // parts
    chips = seeds_axis // 2
    rows = 2 * hid // seeds_axis
    slots, slots_b = operands[1].shape[0], operands[2].shape[0]
    short = rows // 2
    hbm = pl.BlockSpec(memory_space=pl.ANY)
    shape = jax.ShapeDtypeStruct
    dma = pltpu.SemaphoreType.DMA
    return pl.pallas_call(
        functools.partial(step_kernel, sizes),
        out_shape=(shape((chips, unit, hid), bf16), shape((2, parts, short, LANES), bf16), shape((8, LANES), f32)),
        in_specs=[hbm] * 9,
        out_specs=(hbm,) * 3,
        scratch_shapes=[
            pltpu.VMEM((width, two), bf16),
            pltpu.VMEM((width, two * r3), bf16),
            pltpu.VMEM((width, LANES), bf16),
            pltpu.VMEM((slots, q2 + q1), i32),
            pltpu.VMEM((slots_b, q1), i32),
            pltpu.VMEM((slots, LANES), i32),
            pltpu.VMEM((slots_b, LANES), i32),
            pltpu.VMEM((2 * LANES, two), bf16),
            pltpu.VMEM((hid, two), bf16),
            pltpu.VMEM((hid, two), f32),
            pltpu.VMEM((hid, two), f32),
            pltpu.VMEM((1, two), f32),
            pltpu.VMEM((8, two), f32),
            pltpu.VMEM((1, two), f32),
            pltpu.VMEM((two // LANES, 8, LANES), f32),
            pltpu.VMEM((2 * hid, q1 + LANES), bf16),
            pltpu.VMEM((2 * hid, LANES), bf16),
            pltpu.VMEM((q2, LANES), bf16),
            pltpu.VMEM((LANES * r3, LANES), f32),
            pltpu.VMEM((LANES * r2, LANES), f32),
            pltpu.VMEM((hid, hid), bf16),
            pltpu.VMEM((2, parts, chips, 2, short, LANES), bf16),
            pltpu.VMEM((seeds_axis, 8, LANES), f32),
            pltpu.VMEM((2, chips, 2, 2, short, hid), bf16),
            pltpu.VMEM((2, 2, chips, rows, hid), bf16),
            pltpu.VMEM((2, chips, rows, hid), bf16),
            pltpu.VMEM((2, chips, rows, hid), bf16),
            pltpu.VMEM((2, chips, rows, hid), bf16),
            pltpu.VMEM((2, parts, short, LANES), bf16),
            pltpu.VMEM((hid, hid), f32),
            pltpu.VMEM((hid, hid), bf16),
            pltpu.VMEM((hid, LANES), bf16),
            pltpu.VMEM((hid, LANES), bf16),
            pltpu.VMEM((parts, unit, LANES), bf16),
            pltpu.VMEM((unit, LANES), bf16),
            pltpu.VMEM((8, LANES), f32),
            *[pltpu.VMEM(v.shape, f32) for v in operands[6:]],
            *[pltpu.VMEM(v.shape, i32) for v in operands[3:6]],
            dma((17,)),
            dma((2, parts)),
            dma((2, parts)),
            dma((2, parts, chips)),
            dma((2, seeds_axis)),
            dma((2, parts)),
            dma((2, seeds_axis)),
            dma((2, 2)),
            dma((2, 2, chips)),
            dma((2, 2, parts)),
            dma((2, 1)),
            dma((2, parts)),
            dma((2, seeds_axis)),
            dma((4,)),
        ],
        compiler_params=pltpu.CompilerParams(
            vmem_limit_bytes=56 * 2**20, collective_id=0, has_side_effects=True
        ),
    )(*operands)


def adamw(weight, moment, square, grad):
    new_moment = beta_first * moment + (1.0 - beta_first) * grad
    new_square = beta_second * square + (1.0 - beta_second) * grad * grad
    moment_hat = new_moment / (1.0 - beta_first**STEP)
    square_hat = new_square / (1.0 - beta_second**STEP)
    new_weight = weight - learn_rate * (
        moment_hat / (jnp.sqrt(square_hat) + epsilon_adam) + decay_rate * weight
    )
    return (new_moment, new_square, new_weight)


def update_kernel(
    width, classes,
    first_parts, stack_parts, count,
    w_a, m_a, s_a, w_b, m_b, s_b, w_c, m_c, s_c,
    loss_out, count_out, om_a, os_a, ow_a, om_b, os_b, ow_b, om_c, os_c, ow_c,
):
    def put(refs, where, values):
        for ref, value in zip(refs, values):
            ref[where] = value

    half = LANES // 2
    grad_first = jnp.sum(first_parts[...].astype(f32), axis=0)
    grad_stack = jnp.sum(stack_parts[...].astype(f32), axis=1)
    short = grad_stack.shape[1]
    for l in range(2):
        for h in range(2):
            grad = grad_stack[l, :, h * half : (h + 1) * half]
            rows = (l, slice(h * short, (h + 1) * short))
            put((om_b, os_b, ow_b), rows, adamw(w_b[rows], m_b[rows], s_b[rows], grad))
    for part in range(2):
        grad = grad_first[:, part * LANES : part * LANES + width]
        lanes = (slice(None), slice(part * width, (part + 1) * width))
        put((om_a, os_a, ow_a), lanes, adamw(w_a[lanes], m_a[lanes], s_a[lanes], grad))
    gap = LANES - width
    flipped = grad_first.T
    for start, stop, place in ((0, gap, width), (gap, classes, LANES + width)):
        rows = (slice(start, stop), slice(None))
        grad = flipped[place : place + stop - start]
        put((om_c, os_c, ow_c), rows, adamw(w_c[rows], m_c[rows], s_c[rows], grad))
    losses = jnp.where(iota((8, LANES), 1) >= LANES - 3, grad_first[0:8, LANES:], 0.0)
    loss_out[...] = jnp.sum(losses, keepdims=True)
    count_out[...] = count[0:1, 0:1]


def update(width, classes, *operands):
    vmem = pl.BlockSpec(memory_space=pltpu.VMEM)
    shape = jax.ShapeDtypeStruct
    outs = [shape((1, 1), f32)] * 2 + [shape(v.shape, f32) for v in operands[3:]]
    return pl.pallas_call(
        functools.partial(update_kernel, width, classes),
        out_shape=tuple(outs),
        in_specs=[vmem] * len(operands),
        out_specs=(vmem,) * len(outs),
    )(*operands)


def per_device(
    features,
    links_first,
    links_second,
    links_third,
    labels,
    valid,
    weight_first,
    moment_first,
    square_first,
    weight_stack,
    moment_stack,
    square_stack,
    weight_head,
    moment_head,
    square_head,
):
    width, classes = features.shape[1], weight_head.shape[1]
    sizes = (
        features.shape[0], links_first.shape[0], links_second.shape[0], links_third.shape[0],
        lax.axis_size("hid"), lax.axis_size("seed"), width, classes,
    )
    grad_first, grad_stack, count = step(
        sizes,
        features.T, links_first.T, links_second.T, links_third.T,
        labels.reshape(1, -1), valid.reshape(1, -1), weight_first.T, weight_stack, weight_head.T,
    )
    loss_sum, count, m_a, s_a, w_a, m_b, s_b, w_b, m_c, s_c, w_c = update(
        width, classes, grad_first, grad_stack, count,
        weight_first.T, moment_first.T, square_first.T,
        weight_stack, moment_stack, square_stack,
        weight_head.T, moment_head.T, square_head.T,
    )
    return (
        loss_sum.reshape(()), count.reshape(()),
        m_a.T, s_a.T, w_a.T,
        m_b, s_b, w_b,
        m_c.T, s_c.T, w_c.T,
    )


def solution(mesh):
    placed = (
        P("seed", None),
        P("seed", None),
        P("seed", None),
        P("seed", None),
        P("seed"),
        P("seed"),
        P(None, "hid"),
        P(None, "hid"),
        P(None, "hid"),
        P(None, "seed", "hid"),
        P(None, "seed", "hid"),
        P(None, "seed", "hid"),
        P("hid", None),
        P("hid", None),
        P("hid", None),
    )
    return jax.shard_map(
        per_device,
        mesh=mesh,
        in_specs=placed,
        out_specs=(P(), P()) + placed[6:],
        check_vma=False,
    )
```

```python
import functools

import jax
import jax.numpy as jnp
from jax import lax
from jax.experimental import pallas as pl
from jax.experimental.pallas import tpu as pltpu
from jax.sharding import PartitionSpec as P

STEP = 5
LANES = 128


epsilon_norm = 1e-06
epsilon_adam = 1e-08
learn_rate = 0.6
decay_rate = 0.01
beta_first = 0.5
beta_second = 0.5

f32, bf16, i32 = jnp.float32, jnp.bfloat16, jnp.int32
MESH = pl.DeviceIdType.MESH
NT = (((1,), (1,)), ((), ()))
TN = (((0,), (0,)), ((), ()))


def dot(a, b):
    return jnp.dot(a, b, preferred_element_type=f32)


def dot_nt(a, b):
    return lax.dot_general(a, b, NT, preferred_element_type=f32)


def dot_tn(a, b):
    return lax.dot_general(a, b, TN, preferred_element_type=f32)


def iota(shape, axis):
    return lax.broadcasted_iota(i32, shape, axis)


def slot_counts(links, first_row, ratio):
    lanes = links.shape[1]
    base = (first_row + iota((1, lanes), 1)) * ratio
    offsets = links - base
    counts = [
        jnp.sum(jnp.where(offsets == r, 1.0, 0.0), axis=0, keepdims=True) for r in range(ratio)
    ]
    degree = jnp.sum(jnp.where(links >= 0, 1.0, 0.0), axis=0, keepdims=True)
    return counts, degree


def stripes(counts):
    ratio, lanes = len(counts), counts[0].shape[1]
    which = iota((8, lanes), 0) % ratio
    out = jnp.zeros((8, lanes), f32)
    for r in range(ratio):
        out = jnp.where(which == r, counts[r], out)
    return out


def spread(mask, stripe):
    rows = mask.shape[0]
    values = mask.reshape(rows // 8, 8, LANES) * stripe[None]
    return values.reshape(rows, LANES).astype(bf16)


def window_mask(rows, ratio):
    return jnp.where(iota((rows, LANES), 0) // ratio == iota((rows, LANES), 1), 1.0, 0.0)


def sigmoid_parts(preact):
    logistic = 0.5 * jnp.tanh(0.5 * preact) + 0.5
    active = preact * logistic
    return active, logistic + (active - active * logistic)


def activate(preact):
    active, slope = sigmoid_parts(preact)
    scaling = lax.rsqrt(jnp.sum(active * active, axis=0, keepdims=True) + epsilon_norm)
    return (active * scaling).astype(bf16), active, slope, scaling


def activate_back(grad_out, active, slope, scaling):
    inner = jnp.sum(active * grad_out, axis=0, keepdims=True)
    grad_active = scaling * grad_out - active * (scaling * scaling * scaling * inner)
    return (grad_active * slope).astype(bf16)


def placement_rows(classes, columns, width):
    gap = LANES - width
    row, col = iota((classes, columns), 0), iota((classes, columns), 1)
    target = jnp.where(row < gap, width + row, LANES + width + row - gap)
    return jnp.where(col == target, 1.0, 0.0).astype(bf16)


def placement(rows, classes, width):
    gap = LANES - width
    row, col = iota((rows, classes), 0), iota((rows, classes), 1)
    target = jnp.where(col < gap, width + col, LANES + width + col - gap)
    return jnp.where(row == target, 1.0, 0.0).astype(bf16)


def shift_half(x):
    return pltpu.roll(x, LANES // 2, 1)


def step_kernel(
    sizes,
    features, links_first, links_second, links_third, labels, valid, weight_first, weight_stack, weight_head,
    first_out, stack_out, count_out,
    own_rows, child_rows, own_lead, links_a, links_b, links_a_lead, links_b_lead,
    joined_one, hidden_one, active_one, slope_one, scale_one, square_rows, degree_rows, stripe_rows,
    joined_two, joined_three, spread_two, mask_four, mask_eight,
    first_all, stack_all, valid_all, low_stack,
    core_send, core_recv, plane_send, plane_recv, turn_send,
    grad_one, first_send, half_recv, half_send, part_recv, share, count_own, first_own, stack_own, head_own,
    links_c, labels_own, valid_own,
    local_sems, first_sems, cross_sems, block_sems, chips_sems, wide_sems, pair_sems, valid_sems,
    core_sems, plane_sems, turn_sems, half_sems, part_sems, share_sems, out_sems,
):
    n3, n2, n1, n0, parts, seeds_axis, width, classes = sizes
    q2, q1, q0 = n2 // parts, n1 // parts, n0 // parts
    r3, r2, r1 = n3 // n2, n2 // n1, n1 // n0
    s, z = lax.axis_index("seed"), lax.axis_index("hid")
    core, chip = lax.rem(s, 2), s // 2
    chips = seeds_axis // 2
    sibling = s + 1 - 2 * core
    two = q2 + q1 + LANES
    hid = 256
    unit = hid // parts
    own_units = pl.ds(pl.multiple_of(z * unit, unit), unit)
    near = [(0, d) for d in range(1, parts)] + [(k, 0) for k in range(1, seeds_axis)]

    def place(k, d):
        return (lax.rem(s + k, seeds_axis), lax.rem(z + d, parts))

    barrier = pltpu.get_barrier_semaphore()
    for k, d in near:
        pl.semaphore_signal(barrier, inc=1, device_id=place(k, d), device_id_type=MESH)

    def at(size):
        return pl.ds(pl.multiple_of(z * size, LANES), size)

    copies = [
        (weight_stack, stack_own),
        (weight_first, first_own),
        (weight_head, head_own),
        (valid, valid_own),
        (labels, labels_own),
        (links_third, links_c),
        (links_first.at[:, at(q2)], links_a.at[:, pl.ds(0, q2)]),
        (links_first.at[:, at(q1)], links_a.at[:, pl.ds(q2, q1)]),
        (links_first.at[:, pl.ds(0, LANES)], links_a_lead),
        (links_second.at[:, at(q1)], links_b),
        (links_second.at[:, pl.ds(0, LANES)], links_b_lead),
        (features.at[:, pl.ds(0, LANES)], own_lead),
        (features.at[:, at(q2)], own_rows.at[:, pl.ds(0, q2)]),
        (features.at[:, at(q1)], own_rows.at[:, pl.ds(q2, q1)]),
        (features.at[:, at(q2 * r3)], child_rows.at[:, pl.ds(0, q2 * r3)]),
        (features.at[:, at(q1 * r3)], child_rows.at[:, pl.ds(q2 * r3, q1 * r3)]),
        (
            features.at[:, pl.ds(pl.multiple_of(z * q0 * r3, LANES), LANES * r3)],
            child_rows.at[:, pl.ds((q2 + q1) * r3, LANES * r3)],
        ),
    ]
    started = [pltpu.make_async_copy(src, dst, local_sems.at[i]) for i, (src, dst) in enumerate(copies)]
    for copy in started[:4]:
        copy.start()

    started[0].wait()
    depth = stack_own.shape[1]
    short = depth // 2
    row, col = iota((unit, LANES), 0), iota((unit, LANES), 1)
    to_left = jnp.where(row == col, 1.0, 0.0).astype(bf16)
    to_right = jnp.where(row + unit == col, 1.0, 0.0).astype(bf16)
    for l in range(2):
        block = dot(stack_own[l, 0:short].astype(bf16), to_left)
        block += dot(stack_own[l, short:].astype(bf16), to_right)
        stack_all[core, 0, chip, l] = block.astype(bf16)
    for copy in started[4:]:
        copy.start()
    pl.semaphore_wait(barrier, len(near))

    moves = []

    def send(src, dst, sems, where, device):
        copy = pltpu.make_async_remote_copy(
            src_ref=src, dst_ref=dst, send_sem=sems.at[(0, *where)], recv_sem=sems.at[(1, *where)],
            device_id=device, device_id_type=MESH,
        )
        copy.start()
        moves.append(copy)
        return copy

    def arrive(copies):
        for copy in copies:
            copy.wait_recv()

    def drain(count):
        for _ in range(count):
            moves.pop(0).wait_send()

    flip = 1 - 2 * z // parts
    chip_order = [i + (1 - lax.rem(chip, 2)) * (chips - 2 * i) for i in range(1, chips)]
    distances = [0] + [i + flip * (parts - 2 * i) for i in range(1, parts)]

    def half(c):
        return pl.ds(pl.multiple_of(c * LANES, LANES), LANES)

    def units_of(d):
        return pl.ds(pl.multiple_of(lax.rem(z - d + parts, parts) * unit, unit), unit)

    def send_chips(d):
        block = stack_all.at[core, d, chip]
        return [send(block, block, chips_sems, (d, k), place(2 * k, 0)) for k in chip_order]

    def send_plane_wide(d):
        block = stack_all.at[core, d, chip]
        return [send(block, block, wide_sems, (k,), place(k, 0)) for k in range(1, seeds_axis)]

    def send_pair(d):
        block = stack_all.at[core, d]
        return send(block, block, pair_sems, (d,), (sibling, z))

    block_moves = [
        send(stack_all.at[core, 0, chip], stack_all.at[core, d, chip], block_sems, (d,), place(0, d))
        for d in distances[1:]
    ]
    for copy in started[1:4]:
        copy.wait()
    row, col = iota((2 * width, hid), 0), iota((2 * width, hid), 1)
    columns = jnp.where(row < width, row, row - width + LANES)
    lift = jnp.where(columns == col, 1.0, 0.0).astype(bf16)
    seat = placement(hid, classes, width)
    shard = dot(first_own[...].astype(bf16), lift)
    shard += dot_tn(head_own[...].astype(bf16), placement_rows(classes, hid, width))
    first_all[own_units, :] = shard.astype(bf16)
    valid_all[s] = jnp.broadcast_to(valid_own[...].astype(f32), valid_all.shape[1:])

    own_half = first_all.at[own_units, half(core)]
    first_moves = [
        send(own_half, own_half, first_sems, (d,), place(0, d)) for d in reversed(distances[1:])
    ][::-1]
    chips_moves = [send_chips(0)]
    valid_moves = [
        send(valid_all.at[s], valid_all.at[s], valid_sems, (k,), place(k, 0)) for k in range(1, seeds_axis)
    ]

    mask_four[...] = window_mask(LANES * r3, r3)
    mask_eight[...] = window_mask(LANES * r2, r2)
    for part in range(2):
        joined_one[pl.ds((part + 1) * LANES - 32, 32), :] = jnp.zeros((32, two), bf16)
    for copy in started[4:]:
        copy.wait()

    counts_a, degree_a = slot_counts(links_a_lead[...], 0, r3)
    counts_b, degree_b = slot_counts(links_b_lead[...], 0, r2)
    counts_c, degree_c = slot_counts(links_c[...], 0, r1)
    lead = [*counts_a, degree_a, *counts_b, degree_b, *counts_c, degree_c]
    lead += [labels_own[...].astype(f32), valid_own[...].astype(f32)]
    packed = jnp.zeros((32, LANES), f32)
    for k, line in enumerate(lead):
        packed = jnp.where(iota((32, LANES), 0) == k, line, packed)
    source, target = iota((LANES, LANES), 0), iota((LANES, LANES), 1)
    mine = jnp.where((source == target + z * q0) & (target < q0), 1.0, 0.0).astype(bf16)
    packed = dot(packed.astype(bf16), mine)
    take = [packed[k : k + 1] for k in range(len(lead))]
    counts_a, degree_a = take[:r3], 1.0 / jnp.maximum(take[r3], 1.0)
    take = take[r3 + 1 :]
    counts_b, degree_b = take[:r2], 1.0 / jnp.maximum(take[r2], 1.0)
    take = take[r2 + 1 :]
    counts_c, degree_c = take[:r1], 1.0 / jnp.maximum(take[r1], 1.0)
    label, present = take[r1 + 1], take[r1 + 2]
    own_rows[:, pl.ds(q2 + q1, LANES)] = dot(own_lead[...], mine).astype(bf16)

    counts, degree = slot_counts(links_a[:, pl.ds(0, q2)], z * q2, r3)
    for t in range(q2 // LANES):
        stripe_rows[t] = stripes([c[:, t * LANES : (t + 1) * LANES] for c in counts])
    degree_rows[:, pl.ds(0, q2)] = 1.0 / jnp.maximum(degree, 1.0)
    counts, degree = slot_counts(links_a[:, pl.ds(q2, q1)], z * q1, r3)
    for t in range(q1 // LANES):
        stripe_rows[q2 // LANES + t] = stripes([c[:, t * LANES : (t + 1) * LANES] for c in counts])
    degree_rows[:, pl.ds(q2, q1)] = 1.0 / jnp.maximum(degree, 1.0)
    stripe_rows[two // LANES - 1] = stripes(counts_a)
    degree_rows[:, pl.ds(q2 + q1, LANES)] = degree_a

    def mean_tiles(tile, tiles):
        for t in range(tiles):
            lanes = pl.ds(pl.multiple_of((tile + t) * LANES, LANES), LANES)
            kids = pl.ds(pl.multiple_of((tile + t) * LANES * r3, LANES), LANES * r3)
            matrix = spread(mask_four[...], stripe_rows[tile + t])
            mean = dot(child_rows[:, kids], matrix) * degree_rows[:, lanes]
            joined_one[LANES : LANES + width, lanes] = mean.astype(bf16)
            joined_one[0:width, lanes] = own_rows[:, lanes]

    def layer_one(i):
        units = units_of(distances[i])

        def tile_units(tile, tiles):
            lanes = pl.ds(pl.multiple_of(tile * LANES, LANES), LANES * tiles)
            active, slope = sigmoid_parts(dot(first_all[units, :], joined_one[:, lanes]))
            active_one[units, lanes] = active
            slope_one[units, lanes] = slope
            square_rows[i : i + 1, lanes] = jnp.sum(active * active, axis=0, keepdims=True)

        tile_units(0, two // LANES)

    per = 4
    wide = 16
    tail = q1 // LANES + 1
    lax.fori_loop(0, q2 // LANES // per, lambda i, c: (mean_tiles(i * per, per), c)[1], 0)
    mean_tiles(q2 // LANES, tail)

    counts, degree_t = slot_counts(links_b[...], z * q1, r2)
    share_t = 1.0 / jnp.maximum(degree_t, 1.0)
    for t in range(q1 // LANES):
        stripe = stripes([c[:, t * LANES : (t + 1) * LANES] for c in counts])
        spread_two[pl.ds(t * LANES * r2, LANES * r2), :] = spread(mask_eight[...], stripe)
    spread_lead = spread(mask_eight[0 : q0 * r2, :], stripes(counts_b))
    spread_three = spread(mask_eight[0 : q0 * r1, :], stripes(counts_c))

    layer_one(0)
    for d, copy in zip(distances[1:], block_moves):
        arrive([copy])
        chips_moves.append(send_chips(d))
    pair_moves = []
    arrive(chips_moves[0])
    pair_moves.append(send_pair(distances[0]))
    cross_moves = []
    for d, copy in zip(distances[1:], first_moves):
        arrive([copy])
        got = first_all.at[units_of(d), half(core)]
        cross_moves.append(send(got, got, cross_sems, (d,), (sibling, z)))
    for i in range(1, parts):
        arrive(cross_moves[i - 1 : i])
        layer_one(i)
    for i in range(1, parts):
        arrive(chips_moves[i])
        pair_moves.append(send_pair(distances[i]))
    squares = jnp.sum(square_rows[0:parts, :], axis=0, keepdims=True)
    scale_one[...] = lax.rsqrt(squares + epsilon_norm)
    hidden_one[...] = (active_one[...] * scale_one[...]).astype(bf16)
    arrive(valid_moves)
    head = dot(first_all[...], seat).astype(bf16)
    every_valid = jnp.sum(valid_all[...], axis=0)[0:1]
    count = jnp.sum(every_valid, axis=1, keepdims=True)
    count_own[...] = jnp.broadcast_to(count, count_own.shape)
    out_moves = [pltpu.make_async_copy(count_own, count_out, out_sems.at[0])]
    out_moves[0].start()

    joined_two[0:hid, :] = hidden_one[:, pl.ds(q2, q1 + LANES)]
    for t in range(q1 // LANES):
        rows = pl.ds(t * LANES * r2, LANES * r2)
        mean = dot(hidden_one[:, rows], spread_two[rows, :])
        lanes = slice(t * LANES, (t + 1) * LANES)
        joined_two[hid:, lanes] = (mean * share_t[:, lanes]).astype(bf16)
    mean = dot(hidden_one[:, pl.ds(q2, q1)], spread_lead)
    joined_two[hid:, pl.ds(q1, LANES)] = (mean * degree_b).astype(bf16)

    low_half = iota((1, LANES), 1) < unit

    def interleave(left, right):
        return jnp.where(low_half, left, shift_half(right)), jnp.where(low_half, shift_half(left), right)

    def gathered(l):
        for b in range(parts // 2):
            for c in range(2):
                left = stack_all[c, lax.rem(z - 2 * b + parts, parts), :, l].reshape(-1, LANES)
                right = stack_all[c, lax.rem(z - 2 * b - 1 + parts, parts), :, l].reshape(-1, LANES)
                for h, value in enumerate(interleave(left, right)):
                    lanes = slice(b * LANES, (b + 1) * LANES)
                    low_stack[l, :, c, h, :, lanes] = value.astype(bf16).reshape(chips, short, LANES)
        return low_stack[l].reshape(2 * hid, hid)

    arrive(pair_moves)
    weight_two = gathered(0)
    preact = dot_tn(weight_two, joined_two[...])
    output, active_two, slope_two, scale_two = activate(preact)

    joined_three[0:hid, :] = output[:, q1:]
    mean = dot(output[:, 0:q1], spread_three)
    joined_three[hid:, :] = (mean * degree_c).astype(bf16)
    weight_three = gathered(1)
    preact = dot_tn(weight_three, joined_three[...])
    seeds, active_three, slope_three, scale_three = activate(preact)

    logits = dot_tn(head, seeds)
    line = iota(logits.shape, 0)
    peak = jnp.max(logits, axis=0, keepdims=True)
    shifted = jnp.exp(logits - peak)
    totals = jnp.sum(shifted, axis=0, keepdims=True)
    hot = jnp.where(line.astype(f32) == label, 1.0, 0.0)
    weight = present / jnp.maximum(count, 1.0)
    grad_logits = ((shifted / totals - hot) * weight).astype(bf16)
    grad_out = dot(head, grad_logits)

    def keep_grad(l, value):
        value = value.astype(bf16).reshape(chips, 2, depth, hid)
        for c in range(2):
            core_send[l, c] = value[:, c]

    def send_core(l):
        return [send(core_send.at[l, 1 - core], core_recv.at[l], core_sems, (l,), (sibling, z))]

    def send_plane(l):
        plane_send[l] = (core_send[l, core].astype(f32) + core_recv[l].astype(f32)).astype(bf16)
        return [
            send(plane_send.at[l, lax.rem(chip + k, chips)], plane_recv.at[l, k], plane_sems, (l, k), place(2 * k, 0))
            for k in chip_order
        ]

    def send_turn(l):
        total = plane_send[l, chip].astype(f32)
        for k in range(1, chips):
            total += plane_recv[l, k].astype(f32)
        for b in range(parts // 2):
            lanes = slice(b * LANES, (b + 1) * LANES)
            for h, value in enumerate(interleave(total[0:short, lanes], total[short:, lanes])):
                turn_send[l, 2 * b + h] = value.astype(bf16)
        out_moves.append(pltpu.make_async_copy(turn_send.at[l, z], stack_out.at[l, 0], out_sems.at[1 + l]))
        out_moves[-1].start()
        return [
            send(turn_send.at[l, lax.rem(z + d, parts)], stack_out.at[l, d], turn_sems, (l, d), place(0, d))
            for d in range(1, parts)
        ]

    grad_pre = activate_back(grad_out, active_three, slope_three, scale_three)
    keep_grad(1, dot_nt(joined_three[...], grad_pre))
    grad_joined = dot(weight_three, grad_pre)
    grad_mean = (grad_joined[hid:] * degree_c).astype(bf16)
    grad_out = jnp.concatenate([dot_nt(grad_mean, spread_three), grad_joined[0:hid]], axis=1)

    grad_pre = activate_back(grad_out, active_two, slope_two, scale_two)
    core_one = send_core(1)
    keep_grad(0, dot_nt(joined_two[...], grad_pre))
    grad_joined = dot(weight_two, grad_pre)
    grad_mean = (grad_joined[hid:, 0:q1] * share_t).astype(bf16)
    lead_mean = (grad_joined[hid:, q1:] * degree_b).astype(bf16)
    core_moves = [send_core(0), core_one]

    nll = peak + jnp.log(totals) - jnp.sum(hot * logits, axis=0, keepdims=True)
    loss = jnp.sum(jnp.where(present > 0, nll, 0.0), axis=1, keepdims=True)
    placed = dot(seat, grad_logits).astype(bf16)
    grad_one[...] = dot_nt(seeds, placed)
    free = 2 * LANES - 3
    part_a = loss.astype(bf16).astype(f32)
    part_b = (loss - part_a).astype(bf16).astype(f32)
    part_c = loss - part_a - part_b
    row, col = iota((hid, LANES), 0), iota((hid, LANES), 1) + LANES
    notes = jnp.where(col == free, part_a, jnp.where(col == free + 1, part_b, part_c))
    notes = jnp.where((col >= free) & (lax.rem(row, unit) == 2 * z + core), notes, 0.0)
    grad_one[:, LANES:] += notes

    own = grad_joined[0:hid]
    plane_moves, turn_moves = [None, None], [None, None]
    step_lanes = 2 * LANES

    def named(tile):
        group = tile // (LANES * r2) * LANES
        return dot_nt(grad_mean[:, group : group + LANES], spread_two[pl.ds(tile, step_lanes), :])

    pieces = [(q2 + q1, lambda tile: own[:, q1:]), (q2, lambda tile: own[:, 0:q1] + dot_nt(lead_mean, spread_lead))]
    pieces += [(tile, named) for tile in range(0, q2, step_lanes)]
    grad_out = pieces[0][1](pieces[0][0])
    total, waiting = None, None
    for i, (tile, _) in enumerate(pieces):
        ahead = pieces[i + 1][1](pieces[i + 1][0]) if i + 1 < len(pieces) else None
        lanes = pl.ds(tile, grad_out.shape[1])
        grad_pre = activate_back(grad_out, active_one[:, lanes], slope_one[:, lanes], scale_one[:, lanes])
        if waiting is not None:
            total = waiting() if total is None else total + waiting()
        waiting = functools.partial(lambda g, v: dot_nt(g, joined_one[:, v]), grad_pre, lanes)
        grad_out = ahead
    total += waiting()
    first_send[...] = (grad_one[...] + total).astype(bf16)

    def part(d):
        return pl.ds(pl.multiple_of(lax.rem(z + d, parts) * unit, unit), unit)

    sent = len(moves)
    half_moves = [send(first_send.at[:, half(1 - core)], half_recv, half_sems, (0,), (sibling, z))]
    for l in (1, 0):
        arrive(core_moves[l])
        plane_moves[l] = send_plane(l)

    arrive(half_moves)
    half_send[...] = (first_send[:, half(core)].astype(f32) + half_recv[...].astype(f32)).astype(bf16)
    part_moves = [
        send(half_send.at[part(d)], part_recv.at[d], part_sems, (d,), place(0, d)) for d in distances[1:]
    ]
    drain(sent)
    arrive(plane_moves[1])
    turn_moves[1] = send_turn(1)
    arrive(part_moves)
    total = half_send[part(0), :].astype(f32)
    for d in range(1, parts):
        total += part_recv[d].astype(f32)
    share[...] = total.astype(bf16)
    held = first_out.at[chip, :, half(core)]
    out_moves.append(pltpu.make_async_copy(share, held, out_sems.at[3]))
    out_moves[-1].start()
    share_moves = [send(share, held, share_sems, (k,), place(k, 0)) for k in range(1, seeds_axis)]
    arrive(plane_moves[0])
    turn_moves[0] = send_turn(0)

    for copies in turn_moves:
        arrive(copies)
    arrive(share_moves)
    for copy in out_moves:
        copy.wait()
    for copy in moves:
        copy.wait_send()


def step(sizes, *operands):
    n3, n2, n1, n0, parts, seeds_axis, width, classes = sizes
    q2, q1 = n2 // parts, n1 // parts
    r3, r2 = n3 // n2, n2 // n1
    two = q2 + q1 + LANES
    hid = 256
    unit = hid // parts
    chips = seeds_axis // 2
    rows = 2 * hid // seeds_axis
    slots, slots_b = operands[1].shape[0], operands[2].shape[0]
    short = rows // 2
    hbm = pl.BlockSpec(memory_space=pl.ANY)
    shape = jax.ShapeDtypeStruct
    dma = pltpu.SemaphoreType.DMA
    return pl.pallas_call(
        functools.partial(step_kernel, sizes),
        out_shape=(shape((chips, unit, hid), bf16), shape((2, parts, short, LANES), bf16), shape((8, LANES), f32)),
        in_specs=[hbm] * 9,
        out_specs=(hbm,) * 3,
        scratch_shapes=[
            pltpu.VMEM((width, two), bf16),
            pltpu.VMEM((width, two * r3), bf16),
            pltpu.VMEM((width, LANES), bf16),
            pltpu.VMEM((slots, q2 + q1), i32),
            pltpu.VMEM((slots_b, q1), i32),
            pltpu.VMEM((slots, LANES), i32),
            pltpu.VMEM((slots_b, LANES), i32),
            pltpu.VMEM((2 * LANES, two), bf16),
            pltpu.VMEM((hid, two), bf16),
            pltpu.VMEM((hid, two), f32),
            pltpu.VMEM((hid, two), f32),
            pltpu.VMEM((1, two), f32),
            pltpu.VMEM((8, two), f32),
            pltpu.VMEM((1, two), f32),
            pltpu.VMEM((two // LANES, 8, LANES), f32),
            pltpu.VMEM((2 * hid, q1 + LANES), bf16),
            pltpu.VMEM((2 * hid, LANES), bf16),
            pltpu.VMEM((q2, LANES), bf16),
            pltpu.VMEM((LANES * r3, LANES), f32),
            pltpu.VMEM((LANES * r2, LANES), f32),
            pltpu.VMEM((hid, hid), bf16),
            pltpu.VMEM((2, parts, chips, 2, short, LANES), bf16),
            pltpu.VMEM((seeds_axis, 8, LANES), f32),
            pltpu.VMEM((2, chips, 2, 2, short, hid), bf16),
            pltpu.VMEM((2, 2, chips, rows, hid), bf16),
            pltpu.VMEM((2, chips, rows, hid), bf16),
            pltpu.VMEM((2, chips, rows, hid), bf16),
            pltpu.VMEM((2, chips, rows, hid), bf16),
            pltpu.VMEM((2, parts, short, LANES), bf16),
            pltpu.VMEM((hid, hid), f32),
            pltpu.VMEM((hid, hid), bf16),
            pltpu.VMEM((hid, LANES), bf16),
            pltpu.VMEM((hid, LANES), bf16),
            pltpu.VMEM((parts, unit, LANES), bf16),
            pltpu.VMEM((unit, LANES), bf16),
            pltpu.VMEM((8, LANES), f32),
            *[pltpu.VMEM(v.shape, f32) for v in operands[6:]],
            *[pltpu.VMEM(v.shape, i32) for v in operands[3:6]],
            dma((17,)),
            dma((2, parts)),
            dma((2, parts)),
            dma((2, parts)),
            dma((2, parts, chips)),
            dma((2, seeds_axis)),
            dma((2, parts)),
            dma((2, seeds_axis)),
            dma((2, 2)),
            dma((2, 2, chips)),
            dma((2, 2, parts)),
            dma((2, 1)),
            dma((2, parts)),
            dma((2, seeds_axis)),
            dma((4,)),
        ],
        compiler_params=pltpu.CompilerParams(
            vmem_limit_bytes=56 * 2**20, collective_id=0, has_side_effects=True
        ),
    )(*operands)


def adamw(weight, moment, square, grad):
    new_moment = beta_first * moment + (1.0 - beta_first) * grad
    new_square = beta_second * square + (1.0 - beta_second) * grad * grad
    moment_hat = new_moment / (1.0 - beta_first**STEP)
    square_hat = new_square / (1.0 - beta_second**STEP)
    new_weight = weight - learn_rate * (
        moment_hat / (jnp.sqrt(square_hat) + epsilon_adam) + decay_rate * weight
    )
    return (new_moment, new_square, new_weight)


def update_kernel(
    width, classes,
    first_parts, stack_parts, count,
    w_a, m_a, s_a, w_b, m_b, s_b, w_c, m_c, s_c,
    loss_out, count_out, om_a, os_a, ow_a, om_b, os_b, ow_b, om_c, os_c, ow_c,
):
    def put(refs, where, values):
        for ref, value in zip(refs, values):
            ref[where] = value

    half = LANES // 2
    grad_first = jnp.sum(first_parts[...].astype(f32), axis=0)
    grad_stack = jnp.sum(stack_parts[...].astype(f32), axis=1)
    short = grad_stack.shape[1]
    for l in range(2):
        for h in range(2):
            grad = grad_stack[l, :, h * half : (h + 1) * half]
            rows = (l, slice(h * short, (h + 1) * short))
            put((om_b, os_b, ow_b), rows, adamw(w_b[rows], m_b[rows], s_b[rows], grad))
    for part in range(2):
        grad = grad_first[:, part * LANES : part * LANES + width]
        lanes = (slice(None), slice(part * width, (part + 1) * width))
        put((om_a, os_a, ow_a), lanes, adamw(w_a[lanes], m_a[lanes], s_a[lanes], grad))
    gap = LANES - width
    flipped = grad_first.T
    for start, stop, place in ((0, gap, width), (gap, classes, LANES + width)):
        rows = (slice(start, stop), slice(None))
        grad = flipped[place : place + stop - start]
        put((om_c, os_c, ow_c), rows, adamw(w_c[rows], m_c[rows], s_c[rows], grad))
    losses = jnp.where(iota((8, LANES), 1) >= LANES - 3, grad_first[0:8, LANES:], 0.0)
    loss_out[...] = jnp.sum(losses, keepdims=True)
    count_out[...] = count[0:1, 0:1]


def update(width, classes, *operands):
    vmem = pl.BlockSpec(memory_space=pltpu.VMEM)
    shape = jax.ShapeDtypeStruct
    outs = [shape((1, 1), f32)] * 2 + [shape(v.shape, f32) for v in operands[3:]]
    return pl.pallas_call(
        functools.partial(update_kernel, width, classes),
        out_shape=tuple(outs),
        in_specs=[vmem] * len(operands),
        out_specs=(vmem,) * len(outs),
    )(*operands)


def per_device(
    features,
    links_first,
    links_second,
    links_third,
    labels,
    valid,
    weight_first,
    moment_first,
    square_first,
    weight_stack,
    moment_stack,
    square_stack,
    weight_head,
    moment_head,
    square_head,
):
    width, classes = features.shape[1], weight_head.shape[1]
    sizes = (
        features.shape[0], links_first.shape[0], links_second.shape[0], links_third.shape[0],
        lax.axis_size("hid"), lax.axis_size("seed"), width, classes,
    )
    grad_first, grad_stack, count = step(
        sizes,
        features.T, links_first.T, links_second.T, links_third.T,
        labels.reshape(1, -1), valid.reshape(1, -1), weight_first.T, weight_stack, weight_head.T,
    )
    loss_sum, count, m_a, s_a, w_a, m_b, s_b, w_b, m_c, s_c, w_c = update(
        width, classes, grad_first, grad_stack, count,
        weight_first.T, moment_first.T, square_first.T,
        weight_stack, moment_stack, square_stack,
        weight_head.T, moment_head.T, square_head.T,
    )
    return (
        loss_sum.reshape(()), count.reshape(()),
        m_a.T, s_a.T, w_a.T,
        m_b, s_b, w_b,
        m_c.T, s_c.T, w_c.T,
    )


def solution(mesh):
    placed = (
        P("seed", None),
        P("seed", None),
        P("seed", None),
        P("seed", None),
        P("seed"),
        P("seed"),
        P(None, "hid"),
        P(None, "hid"),
        P(None, "hid"),
        P(None, "seed", "hid"),
        P(None, "seed", "hid"),
        P(None, "seed", "hid"),
        P("hid", None),
        P("hid", None),
        P("hid", None),
    )
    return jax.shard_map(
        per_device,
        mesh=mesh,
        in_specs=placed,
        out_specs=(P(), P()) + placed[6:],
        check_vma=False,
    )
```
